32 devices in a mesh: seq: 2 (over y), batch: 16 (over z, x, core).
Axes of the slice: x: 2, y: 2, z: 4, core: 2. Of those that a mesh axis runs over, the one named last changes fastest.
Arguments:
- layer_input: bfloat16 [32, 2, 256, 768], P('batch', 'seq'), may hold values from -6 to 6
- cotangent: bfloat16 [32, 2, 256, 768], P('batch', 'seq'), may hold values from -6 to 6
- timesteps: int32 [32], P('batch'), may hold values from 0 to 1999
- src_len: int32 [32], P('batch'), may hold values from 64 to 256, as said below
- seq_len: int32 [32], P('batch'), may hold values from 128 to 512, as said below
- key_keep: int32 [32, 2, 256], P('batch'), may hold values 0 or 1
- query_weight: bfloat16 [768, 768], replicated, may hold values from -0.21875 to 0.21875
- query_bias: float32 [768], replicated, may hold values from -3 to 3
- key_weight: bfloat16 [768, 768], replicated, may hold values from -0.21875 to 0.21875
- value_weight: bfloat16 [768, 768], replicated, may hold values from -0.21875 to 0.21875
- value_bias: float32 [768], replicated, may hold values from -3 to 3
- output_weight: bfloat16 [768, 768], replicated, may hold values from -6 to 6
- output_bias: float32 [768], replicated, may hold values from -3 to 3
- first_gain: float32 [768], replicated, may hold values from 0.5 to 1.5
- first_shift: float32 [768], replicated, may hold values from -2 to 2
- expand_weight: bfloat16 [768, 3072], replicated, may hold values from -0.21875 to 0.21875
- expand_bias: float32 [3072], replicated, may hold values from -3 to 3
- reduce_weight: bfloat16 [3072, 768], replicated, may hold values from -0.109375 to 0.109375
- reduce_bias: float32 [768], replicated, may hold values from -3 to 3
- second_gain: float32 [768], replicated, may hold values from 0.5 to 1.5
- second_shift: float32 [768], replicated, may hold values from -2 to 2
- time_inner: bfloat16 [128, 512], replicated, may hold values from -0.5 to 0.5
- time_inner_bias: float32 [512], replicated, may hold values from -3 to 3
- time_outer: bfloat16 [512, 768], replicated, may hold values from -0.25 to 0.25
- time_outer_bias: float32 [768], replicated, may hold values from -3 to 3
Outputs:
- output: bfloat16 [32, 2, 256, 768], P('batch', 'seq')
- input_grad: bfloat16 [32, 2, 256, 768], P('batch', 'seq')
- grad_query_weight: float32 [768, 768], replicated
- grad_query_bias: float32 [768], replicated
- grad_key_weight: float32 [768, 768], replicated
- grad_value_weight: float32 [768, 768], replicated
- grad_value_bias: float32 [768], replicated
- grad_output_weight: float32 [768, 768], replicated
- grad_output_bias: float32 [768], replicated
- grad_first_gain: float32 [768], replicated
- grad_first_shift: float32 [768], replicated
- grad_expand_weight: float32 [768, 3072], P(None, ('seq', 'batch'))
- grad_expand_bias: float32 [3072], replicated
- grad_reduce_weight: float32 [3072, 768], P(('seq', 'batch'))
- grad_reduce_bias: float32 [768], replicated
- grad_second_gain: float32 [768], replicated
- grad_second_shift: float32 [768], replicated
- grad_time_inner: float32 [128, 512], replicated
- grad_time_inner_bias: float32 [512], replicated
- grad_time_outer: float32 [512, 768], replicated
- grad_time_outer_bias: float32 [768], replicated
The draws below stay inside these ranges and needn't reach their ends.
Inputs may be any that keep to these rules, and one draw needn't show every extreme that they name: Some sequence has src_len = 256 and another src_len = 64. seq_len - src_len lies in 64 to 256; some sequence has both parts 256 long, another both 256 // 4.
All inputs are finite; a program needn't handle non-finite values. No bound on the sum of `key_keep` on one device may be relied on, other than what follows from the above.
Results may differ from the reference program's by a relative error of at most 0.018.
The reference program's roundings to bfloat16 on the way count: a program that leaves them out, or rounds other values in their place, can miss the bound.
Values may be sent and summed in bfloat16 or wider, within the bound.
No kernel may reach another device: no remote copies, remote signals or barrier semaphores. Data moves between devices by JAX's collectives and lax.ppermute only.
A program may use at most 192 MiB of HBM per device.

```python
import math
import jax
import jax.numpy as jnp
from jax import lax

D = 768
HEADS = 12
HEAD_DIM = 64
FF = 3072
TDIM = 128
TFF = 512
CAP = 256
SEQS = 32


def length_pairs(key):
    first_key, second_key, third_key, fourth_key = jax.random.split(key, 4)
    source = jax.random.randint(first_key, (SEQS,), CAP // 4, CAP + 1)
    target = jax.random.randint(second_key, (SEQS,), CAP // 4, CAP + 1)
    longest = jax.random.randint(third_key, (), 0, SEQS)
    shortest = (longest + 1 + jax.random.randint(fourth_key, (), 0, SEQS - 1)) % SEQS
    position = jnp.arange(SEQS)
    source = jnp.where(position == longest, CAP, jnp.where(position == shortest, CAP // 4, source))
    target = jnp.where(position == longest, CAP, jnp.where(position == shortest, CAP // 4, target))
    return (source.astype(jnp.int32), target.astype(jnp.int32))


def draw_src_len(key, part):
    source, target = length_pairs(key)
    return source


def draw_seq_len(key, part):
    source, target = length_pairs(key)
    return (source + target).astype(jnp.int32)


def place_ends(entries, own_key, low, largest):
    shape = entries.shape
    index_at = [jax.random.randint(jax.random.fold_in(own_key, axis), (), 0, shape[axis]) for axis in range(len(shape))]
    entries = entries.at[tuple(index_at)].set(low)
    longest = shape.index(max(shape))
    index_at[longest] = (index_at[longest] + 1) % shape[longest]
    return entries.at[tuple(index_at)].set(largest)


def levels(own_key, shape, pieces, smallest, top_value):
    def one(axis_at, blocks):
        draws = jax.random.uniform(jax.random.fold_in(jax.random.fold_in(own_key, 6), axis_at), (blocks,), jnp.float32, smallest / len(pieces), top_value / len(pieces))
        return jnp.repeat(jnp.exp(draws), shape[axis_at] // blocks).reshape((-1,) + (1,) * (len(shape) - axis_at - 1))

    level = one(*pieces[0])
    for cut in pieces[1:]:
        level = level * one(*cut)
    return level


def noise(rng, shape, scale, most, pieces=(), kind=jnp.bfloat16):
    factor_of = levels(rng, shape, pieces, -0.22, 0.18) if pieces else 1.0
    values = jax.random.normal(rng, shape, jnp.float32) * scale * factor_of
    return jnp.minimum(jnp.maximum(values, -most), most).astype(kind)


def setup_inputs(seed: int = 0) -> dict:
    streams_of = jax.random.split(jax.random.key(seed), 26)
    return {
        "layer_input": noise(streams_of[0], (SEQS, 2, CAP, D), 1.0, 6.0, ((0, 16), (1, 2))),
        "cotangent": noise(streams_of[1], (SEQS, 2, CAP, D), 1.0, 6.0, ((0, 16), (1, 2))),
        "timesteps": place_ends(jax.random.randint(streams_of[2], (SEQS,), 0, 2000), jax.random.fold_in(streams_of[2], 1), 0, 1999).astype(jnp.int32),
        "src_len": draw_src_len(jax.random.fold_in(streams_of[25], 71), 0),
        "seq_len": draw_seq_len(jax.random.fold_in(streams_of[25], 71), 0),
        "key_keep": place_ends((jax.random.randint(streams_of[5], (SEQS, 2, CAP), 0, 8) < 7).astype(jnp.int32), jax.random.fold_in(streams_of[5], 1), 0, 1),
        "query_weight": noise(streams_of[6], (D, D), D ** -0.5, 0.21875),
        "query_bias": noise(streams_of[7], (D,), 0.5, 3.0, (), jnp.float32),
        "key_weight": noise(streams_of[8], (D, D), D ** -0.5, 0.21875),
        "value_weight": noise(streams_of[9], (D, D), D ** -0.5, 0.21875),
        "value_bias": noise(streams_of[10], (D,), 0.5, 3.0, (), jnp.float32),
        "output_weight": noise(streams_of[11], (D, D), (max(1, D // (2 * CAP))) ** -0.5, 6.0),
        "output_bias": noise(streams_of[12], (D,), 0.5, 3.0, (), jnp.float32),
        "first_gain": jnp.clip(1.0 + 0.1 * jax.random.normal(streams_of[13], (D,), jnp.float32), 0.5, 1.5),
        "first_shift": noise(streams_of[14], (D,), 0.3, 2.0, (), jnp.float32),
        "expand_weight": noise(streams_of[15], (D, FF), D ** -0.5, 0.21875),
        "expand_bias": noise(streams_of[16], (FF,), 0.5, 3.0, (), jnp.float32),
        "reduce_weight": noise(streams_of[17], (FF, D), FF ** -0.5, 0.109375),
        "reduce_bias": noise(streams_of[18], (D,), 0.5, 3.0, (), jnp.float32),
        "second_gain": jnp.clip(1.0 + 0.1 * jax.random.normal(streams_of[19], (D,), jnp.float32), 0.5, 1.5),
        "second_shift": noise(streams_of[20], (D,), 0.3, 2.0, (), jnp.float32),
        "time_inner": noise(streams_of[21], (TDIM, TFF), TDIM ** -0.5, 0.5),
        "time_inner_bias": noise(streams_of[22], (TFF,), 0.5, 3.0, (), jnp.float32),
        "time_outer": noise(streams_of[23], (TFF, D), TFF ** -0.5, 0.25),
        "time_outer_bias": noise(streams_of[24], (D,), 0.5, 3.0, (), jnp.float32),
    }


@jax.custom_vjp
def low(v):
    return lax.optimization_barrier(v.astype(jnp.bfloat16)).astype(jnp.float32)

@jax.custom_vjp
def low_back(v):
    return v

def low_keep(v):
    return (low(v), None)

def low_pass(kept, grad):
    return (grad,)

def back_keep(v):
    return (v, None)

def back_low(kept, grad):
    return (low(grad),)
low.defvjp(low_keep, low_pass)
low_back.defvjp(back_keep, back_low)
highest = lax.Precision.HIGHEST
norm_epsilon = 1e-12
masked_score = -1000000000.0

def time_features(stamps, width):
    half_width = width // 2
    frequency = jnp.exp(-math.log(10000.0) * jnp.arange(half_width, dtype=jnp.float32) / half_width)
    angles = stamps.astype(jnp.float32)[:, None] * frequency[None, :]
    return jnp.concatenate([jnp.cos(angles), jnp.sin(angles)], axis=1)

def time_branch(inner, inner_bias, outer, outer_bias, features):
    middle = jax.nn.silu(jnp.dot(features, inner, precision=highest) + inner_bias)
    return jnp.dot(middle, outer, precision=highest) + outer_bias

def product(left, right):
    return jnp.dot(left, right, precision=highest)

def normalize(values):
    center = values - lax.optimization_barrier(jnp.mean(values, axis=-1, keepdims=True))
    spread = lax.optimization_barrier(jnp.mean(center * center, axis=-1, keepdims=True))
    return center * lax.rsqrt(spread + norm_epsilon)

def layer(params, stream_rows, stamp, source, length, keep_flags):
    query_weight, query_bias, key_weight, value_weight, value_bias, output_weight, output_bias, first_gain, first_shift, expand_weight, expand_bias, reduce_weight, reduce_bias, second_gain, second_shift, time_inner, time_inner_bias, time_outer, time_outer_bias = params
    features = time_features(stamp[None], TDIM)
    time_vector = time_branch(time_inner, time_inner_bias, time_outer, time_outer_bias, features)[0]
    slot_index = jnp.arange(CAP).astype(jnp.int32)
    stream_length = jnp.stack([source, length - source]).astype(jnp.int32)
    valid = slot_index[None, :] < stream_length[:, None]
    allowed = jnp.logical_and(valid, keep_flags == 1).reshape(2 * CAP)
    hidden = stream_rows.reshape(2 * CAP, D) + time_vector[None, :]
    hidden_low = low(hidden)
    queries = low(low_back(product(hidden_low, query_weight) + query_bias))
    keys = low(low_back(product(hidden_low, key_weight)))
    values = low(low_back(product(hidden_low, value_weight) + value_bias))
    query_heads = queries.reshape(2 * CAP, HEADS, HEAD_DIM)
    key_heads = keys.reshape(2 * CAP, HEADS, HEAD_DIM)
    value_heads = values.reshape(2 * CAP, HEADS, HEAD_DIM)
    raw_scores = jnp.einsum('qhd,khd->hqk', query_heads, key_heads, precision=highest) * 0.125
    scores = jnp.where(allowed[None, None, :], low_back(raw_scores), masked_score)
    weights = low(jax.nn.softmax(scores, axis=-1))
    attended = jnp.einsum('hqk,khd->qhd', weights, value_heads, precision=highest).reshape(2 * CAP, D)
    attended = low(low_back(attended))
    branch = low_back(product(attended, output_weight) + output_bias)
    mixed = normalize(hidden + branch) * first_gain + first_shift
    expanded = low_back(product(low(mixed), expand_weight) + expand_bias)
    activated = low(jax.nn.gelu(expanded, approximate=False))
    reduced = low_back(product(activated, reduce_weight) + reduce_bias)
    result = normalize(mixed + reduced) * second_gain + second_shift
    return result.reshape(2, CAP, D) * valid[:, :, None].astype(jnp.float32)

def reference(layer_input, cotangent, timesteps, src_len, seq_len, key_keep, query_weight, query_bias, key_weight, value_weight, value_bias, output_weight, output_bias, first_gain, first_shift, expand_weight, expand_bias, reduce_weight, reduce_bias, second_gain, second_shift, time_inner, time_inner_bias, time_outer, time_outer_bias):
    params = tuple((array_item.astype(jnp.float32) for array_item in (query_weight, query_bias, key_weight, value_weight, value_bias, output_weight, output_bias, first_gain, first_shift, expand_weight, expand_bias, reduce_weight, reduce_bias, second_gain, second_shift, time_inner, time_inner_bias, time_outer, time_outer_bias)))

    def one_sequence(totals, items):
        stream_rows, stream_cot, stamp, source, length, keep_flags = items

        def apply(weights_in, rows_in):
            return layer(weights_in, rows_in, stamp, source, length, keep_flags)
        result, pull = jax.vjp(apply, params, stream_rows.astype(jnp.float32))
        param_grads, row_grads = pull(stream_cot.astype(jnp.float32))
        totals = jax.tree.map(lambda left, right: left + right, totals, param_grads)
        return (totals, (result.astype(jnp.bfloat16), row_grads.astype(jnp.bfloat16)))
    start = jax.tree.map(jnp.zeros_like, params)
    totals, (outputs, input_grads) = lax.scan(one_sequence, start, (layer_input, cotangent, timesteps, src_len, seq_len, key_keep))
    return (outputs, input_grads, totals[0], totals[1], totals[2], totals[3], totals[4], totals[5], totals[6], totals[7], totals[8], totals[9], totals[10], totals[11], totals[12], totals[13], totals[14], totals[15], totals[16], totals[17], totals[18])
```

```python
import math

import jax
import jax.numpy as jnp
from jax import lax
from jax.experimental import pallas as pl
from jax.experimental.pallas import tpu as pltpu
from jax.sharding import PartitionSpec as P

D = 768
HEADS = 12
HEAD_DIM = 64
FF = 3072
TDIM = 128
TFF = 512
CAP = 256
ROWS = 2 * CAP
EXTRA = 16

f32 = jnp.float32
bf16 = jnp.bfloat16
highest = lax.Precision.HIGHEST
norm_epsilon = 1e-12
masked_score = -1000000000.0
root_half = 0.7071067811865476
density_scale = 0.3989422804014327


def swapped(value, stage):
    axis, bit = stage
    return lax.ppermute(value, axis, [(i, i ^ (1 << bit)) for i in range(lax.axis_size(axis))])


def own_bit(stage):
    axis, bit = stage
    return (lax.axis_index(axis) >> bit) & 1


def stage_lists():
    bits = lax.axis_size("batch").bit_length() - 1
    slow_first = [("seq", 0)] + [("batch", k) for k in reversed(range(bits))]
    core, near, side = ("batch", 0), ("batch", 1), ("seq", 0)
    far = [("batch", k) for k in range(2, bits)]
    return slow_first, core, near, side, far


def added(kept, received):
    return (kept.astype(f32) + received.astype(f32)).astype(bf16)


def halves(buffer, labels, stage):
    at = labels.index(stage)
    bit = own_bit(stage)
    kept = lax.dynamic_index_in_dim(buffer, bit, axis=at, keepdims=False)
    sent = lax.dynamic_index_in_dim(buffer, 1 - bit, axis=at, keepdims=False)
    return kept, sent, labels[:at] + labels[at + 1 :]


def exchange(buffer, labels, stage, riders=None):
    kept, sent, labels = halves(buffer, labels, stage)
    rows = sent.reshape(-1, D)
    if riders is None:
        return added(kept, swapped(rows, stage).reshape(kept.shape)), labels, None
    received = swapped(jnp.concatenate([rows, riders], axis=0), stage)
    return (
        added(kept, received[: rows.shape[0]].reshape(kept.shape)),
        labels,
        added(riders, received[rows.shape[0] :]),
    )


def scattered_sum(shares, riders=None):
    slow_first, core, near, side, far = stage_lists()
    rows = shares.shape[1]
    buffer = shares.reshape((2,) * len(slow_first) + (rows, D))
    buffer, labels, riders = exchange(buffer, slow_first, core, riders)
    cut = rows // 2
    first, first_labels, riders = exchange(buffer[..., :cut, :], labels, near, riders)
    second, second_labels, _ = exchange(buffer[..., cut:, :], labels, side)
    first, first_labels, riders = exchange(first, first_labels, side, riders)
    second, second_labels, _ = exchange(second, second_labels, near)
    buffer = jnp.concatenate([first, second], axis=-2)
    labels = first_labels
    for stage in far:
        buffer, labels, riders = exchange(buffer, labels, stage, riders)
    return buffer, riders


def gathered(share):
    slow_first, core, near, side, far = stage_lists()
    order = [core, near, side] + far
    place = {stage: len(slow_first) - 1 - k for k, stage in enumerate(slow_first)}
    buffer = share[None]
    done = []
    for stage in reversed(order):
        buffer = jnp.concatenate([buffer, swapped(buffer, stage)], axis=0)
        done.append(stage)
    bits = len(order)
    buffer = buffer.reshape((2,) * bits + share.shape)
    current = list(reversed(done))
    return jnp.transpose(buffer, [current.index(stage) for stage in slow_first] + [bits, bits + 1]).reshape(
        (1 << bits,) + share.shape
    )


def unpack_kernel(me, shares, *outs):
    step = pl.program_id(0)
    per = pl.num_programs(0) // len(outs)
    for k, out in enumerate(outs):

        @pl.when(step // per == k)
        def _():
            out[0] = shares[0, : out.shape[1]].astype(f32)


def unpacked(buffer, count, me):
    devices = buffer.shape[0]
    per = devices // count
    rows = D // per
    outs = pl.pallas_call(
        unpack_kernel,
        grid_spec=pltpu.PrefetchScalarGridSpec(
            num_scalar_prefetch=1,
            grid=(devices,),
            in_specs=[pl.BlockSpec((1,) + buffer.shape[1:], lambda j, me: (j ^ me[0], 0, 0))],
            out_specs=[
                pl.BlockSpec((1, rows, D), lambda j, me, k=k: (jnp.clip(j - k * per, 0, per - 1), 0, 0))
                for k in range(count)
            ],
        ),
        out_shape=[jax.ShapeDtypeStruct((per, rows, D), f32)] * count,
    )(me.reshape(1).astype(jnp.int32), buffer)
    return [out.reshape(D, D) for out in outs]


def time_features(stamps, width):
    half_width = width // 2
    frequency = jnp.exp(-math.log(10000.0) * jnp.arange(half_width, dtype=jnp.float32) / half_width)
    angles = stamps.astype(jnp.float32)[:, None] * frequency[None, :]
    return jnp.concatenate([jnp.cos(angles), jnp.sin(angles)], axis=1)


def time_branch(inner, inner_bias, outer, outer_bias, features):
    middle = jax.nn.silu(jnp.dot(features, inner, precision=highest) + inner_bias)
    return jnp.dot(middle, outer, precision=highest) + outer_bias


def normalize(values):
    center = values - jnp.mean(values, axis=-1, keepdims=True)
    spread = jnp.mean(center * center, axis=-1, keepdims=True)
    inverse = lax.rsqrt(spread + norm_epsilon)
    return (center * inverse, inverse)


def norm_backward(upstream, normed, inverse):
    first_mean = jnp.mean(upstream, axis=-1, keepdims=True)
    second_mean = jnp.mean(upstream * normed, axis=-1, keepdims=True)
    return inverse * (upstream - first_mean - normed * second_mean)


def gelu_slope(inputs):
    return (
        0.5 * (1.0 + lax.erf(inputs * root_half))
        + inputs * jnp.exp(-0.5 * inputs * inputs) * density_scale
    )


def matmul(left, right):
    return jnp.dot(left, right, preferred_element_type=jnp.float32)


def column_sum(values):
    return jnp.sum(values.astype(f32), axis=0)


def on_device(
    layer_input,
    cotangent,
    timesteps,
    src_len,
    seq_len,
    key_keep,
    query_weight,
    query_bias,
    key_weight,
    value_weight,
    value_bias,
    output_weight,
    output_bias,
    first_gain,
    first_shift,
    expand_weight,
    expand_bias,
    reduce_weight,
    reduce_bias,
    second_gain,
    second_shift,
    time_inner,
    time_inner_bias,
    time_outer,
    time_outer_bias,
):
    stream = lax.axis_index("seq")
    devices = lax.axis_size("seq") * lax.axis_size("batch")
    me = stream * lax.axis_size("batch") + lax.axis_index("batch")
    side = ("seq", 0)

    def whole_sequence(rows):
        own = lax.dynamic_index_in_dim(rows[:, 0], stream, axis=0, keepdims=False)
        other = lax.dynamic_index_in_dim(rows[:, 0], 1 - stream, axis=0, keepdims=False)
        return own, swapped(other, side)

    def both_sequences(rows):
        own, far = rows[:CAP], swapped(rows[CAP:], side)
        return jnp.where(stream == 0, jnp.stack([own, far]), jnp.stack([far, own]))[:, None]

    input_rows = jnp.concatenate(whole_sequence(layer_input), axis=0)
    cotangent_rows = jnp.concatenate(whole_sequence(cotangent), axis=0)
    pick = lambda values: lax.dynamic_index_in_dim(values, stream, axis=0, keepdims=False)
    source, target = pick(src_len), pick(seq_len) - pick(src_len)
    own_length = jnp.where(stream == 0, source, target)
    far_length = jnp.where(stream == 0, target, source)
    slots = jnp.arange(CAP)
    valid = jnp.concatenate([slots < own_length, slots < far_length])
    flags = pick(key_keep)
    keep = jnp.where(stream == 0, flags, flags[::-1]).reshape(ROWS) == 1
    allowed = jnp.logical_and(valid, keep)
    row_mask = valid.astype(f32)[:, None]

    features = time_features(pick(timesteps)[None], TDIM)
    inner_sum = jnp.dot(features, time_inner.astype(f32), precision=highest) + time_inner_bias
    gate = jax.nn.sigmoid(inner_sum)
    middle = inner_sum * gate
    time_vector = jnp.dot(middle, time_outer.astype(f32), precision=highest) + time_outer_bias

    hidden = input_rows.astype(f32) + time_vector
    hidden_low = hidden.astype(bf16)
    queries = (matmul(hidden_low, query_weight) + query_bias).astype(bf16)
    keys = matmul(hidden_low, key_weight).astype(bf16)
    values = (matmul(hidden_low, value_weight) + value_bias).astype(bf16)
    heads = lambda rows: rows.reshape(ROWS, HEADS, HEAD_DIM)
    query_heads, key_heads, value_heads = heads(queries), heads(keys), heads(values)
    scores = jnp.einsum("qhd,khd->hqk", query_heads, key_heads, preferred_element_type=f32) * 0.125
    scores = jnp.where(allowed, scores, masked_score)
    top = jnp.max(scores, axis=-1, keepdims=True)
    exponent = jnp.exp(scores - top)
    probs = exponent / jnp.sum(exponent, axis=-1, keepdims=True)
    probs_low = probs.astype(bf16)
    attended = jnp.einsum("hqk,khd->qhd", probs_low, value_heads, preferred_element_type=f32)
    attended = attended.astype(bf16).reshape(ROWS, D)
    first_sum = hidden + matmul(attended, output_weight) + output_bias
    first_normed, first_inverse = normalize(first_sum)
    mixed = first_normed * first_gain + first_shift
    mixed_low = mixed.astype(bf16)
    expanded = matmul(mixed_low, expand_weight) + expand_bias
    activated = jax.nn.gelu(expanded, approximate=False).astype(bf16)
    second_sum = mixed + matmul(activated, reduce_weight) + reduce_bias
    second_normed, second_inverse = normalize(second_sum)
    output = both_sequences(((second_normed * second_gain + second_shift) * row_mask).astype(bf16))

    d_out = cotangent_rows.astype(f32) * row_mask
    grad_second_shift = jnp.sum(d_out, axis=0)
    grad_second_gain = jnp.sum(d_out * second_normed, axis=0)
    d_second = norm_backward(d_out * second_gain, second_normed, second_inverse)
    d_reduced = d_second.astype(bf16)
    grad_reduce_bias = column_sum(d_reduced)
    grad_reduce = matmul(activated.T, d_reduced).astype(bf16)
    reduce_share, _ = scattered_sum(grad_reduce.reshape(devices, FF // devices, D))
    d_expanded = (matmul(d_reduced, reduce_weight.T) * gelu_slope(expanded)).astype(bf16)
    grad_expand_bias = column_sum(d_expanded)
    grad_expand = matmul(d_expanded.T, mixed_low).astype(bf16)
    expand_share, _ = scattered_sum(grad_expand.reshape(devices, FF // devices, D))
    d_mixed = d_second + matmul(d_expanded, expand_weight.T)
    grad_first_shift = jnp.sum(d_mixed, axis=0)
    grad_first_gain = jnp.sum(d_mixed * first_normed, axis=0)
    d_first = norm_backward(d_mixed * first_gain, first_normed, first_inverse)
    d_branch = d_first.astype(bf16)
    grad_output_bias = column_sum(d_branch)
    grad_output = matmul(attended.T, d_branch).astype(bf16)
    d_attended = matmul(d_branch, output_weight.T).astype(bf16)
    d_heads = heads(d_attended)
    d_values = jnp.einsum("hqk,qhd->khd", probs_low, d_heads, preferred_element_type=f32)
    d_probs = jnp.einsum("qhd,khd->hqk", d_heads, value_heads, preferred_element_type=f32)
    center = jnp.sum(probs * d_probs, axis=-1, keepdims=True)
    d_scores = jnp.where(allowed, probs * (d_probs - center), 0.0).astype(bf16)
    d_queries = 0.125 * jnp.einsum("hqk,khd->qhd", d_scores, key_heads, preferred_element_type=f32)
    d_keys = 0.125 * jnp.einsum("hqk,qhd->khd", d_scores, query_heads, preferred_element_type=f32)
    query_low = d_queries.astype(bf16).reshape(ROWS, D)
    key_low = d_keys.astype(bf16).reshape(ROWS, D)
    value_low = d_values.astype(bf16).reshape(ROWS, D)
    small = [matmul(hidden_low.T, low).astype(bf16) for low in (query_low, key_low, value_low)]
    small.append(grad_output)
    d_hidden = (
        d_first
        + matmul(query_low, query_weight.T)
        + matmul(key_low, key_weight.T)
        + matmul(value_low, value_weight.T)
    )
    input_grad = both_sequences(d_hidden.astype(bf16))

    riders = jnp.stack(
        [
            column_sum(query_low),
            column_sum(value_low),
            grad_output_bias,
            grad_first_gain,
            grad_first_shift,
            grad_reduce_bias,
            grad_second_gain,
            grad_second_shift,
        ]
    )
    riders = jnp.concatenate([riders, grad_expand_bias.reshape(4, D), jnp.zeros((4, D), f32)], axis=0)
    small = jnp.concatenate(small, axis=0).reshape(devices, 4 * D // devices, D)
    small_share, riders = scattered_sum(small, riders.astype(bf16))
    riders = riders.astype(f32)

    d_time = jnp.sum(d_hidden, axis=0, keepdims=True)
    d_middle = jnp.dot(d_time, time_outer.astype(f32).T, precision=highest)
    d_inner = d_middle * (gate * (1.0 + inner_sum * (1.0 - gate)))
    factors = jnp.concatenate([d_time, d_inner, middle, features], axis=1).astype(bf16)
    factors = jnp.pad(factors, ((0, 0), (0, EXTRA * D - factors.shape[1]))).reshape(EXTRA, D)
    everyone = gathered(jnp.concatenate([small_share, factors], axis=0))
    grad_query, grad_key, grad_value, grad_output = unpacked(everyone, 4, me)
    factors = everyone[:, -EXTRA:].reshape(devices, EXTRA * D)
    cuts = (0, D, D + TFF, D + 2 * TFF, D + 2 * TFF + TDIM)
    d_time, d_inner, middle, features = [factors[:, a:b] for a, b in zip(cuts, cuts[1:])]
    return (
        output,
        input_grad,
        grad_query,
        riders[0],
        grad_key,
        grad_value,
        riders[1],
        grad_output,
        riders[2],
        riders[3],
        riders[4],
        expand_share.astype(f32).T,
        riders[8:12].reshape(FF),
        reduce_share.astype(f32),
        riders[5],
        riders[6],
        riders[7],
        matmul(features.T, d_inner),
        column_sum(d_inner),
        matmul(middle.T, d_time),
        column_sum(d_time),
    )


def solution(mesh):
    rows = P("batch", "seq", None, None)
    in_specs = (rows, rows, P("batch"), P("batch"), P("batch"), P("batch", None, None)) + (P(),) * 19
    out_specs = (rows, rows) + (P(),) * 9 + (P(None, ("seq", "batch")), P(), P(("seq", "batch"), None)) + (P(),) * 7
    return jax.shard_map(on_device, mesh=mesh, in_specs=in_specs, out_specs=out_specs, check_vma=False)
```

```python
import functools
import math

import jax
import jax.numpy as jnp
from jax import lax
from jax.experimental import pallas as pl
from jax.experimental.pallas import tpu as pltpu
from jax.sharding import PartitionSpec as P

D = 768
HEADS = 12
HEAD_DIM = 64
FF = 3072
TDIM = 128
TFF = 512
CAP = 256
ROWS = 2 * CAP

f32 = jnp.float32
bf16 = jnp.bfloat16
highest = lax.Precision.HIGHEST
norm_epsilon = 1e-12
masked_score = -1000000000.0
root_half = 0.7071067811865476
density_scale = 0.3989422804014327


core, near, side = ("c", 0), ("x", 0), ("y", 0)


def swapped(value, stage):
    axis, bit = stage
    return lax.ppermute(value, axis, [(i, i ^ (1 << bit)) for i in range(lax.axis_size(axis))])


def own_bit(stage):
    axis, bit = stage
    return (lax.axis_index(axis) >> bit) & 1


def stage_lists():
    bits = lax.axis_size("z").bit_length() - 1
    far = [("z", k) for k in range(bits)]
    return [side] + far[::-1] + [near, core], far


def added(kept, received):
    return lax.reduce_precision(kept.astype(f32) + received.astype(f32), 8, 7).astype(bf16)


def halves(buffer, labels, stage):
    at = labels.index(stage)
    bit = own_bit(stage)
    kept = lax.dynamic_index_in_dim(buffer, bit, axis=at, keepdims=False)
    sent = lax.dynamic_index_in_dim(buffer, 1 - bit, axis=at, keepdims=False)
    return kept, sent, labels[:at] + labels[at + 1 :]


def exchange(buffer, labels, stage, riders=None):
    kept, sent, labels = halves(buffer, labels, stage)
    rows = sent.reshape(-1, D)
    if riders is None:
        return added(kept, swapped(rows, stage).reshape(kept.shape)), labels, None
    received = swapped(jnp.concatenate([rows, riders], axis=0), stage)
    return (
        added(kept, received[: rows.shape[0]].reshape(kept.shape)),
        labels,
        added(riders, received[rows.shape[0] :]),
    )


def scattered_sum(shares, riders=None):
    slow_first, far = stage_lists()
    rows = shares.shape[1]
    buffer = shares.reshape((2,) * len(slow_first) + (rows, D))
    buffer, labels, riders = exchange(buffer, slow_first, core, riders)
    cut = rows // 2
    first, first_labels, riders = exchange(buffer[..., :cut, :], labels, near, riders)
    second, second_labels, _ = exchange(buffer[..., cut:, :], labels, side)
    first, first_labels, riders = exchange(first, first_labels, side, riders)
    second, second_labels, _ = exchange(second, second_labels, near)
    buffer = jnp.concatenate([first, second], axis=-2)
    labels = first_labels
    for stage in far:
        buffer, labels, riders = exchange(buffer, labels, stage, riders)
    return buffer, riders


def gathered(share):
    slow_first, far = stage_lists()
    order = [core, near, side] + far
    buffer = share[None]
    done = []
    for stage in reversed(order):
        buffer = jnp.concatenate([buffer, swapped(buffer, stage)], axis=0)
        done.append(stage)
    bits = len(order)
    buffer = buffer.reshape((2,) * bits + share.shape)
    current = list(reversed(done))
    return jnp.transpose(buffer, [current.index(stage) for stage in slow_first] + [bits, bits + 1]).reshape(
        (1 << bits,) + share.shape
    )


def matmul(left, right):
    return jnp.dot(left, right, preferred_element_type=f32)


def column_sum(values):
    return jnp.sum(values.astype(f32), axis=0)


def dot(left, right, dims):
    return lax.dot_general(left, right, (((dims[0],), (dims[1],)), ((), ())), preferred_element_type=f32)


def nn(left, right):
    return dot(left, right, (1, 0))


def nt(left, right):
    return dot(left, right, (1, 1))


def tn(left, right):
    return dot(left, right, (0, 0))


def whole(*shape):
    return pl.BlockSpec(shape, lambda *at: (0,) * len(shape))


def vector(size):
    return pl.BlockSpec((size,), lambda *at: (0,))


def vector_tile(width):
    return pl.BlockSpec((width,), lambda j, *at: (j,))


def row(ref):
    return ref[...].reshape(1, -1)


def column_tile(rows, width):
    return pl.BlockSpec((rows, width), lambda j, *at: (0, j))


def row_tile(height, width):
    return pl.BlockSpec((height, width), lambda j, *at: (j, 0))


def run(body, grid, operands, in_specs, outs, out_specs, flops, scratch=(), scalars=(), after=(), aliases=None):
    shapes = [jax.ShapeDtypeStruct(shape, dtype) for shape, dtype in outs]
    sizes = [x.size * x.dtype.itemsize for x in list(operands) + shapes]
    used = len(scalars) + len(operands)

    def wrapped(*refs):
        body(*refs[:used], *refs[used + len(after) :])

    return pl.pallas_call(
        wrapped,
        grid_spec=pltpu.PrefetchScalarGridSpec(
            num_scalar_prefetch=len(scalars),
            grid=grid,
            in_specs=in_specs + [pl.BlockSpec(memory_space=pl.ANY)] * len(after),
            out_specs=out_specs,
            scratch_shapes=scratch,
        ),
        out_shape=shapes,
        input_output_aliases=aliases or {},
        compiler_params=pltpu.CompilerParams(vmem_limit_bytes=63 << 20),
        cost_estimate=pl.CostEstimate(flops=int(flops), bytes_accessed=sum(sizes), transcendentals=0),
    )(*scalars, *operands, *after)


def nothing(*refs):
    pass


def tie(values, after):
    anywhere = pl.BlockSpec(memory_space=pl.ANY)
    return pl.pallas_call(
        nothing,
        in_specs=[anywhere] * (len(values) + len(after)),
        out_specs=[anywhere] * len(values),
        out_shape=[jax.ShapeDtypeStruct(value.shape, value.dtype) for value in values],
        input_output_aliases={k: k for k in range(len(values))},
    )(*values, *after)


def normalized(values):
    center = values - jnp.mean(values, axis=-1, keepdims=True)
    spread = jnp.mean(center * center, axis=-1, keepdims=True)
    inverse = lax.rsqrt(spread + norm_epsilon)
    return center * inverse, inverse


def norm_backward(upstream, normed, inverse):
    first_mean = jnp.mean(upstream, axis=-1, keepdims=True)
    second_mean = jnp.mean(upstream * normed, axis=-1, keepdims=True)
    return inverse * (upstream - first_mean - normed * second_mean)


def row_sum(values):
    return jnp.sum(values, axis=0, keepdims=True)


def prepare_body(bits, stamps, src_len, seq_len, flags, inner, inner_bias, outer, outer_bias, *outs):
    features, inner_sum, middle, stamp, allowed, valid, masked = outs
    y = bits[2]
    lane = lax.broadcasted_iota(jnp.int32, (1, TDIM), 1)
    half = TDIM // 2
    frequency = jnp.exp(-math.log(10000.0) * lax.rem(lane, half).astype(f32) / half)
    angles = jnp.broadcast_to(stamps[y].astype(f32), (1, TDIM)) * frequency
    waves = jnp.where(lane < half, jnp.cos(angles), jnp.sin(angles))
    features[...] = waves
    total = jnp.dot(waves, inner[...].astype(f32), precision=highest) + row(inner_bias)
    inner_sum[...] = total
    gated = total * (1.0 / (1.0 + jnp.exp(-total)))
    middle[...] = gated
    stamp[...] = jnp.dot(gated, outer[...].astype(f32), precision=highest) + row(outer_bias)
    source, target = src_len[y], seq_len[y] - src_len[y]
    slots = lax.broadcasted_iota(jnp.int32, (CAP, 1), 0)
    lengths = jnp.where(y == 0, source, target), jnp.where(y == 0, target, source)
    for at, (length, stream) in enumerate(zip(lengths, (y, 1 - y))):
        inside = jnp.where(slots < length, 1.0, 0.0)
        kept = jnp.where(flags[y, pl.ds(stream, 1)] == 1, 1.0, 0.0)
        kept = jnp.broadcast_to(kept, (8, CAP)).T[:, :1]
        here = slice(at * CAP, (at + 1) * CAP)
        valid[here] = inside
        allowed[here] = inside * kept
        masked[here] = (1.0 - inside * kept) * masked_score


def prepare(bits, stamps, src_len, seq_len, flags, inner, inner_bias, outer, outer_bias):
    return run(
        prepare_body,
        (1,),
        (flags, inner, inner_bias, outer, outer_bias),
        [whole(2, 2, CAP), whole(TDIM, TFF), vector(TFF), whole(TFF, D), vector(D)],
        [((1, size), f32) for size in (TDIM, TFF, TFF, D)] + [((ROWS, 1), f32)] * 3,
        [whole(1, size) for size in (TDIM, TFF, TFF, D)] + [whole(ROWS, 1)] * 3,
        0,
        scalars=(bits, stamps, src_len, seq_len),
    )


def project_body(rows, stamp, keep, qw, qb, kw, vw, vb, q, k, v, low_out):
    low = (rows[...].astype(f32) + stamp[...]).astype(bf16)
    low_out[...] = low
    q[...] = ((nn(low, qw[...]) + row(qb)).astype(bf16).astype(f32) * 0.125).astype(bf16)
    k[...] = (nn(low, kw[...]) * keep[...]).astype(bf16)
    v[...] = (nn(low, vw[...]) + row(vb)).astype(bf16)


def project(rows, half, stamp, keep, qw, qb, kw, vw, vb):
    tile = 256
    return run(
        project_body,
        (D // tile,),
        (rows, stamp, keep, qw, qb, kw, vw, vb),
        [whole(CAP, D), whole(1, D), pl.BlockSpec((CAP, 1), lambda *at: (half, 0))]
        + [column_tile(D, tile), vector_tile(tile), column_tile(D, tile), column_tile(D, tile), vector_tile(tile)],
        [((CAP, D), bf16)] * 4,
        [column_tile(CAP, tile)] * 3 + [whole(CAP, D)],
        6 * CAP * D * D,
    )


def lanes_of(shape):
    return lax.broadcasted_iota(jnp.int32, shape, 1)


def both(own, far):
    return jnp.concatenate([own[...], far[...]], axis=0)


def attend_body(qo, qf, ko, kf, vo, vf, lo, lf, masked, attended, for_core, probs):
    q, k, v = both(qo, qf), both(ko, kf), both(vo, vf)
    lane = lanes_of(q.shape)
    flag = jnp.broadcast_to(masked[...], q.shape).astype(bf16)
    v_turned = v.T
    pieces = []
    for head in range(2):
        mine = (lane // HEAD_DIM) == head
        spare = lane == (1 - head) * HEAD_DIM
        k_head = jnp.where(mine, k, jnp.where(spare, flag, 0))
        q_head = jnp.where(mine, q, jnp.where(spare, 1, 0).astype(bf16))
        scores = nt(k_head, q_head)
        top = jnp.max(scores, axis=0, keepdims=True)
        exponent = jnp.exp(scores - top)
        inverse = 1.0 / jnp.sum(exponent, axis=0, keepdims=True)
        low = (exponent * inverse).astype(bf16)
        probs[head] = low
        pieces.append(nn(v_turned[head * HEAD_DIM : (head + 1) * HEAD_DIM], low))
    low = jnp.concatenate(pieces, axis=0).T.astype(bf16)
    attended[...] = low
    for_core[0], for_core[1] = both(lo, lf), low


def attend(q, k, v, low, masked):
    pair = 2 * HEAD_DIM
    return run(
        attend_body,
        (D // pair,),
        (*q, *k, *v, *low, masked),
        [column_tile(CAP, pair)] * 8 + [whole(ROWS, 1)],
        [((ROWS, D), bf16), ((2, ROWS, D), bf16), ((HEADS, ROWS, ROWS), bf16)],
        [column_tile(ROWS, pair), pl.BlockSpec((2, ROWS, pair), lambda j: (0, 0, j))]
        + [pl.BlockSpec((2, ROWS, ROWS), lambda j: (j, 0, 0))],
        4 * HEADS * ROWS * ROWS * 256,
    )


SHARE = 96
COLOUR = 48


half_tile = pl.BlockSpec((ROWS, D // 2), lambda j, *at: (0, j))


FOR_CORE = (ROWS, FF + 2 * D)


def by_core(values):
    return [
        jnp.concatenate([values[:, at : at + SHARE] for at in range(start, D, 2 * SHARE)], axis=1) for start in (0, SHARE)
    ]


def store_by_core(bits, values, other, own):
    zero, one = by_core(values)

    @pl.when(bits[0] == 0)
    def _():
        own[...], other[...] = zero, one

    @pl.when(bits[0] == 1)
    def _():
        own[...], other[...] = one, zero


def feed_forward_body(
    bits, attended, own, far, stamp, ow, ob, gain, shift, ew, eb, rw, rb, gain2, shift2, valid, cot_own, cot_far,
    output, for_core, activated_own, slope, mixed_low, normed, inverse, d_second, d_reduced, sums, mixed, total,
    activated,
):
    step = pl.program_id(0)

    @pl.when(step == 0)
    def _():
        hidden = both(own, far).astype(f32) + stamp[...]
        n1, inv = normalized(hidden + nn(attended[...], ow[...]) + row(ob))
        value = n1 * row(gain) + row(shift)
        normed[...] = n1
        inverse[...] = inv
        mixed[...] = value
        mixed_low[...] = value.astype(bf16)
        total[...] = value + row(rb)

    added_up = None
    bias = eb[pl.ds(pl.multiple_of(step * D, D), D)].reshape(1, -1)
    for part in range(D // SUB):
        cut = slice(part * SUB, (part + 1) * SUB)
        expanded = nn(mixed_low[...], ew[:, cut]) + bias[:, cut]
        chance = 0.5 * (1.0 + lax.erf(expanded * root_half))
        slope[:, cut] = chance + expanded * jnp.exp(-0.5 * expanded * expanded) * density_scale
        low = (expanded * chance).astype(bf16)
        activated[:, cut] = low
        product = nn(low, rw[cut, :])
        added_up = product if added_up is None else added_up + product
    total[...] += added_up
    here = pl.ds(pl.multiple_of(step * (D // 2), D // 2), D // 2)
    store_by_core(bits, activated[...], for_core.at[:, here], activated_own)

    @pl.when(step == pl.num_programs(0) - 1)
    def _():
        n2, inv = normalized(total[...])
        weight = valid[...]
        output[...] = ((n2 * row(gain2) + row(shift2)) * weight).astype(bf16)
        d_out = both(cot_own, cot_far).astype(f32) * weight
        back = norm_backward(d_out * row(gain2), n2, inv)
        low = back.astype(bf16)
        d_second[...] = back
        d_reduced[...] = low
        for_core[:, 2 * D : 3 * D] = low
        for_core[:, 3 * D :] = mixed_low[...]
        sums[...] = jnp.concatenate(
            [jnp.zeros((5, D), f32), row_sum(low.astype(f32)), row_sum(d_out * n2), row_sum(d_out)], axis=0
        )


SUB = 256


def feed_forward(
    bits, attended, own, far, stamp, ow, ob, gain, shift, ew, eb, rw, rb, gain2, shift2, valid, cot_own, cot_far
):
    line, square, half = vector(D), whole(ROWS, D), whole(CAP, D)
    return run(
        feed_forward_body,
        (FF // D,),
        (attended, own, far, stamp, ow, ob, gain, shift, ew, eb, rw, rb, gain2, shift2, valid, cot_own, cot_far),
        [square, half, half, whole(1, D), whole(D, D), line, line, line, column_tile(D, D), vector(FF), row_tile(D, D)]
        + [line, line, line, whole(ROWS, 1), half, half],
        [
            ((ROWS, D), bf16),
            (FOR_CORE, bf16),
            ((ROWS, FF // 2), bf16),
            ((ROWS, FF), f32),
            ((ROWS, D), bf16),
            ((ROWS, D), f32),
            ((ROWS, 1), f32),
            ((ROWS, D), f32),
            ((ROWS, D), bf16),
            ((8, D), f32),
        ],
        [square, whole(ROWS, 4 * D), half_tile, column_tile(ROWS, D), square, square, whole(ROWS, 1), square, square, whole(8, D)],
        2 * ROWS * D * (D + 2 * FF),
        scratch=[pltpu.VMEM((ROWS, D), f32)] * 2 + [pltpu.VMEM((ROWS, D), bf16)],
        scalars=(bits,),
    )


def hidden_grad_body(bits, activated, d_reduced, d_expanded, mixed, activated_got, reduced_got, mixed_got, expanded_got, kept, sent):
    step = pl.program_id(0)
    tile = step % 2

    def store(kind, grad):
        low = grad.astype(bf16)
        for at in range(8):
            x, z = at % 2, at // 2
            here = jnp.where(bits[0] == 0, tile, x) * 4 + (z % 2 * 2 + z // 2)
            block = low[at * SHARE : (at + 1) * SHARE]
            mine = jnp.where(bits[0] == 0, x, tile) == bits[5]

            @pl.when(mine)
            def _():
                kept[here, kind] = block

            @pl.when(jnp.logical_not(mine))
            def _():
                sent[here, kind] = block

    @pl.when(step < 2)
    def _():
        store(0, tn(activated[...], d_reduced[...]) + tn(activated_got[...], reduced_got[...]))

    @pl.when(step >= 2)
    def _():
        store(1, tn(d_expanded[...], mixed[...]) + tn(expanded_got[...], mixed_got[...]))


def hidden_grad(bits, activated, d_reduced, d_expanded, mixed, got, after):
    first = lambda start: pl.BlockSpec((ROWS, D), lambda j, bits: (0, start + jnp.minimum(j, 1)))
    second = lambda start: pl.BlockSpec((ROWS, D), lambda j, bits: (0, start + jnp.maximum(j - 2, 0)))
    square = lambda at: pl.BlockSpec((ROWS, D), lambda j, bits: (0, at))
    return run(
        hidden_grad_body,
        (4,),
        (activated, d_reduced, d_expanded, mixed, got, got, got, got),
        [first(0), square(0), second(0), square(0), first(0), square(2), square(3), second(4)],
        [((8, 2, SHARE, D), bf16)] * 2,
        [whole(8, 2, SHARE, D)] * 2,
        4 * ROWS * D * FF,
        scalars=(bits,),
        after=after,
    )


def expand_back_body(
    bits, d_reduced, rw, slope, ew, d_second, normed, inverse, gain, for_core,
    expanded_other, expanded_own, bias, d_first, d_branch, sums, total,
):
    step = pl.program_id(0)
    d_expanded = (nt(d_reduced[...], rw[...]) * slope[...]).astype(bf16)
    bias[0] = row_sum(d_expanded.astype(f32))
    store_by_core(bits, d_expanded, expanded_other, expanded_own)
    product = nt(d_expanded, ew[...])

    @pl.when(step == 0)
    def _():
        total[...] = d_second[...] + product

    @pl.when(step > 0)
    def _():
        total[...] += product

    @pl.when(step == pl.num_programs(0) - 1)
    def _():
        d_mixed = total[...]
        n1 = normed[...]
        back = norm_backward(d_mixed * row(gain), n1, inverse[...])
        low = back.astype(bf16)
        d_first[...] = back
        d_branch[...] = low
        sums[...] = jnp.concatenate(
            [jnp.zeros((2, D), f32), row_sum(low.astype(f32)), row_sum(d_mixed * n1), row_sum(d_mixed), jnp.zeros((3, D), f32)],
            axis=0,
        )


def expand_back(bits, d_reduced, rw, slope, ew, d_second, normed, inverse, gain, for_core, after):
    steps = FF // D
    square = whole(ROWS, D)
    return run(
        expand_back_body,
        (steps,),
        (d_reduced, rw, slope, ew, d_second, normed, inverse, gain, for_core),
        [square, row_tile(D, D), column_tile(ROWS, D), column_tile(D, D), square, square, whole(ROWS, 1), vector(D)]
        + [pl.BlockSpec(memory_space=pl.ANY)],
        [(FOR_CORE, bf16), ((ROWS, FF // 2), bf16)] + [((steps, 1, D), f32), ((ROWS, D), f32), ((ROWS, D), bf16), ((8, D), f32)],
        [pl.BlockSpec((ROWS, D // 2), lambda j, *at: (0, 8 + j)), half_tile]
        + [pl.BlockSpec((1, 1, D), lambda j, *at: (j, 0, 0)), square, square, whole(8, D)],
        4 * ROWS * D * FF,
        scratch=[pltpu.VMEM((ROWS, D), f32)],
        aliases={9: 0},
        scalars=(bits,),
        after=after,
    )


def attend_back_body(bits, d_branch, branch, ow, probs, qo, qf, ko, kf, vo, vf, keep, grads, kept, sent, sums):
    q, k, v = both(qo, qf), both(ko, kf), both(vo, vf)
    lane = lanes_of(q.shape)
    low_half = lane < HEAD_DIM
    upstream = nt(d_branch[...], ow[...]).astype(bf16)
    k_turned = k.T
    d_q, d_k, d_v = [], [], []
    for head in range(2):
        rows = slice(head * HEAD_DIM, (head + 1) * HEAD_DIM)
        mine = low_half if head == 0 else jnp.logical_not(low_half)
        low = probs[head]
        wide = low.astype(f32)
        weighted = wide * nt(jnp.where(mine, v, 0), upstream)
        d_scores = (weighted - wide * row_sum(weighted)).astype(bf16)
        d_v.append(nn(low, upstream))
        d_k.append(nn(d_scores, q))
        d_q.append(nn(k_turned[rows], d_scores))
    q_low = (jnp.concatenate(d_q, axis=0).T * 0.125).astype(bf16)
    v_low = jnp.where(low_half, d_v[0], d_v[1]).astype(bf16)
    k_low = (jnp.where(low_half, d_k[0], d_k[1]) * keep[...]).astype(bf16)
    grads[0], grads[1], grads[2] = q_low, k_low, v_low

    def share(first, second):
        first[0], first[1] = q_low, k_low
        second[0], second[1] = v_low, branch[...]

    @pl.when(bits[0] == 0)
    def _():
        share(kept, sent)

    @pl.when(bits[0] == 1)
    def _():
        share(sent, kept)

    sums[...] = jnp.concatenate(
        [row_sum(q_low.astype(f32)), row_sum(v_low.astype(f32)), jnp.zeros((6, q.shape[1]), f32)], axis=0
    )


def attend_back(bits, d_branch, ow, probs, q, k, v, keep, after):
    pair = 2 * HEAD_DIM
    return run(
        attend_back_body,
        (D // pair,),
        (d_branch, d_branch, ow, probs, *q, *k, *v, keep),
        [whole(ROWS, D), column_tile(ROWS, pair), row_tile(pair, D), pl.BlockSpec((2, ROWS, ROWS), lambda j, *at: (j, 0, 0))]
        + [column_tile(CAP, pair)] * 6
        + [whole(ROWS, 1)],
        [((count, ROWS, D), bf16) for count in (3, 2, 2)] + [((8, D), f32)],
        [pl.BlockSpec((count, ROWS, pair), lambda j, *at: (0, 0, j)) for count in (3, 2, 2)] + [column_tile(8, pair)],
        10 * HEADS * ROWS * ROWS * 256,
        scalars=(bits,),
        after=after,
    )


def pair_grad_body(bits, left, right, left_got, right_got, kept, sent):
    low = (tn(left[0], right[0]) + tn(left_got[0], right_got[0])).astype(bf16)
    zero, one = [low[at * D // 2 : (at + 1) * D // 2].reshape(8, COLOUR, D) for at in range(2)]
    kept[:, 0] = jnp.where(bits[5] == 0, zero, one)
    sent[:, 0] = jnp.where(bits[5] == 0, one, zero)


def pair_grad(bits, left, right, left_got, right_got, after):
    lefts = pl.BlockSpec((1, ROWS, D), lambda j, bits: (j * bits[0], 0, 0))
    rights = pl.BlockSpec((1, ROWS, D), lambda j, bits: (j, 0, 0))
    return run(
        pair_grad_body,
        (2,),
        (left, right, left_got, right_got),
        [lefts, rights] * 2,
        [((8, 2, COLOUR, D), bf16)] * 2,
        [pl.BlockSpec((8, 1, COLOUR, D), lambda j, *at: (0, j, 0, 0))] * 2,
        8 * ROWS * D * D,
        scalars=(bits,),
        after=after,
    )


def input_grad_body(grads, qw, kw, vw, d_first, d_rows, d_time):
    total = d_first[...] + nt(grads[0], qw[...]) + nt(grads[1], kw[...]) + nt(grads[2], vw[...])
    d_rows[...] = total.astype(bf16)
    d_time[...] = row_sum(total)


def input_grad(grads, qw, kw, vw, d_first, after):
    tile = 256
    return run(
        input_grad_body,
        (D // tile,),
        (grads, qw, kw, vw, d_first),
        [whole(3, ROWS, D)] + [row_tile(tile, D)] * 3 + [column_tile(ROWS, tile)],
        [((ROWS, D), bf16), ((1, D), f32)],
        [column_tile(ROWS, tile), column_tile(1, tile)],
        6 * ROWS * D * D,
        after=after,
    )


everywhere = ("y", "z", "x", "c")
low_far, high_far = ("z", 0), ("z", 1)


def crossed(value, first):
    sizes = [lax.axis_size(axis) for axis in everywhere]
    pairs = []
    for at in range(math.prod(sizes)):
        c, x = at % 2, at // 2 % 2
        along_x = (c == 0) == first
        step = 2 * (1 - 2 * x) if along_x else (math.prod(sizes) // 2) * (1 - 2 * (at // (math.prod(sizes) // 2)))
        pairs.append((at, at + step))
    return lax.ppermute(value, everywhere, pairs)


def plus(left, right):
    return (left.astype(f32) + right.astype(f32)).astype(bf16)


def halved(own, got, bit):
    own, got = [value.reshape((2, -1) + value.shape[1:]) for value in (own, got)]
    at = lambda place: [lax.dynamic_index_in_dim(value, place, 0, keepdims=False) for value in (own, got)]
    return plus(*at(bit)), plus(*at(1 - bit))


BLOCK = 32


def block_body(bits, first, second, third, bias, d_time, inner_sum, middle, features, outer, out):
    riders = first[...] + second[...] + third[...]
    total = inner_sum[...]
    gate = 1.0 / (1.0 + jnp.exp(-total))
    d_middle = lax.dot_general(
        d_time[...], outer[...].astype(f32), (((1,), (1,)), ((), ())), precision=highest, preferred_element_type=f32
    )
    d_inner = d_middle * (gate * (1.0 + total * (1.0 - gate)))
    wide = D - TFF
    rows = [jnp.concatenate([d_time[:, at * wide : (at + 1) * wide], middle[...]], axis=1) for at in range(3)]
    rows.append(jnp.concatenate([d_inner, features[...], jnp.zeros((1, wide - TDIM), f32)], axis=1))
    index = lax.broadcasted_iota(jnp.int32, (16, D), 0)
    factors = jnp.zeros((16, D), f32)
    for at, values in enumerate(rows):
        factors = jnp.where(index == 4 * (bits[3] + 2 * bits[4]) + at, values, factors)
    biases = jnp.zeros((8, D), f32)
    index = lax.broadcasted_iota(jnp.int32, (8, D), 0)
    for at in range(4):
        biases = jnp.where(index == at, bias[at], biases)
    out[...] = jnp.concatenate([riders, biases, factors], axis=0).astype(bf16)


def block_rows(bits, *operands):
    return run(
        block_body,
        (1,),
        operands,
        [whole(*operand.shape) for operand in operands],
        [((BLOCK, D), bf16)],
        [whole(BLOCK, D)],
        0,
        scalars=(bits,),
    )[0]


def sum_rows(own, got):
    return lax.reduce_precision(own.astype(f32) + got.astype(f32), 8, 7).astype(bf16)


def longer(data, block, send, join):
    got = send(jnp.concatenate([data, block]))
    size = data.shape[0]
    data, got = jnp.concatenate([data, got[:size]]), got[size:]
    if not join:
        return data, sum_rows(block, got)
    return data, jnp.concatenate([sum_rows(block[:16], got[:16]), block[16:], got[16:]])


def unpack_body(bits, own, got, *refs):
    outs = refs[-4:]
    for at in range(8):
        here, there = (bits[6] % 8) ^ at, (bits[7] % 8) ^ at
        for matrix in range(2):
            rows = slice(at * SHARE + matrix * COLOUR, at * SHARE + (matrix + 1) * COLOUR)
            mine, other = own[rows].astype(f32), got[rows].astype(f32)
            outs[matrix][here] = jnp.where(bits[0] == 0, mine, other)
            outs[2 + matrix][there] = jnp.where(bits[0] == 0, other, mine)


def unpack(bits, own, got, turn, outs):
    shape = (16, COLOUR, D)
    blocks = [pl.BlockSpec((8, COLOUR, D), lambda j, bits, at=at: ((bits[at] // 8) ^ turn, 0, 0)) for at in (6, 7)]
    return run(
        unpack_body,
        (1,),
        (own, got, *outs),
        [whole(D, D)] * 2 + [pl.BlockSpec(memory_space=pl.ANY)] * len(outs),
        [(shape, f32)] * 4,
        [blocks[0]] * 2 + [blocks[1]] * 2,
        0,
        scalars=(bits,),
        aliases={3 + k: k for k in range(len(outs))},
    )


def finish_body(own, turned, own_far, turned_far, *outs):
    blocks = [ref[...].astype(f32) for ref in (own, turned, own_far, turned_far)]
    sums = (blocks[0][:16] + blocks[1][:16]) + (blocks[2][:16] + blocks[3][:16])
    for at in range(8):
        outs[at][...] = sums[at]
    for at in range(4):
        outs[8][at] = sums[8 + at : 9 + at]
    factors = jnp.concatenate([block[16:] for block in blocks], axis=0)
    index = lax.broadcasted_iota(jnp.int32, factors.shape, 0) % 4
    wide = D - TFF
    inner, inner_bias, outer, outer_bias = outs[9:]
    for at in range(3):
        rows = jnp.where(index == at, factors, 0.0)
        d_time = rows[:, :wide]
        here = slice(at * wide, (at + 1) * wide)
        outer[:, here] = tn(rows[:, wide:].astype(bf16), d_time.astype(bf16))
        outer_bias[here] = jnp.sum(d_time, axis=0)
    rows = jnp.where(index == 3, factors, 0.0)
    d_inner = rows[:, :TFF]
    inner[...] = tn(rows[:, TFF : TFF + TDIM].astype(bf16), d_inner.astype(bf16))
    inner_bias[...] = jnp.sum(d_inner, axis=0)


def finish(*messages):
    last = pl.BlockSpec((48, D), lambda j, *at: (D // 48, 0))
    shapes = [(D,)] * 8 + [(4, 1, D), (TDIM, TFF), (TFF,), (TFF, D), (D,)]
    return run(finish_body, (1,), messages, [last] * 4, [(shape, f32) for shape in shapes], [whole(*shape) for shape in shapes], 0)


def plain_rows(first_class, second_class):
    zero = jnp.concatenate(first_class).reshape(2, 2, 2, 2, SHARE, D)
    one = jnp.concatenate(second_class).reshape(2, 2, 2, 2, SHARE, D)
    classes = jnp.stack([jnp.transpose(zero, (1, 3, 2, 0, 4, 5)), jnp.transpose(one, (0, 3, 2, 1, 4, 5))], axis=4)
    return classes.reshape(FF, D)


def everyones(sums, bias, d_time, inner_sum, middle, features, outer):
    gate = jax.nn.sigmoid(inner_sum)
    d_inner = jnp.dot(d_time, outer.astype(f32).T, precision=highest) * (gate * (1.0 + inner_sum * (1.0 - gate)))
    riders = jnp.concatenate([sums, bias.reshape(4, D), jnp.zeros((4, D), f32)])
    factors = jnp.concatenate([d_time, d_inner, middle, features], axis=1)
    for stage in stage_lists()[0]:
        riders = riders + swapped(riders, stage)
        factors = jnp.concatenate([factors, swapped(factors, stage)])
    cuts = (0, D, D + TFF, D + 2 * TFF, D + 2 * TFF + TDIM)
    d_time, d_inner, middle, features = [factors[:, a:b] for a, b in zip(cuts, cuts[1:])]
    inner, outer = matmul(features.T, d_inner), matmul(middle.T, d_time)
    return list(riders[:8]), riders[8:12], inner, column_sum(d_inner), outer, column_sum(d_time)


def on_device(
    layer_input,
    cotangent,
    timesteps,
    src_len,
    seq_len,
    key_keep,
    query_weight,
    query_bias,
    key_weight,
    value_weight,
    value_bias,
    output_weight,
    output_bias,
    first_gain,
    first_shift,
    expand_weight,
    expand_bias,
    reduce_weight,
    reduce_bias,
    second_gain,
    second_shift,
    time_inner,
    time_inner_bias,
    time_outer,
    time_outer_bias,
):
    stream = lax.axis_index("y")
    sizes = [lax.axis_size(axis) for axis in ("y", "z", "x", "c")]
    devices = math.prod(sizes)
    tuned = sizes == [2, 4, 2, 2]
    c, x, z = lax.axis_index("c") if tuned else 0, lax.axis_index("x"), lax.axis_index("z")
    first, second = jnp.where(c == 0, x, stream), jnp.where(c == 0, stream, x)
    wanted = first if tuned else 0
    places = [one * 8 + two * 4 + (z & 1) * 2 + (z >> 1) for one, two in ((x, stream), (stream, x))]
    bits = jnp.stack([c, x, stream, z & 1, z >> 1, wanted, *places]).astype(jnp.int32)

    def whole_sequence(rows):
        own = lax.dynamic_index_in_dim(rows[:, 0], stream, axis=0, keepdims=False)
        other = lax.dynamic_index_in_dim(rows[:, 0], 1 - stream, axis=0, keepdims=False)
        return own, swapped(other, side)

    def both_sequences(rows, far):
        own = rows[:CAP]
        return jnp.where(stream == 0, jnp.stack([own, far]), jnp.stack([far, own]))[:, None]

    own, far = whole_sequence(layer_input)
    cotangent, far = lax.optimization_barrier((cotangent, far))
    cot_own, cot_far = whole_sequence(cotangent)
    features, inner_sum, middle, stamp, allowed, valid, masked = prepare(
        bits, timesteps, src_len, seq_len, key_keep, time_inner, time_inner_bias, time_outer, time_outer_bias
    )
    weights = (query_weight, query_bias, key_weight, value_weight, value_bias)
    *first_rows, own_low = project(own, 0, stamp, allowed, *weights)
    (far,) = tie([far], first_rows[:1])
    *other_rows, far_low = project(far, 1, stamp, allowed, *weights)
    q, k, v = zip(first_rows, other_rows)
    low = (own_low, far_low)
    attended, lefts, probs = attend(q, k, v, low, masked)
    (lefts,) = tie([lefts], [cot_far])
    output, for_core, activated, slope, mixed_low, normed, inverse, d_second, d_reduced, second_sums = feed_forward(
        bits,
        attended,
        own,
        far,
        stamp,
        output_weight,
        output_bias,
        first_gain,
        first_shift,
        expand_weight,
        expand_bias,
        reduce_weight,
        reduce_bias,
        second_gain,
        second_shift,
        valid,
        cot_own,
        cot_far,
    )
    lefts_got = swapped(lefts, core)
    (output,) = tie([output], [lefts_got])
    output_got = swapped(output[CAP:], side)
    for_core, d_expanded, expand_bias_grad, d_first, d_branch, first_sums = expand_back(
        bits,
        d_reduced,
        reduce_weight,
        slope,
        expand_weight,
        d_second,
        normed,
        inverse,
        first_gain,
        for_core,
        [lefts_got],
    )
    (for_core,) = tie([for_core], [output_got])
    grads, kept, sent, attend_sums = attend_back(bits, d_branch, output_weight, probs, q, k, v, allowed, [for_core])
    block_parts = (inner_sum, middle, features, time_outer)
    if tuned:
        (hidden_got,) = tie([swapped(for_core, core)], [grads])
        (sent,) = tie([sent], [hidden_got])
        small, small_sent = pair_grad(bits, lefts, kept, lefts_got, swapped(sent, core), [])
        small_got = crossed(small_sent, True)
        hidden, hidden_sent = hidden_grad(bits, activated, d_reduced, d_expanded, mixed_low, hidden_got, [small])
        (small_got,) = tie([small_got], [hidden])
        small, small_sent = halved(small, small_got, second)
        small_got = crossed(small_sent, False)
        d_rows, d_time = input_grad(grads, query_weight, key_weight, value_weight, d_first, [small_sent])
        (small_got,) = tie([small_got], [d_rows])
        small, small_sent = halved(small, small_got, z & 1)
        small_got = swapped(small_sent, low_far)
        hidden_sent, d_rows, d_time = tie([hidden_sent, d_rows, d_time], [small_sent])
        hidden_got = crossed(hidden_sent, True)
        input_got = swapped(d_rows[CAP:], side)
        block = block_rows(bits, attend_sums, first_sums, second_sums, expand_bias_grad, d_time, *block_parts)
        small, small_sent = halved(small, small_got, z >> 1)
        share = plus(small, swapped(small_sent, high_far)).reshape(SHARE, D)
        data, block = longer(share, block, lambda value: swapped(value, high_far), False)
        data, block = longer(data, block, lambda value: swapped(value, low_far), False)
        hidden, hidden_sent = halved(hidden, hidden_got, second)
        hidden_got = crossed(hidden_sent, False)
        (data,) = tie([data], [hidden_sent])
        data, block = longer(data, block, lambda value: crossed(value, False), True)
        hidden, hidden_sent = halved(hidden, hidden_got, z & 1)
        hidden_got = swapped(hidden_sent, low_far)
        (data,) = tie([data], [hidden_sent])
        message = jnp.concatenate([data, block])
        turned = crossed(message, True)
        message_far = swapped(message, core)
        outs = unpack(bits, message, message_far, 0, ())
        hidden, hidden_sent = halved(hidden, hidden_got, z >> 1)
        hidden_got = swapped(hidden_sent, high_far)
        turned_far = swapped(turned, core)
        outs = unpack(bits, turned, turned_far, 1, outs)
        *vectors, expand_bias_grad, inner, inner_bias, outer, outer_bias = finish(message, turned, message_far, turned_far)
        grad_query, grad_key, grad_value, grad_output = [out.reshape(D, D) for out in outs]
        shares = (hidden.astype(f32) + hidden_got.astype(f32))[0]
        reduce_share, expand_share = shares[0], shares[1]
        input_grad_rows = both_sequences(d_rows, input_got)
    else:
        d_rows, d_time = input_grad(grads, query_weight, key_weight, value_weight, d_first, ())
        reduce_parts, expand_parts, pairs = [], [], []
        nothing_got = jnp.zeros_like(for_core)
        for core_bit, pair, left, right in (
            (0, kept, activated, d_expanded),
            (1, sent, for_core[:, : 2 * D], for_core[:, 4 * D :]),
        ):
            as_core = bits.at[0].set(core_bit)
            hidden = hidden_grad(as_core, left, d_reduced, right, mixed_low, nothing_got, ())
            reduce_parts.append([part[:, 0] for part in hidden])
            expand_parts.append([part[:, 1] for part in hidden])
            grad = pair_grad(as_core, lefts, pair, lefts, jnp.zeros_like(pair), ())
            pairs.append(jnp.moveaxis(jnp.concatenate(grad), 1, 0).reshape(2, D, D))
        per = FF // devices
        reduce_share, _ = scattered_sum(plain_rows(*reduce_parts).reshape(devices, per, D))
        expand_share, _ = scattered_sum(plain_rows(*expand_parts).reshape(devices, per, D))
        small_share, _ = scattered_sum(jnp.concatenate(pairs).reshape(devices, per, D))
        me = ((stream * sizes[1] + z) * 2 + x) * 2 + lax.axis_index("c")
        small = gathered(small_share)[jnp.arange(devices) ^ me].astype(f32).reshape(4, D, D)
        grad_query, grad_key, grad_value, grad_output = [small[at] for at in range(4)]
        vectors, expand_bias_grad, inner, inner_bias, outer, outer_bias = everyones(
            attend_sums + first_sums + second_sums, expand_bias_grad, d_time, *block_parts
        )
        input_grad_rows = both_sequences(d_rows, swapped(d_rows[CAP:], side))
    return (
        both_sequences(output, output_got),
        input_grad_rows,
        grad_query,
        vectors[0],
        grad_key,
        grad_value,
        vectors[1],
        grad_output,
        vectors[2],
        vectors[3],
        vectors[4],
        expand_share.astype(f32).T,
        expand_bias_grad.reshape(FF),
        reduce_share.astype(f32),
        vectors[5],
        vectors[6],
        vectors[7],
        inner,
        inner_bias,
        outer,
        outer_bias,
    )


def solution(mesh):
    seq, batch = mesh.devices.shape
    mesh = jax.sharding.Mesh(mesh.devices.reshape(seq, batch // 4, 2, 2), ("y", "z", "x", "c"))
    sequences, everyone = ("z", "x", "c"), ("y", "z", "x", "c")
    rows = P(sequences, "y", None, None)
    in_specs = (rows, rows) + (P(sequences),) * 3 + (P(sequences, None, None),) + (P(),) * 19
    out_specs = (rows, rows) + (P(),) * 9 + (P(None, everyone), P(), P(everyone, None)) + (P(),) * 7
    return jax.shard_map(on_device, mesh=mesh, in_specs=in_specs, out_specs=out_specs, check_vma=False)
```

```python
import functools
import math

import jax
import jax.numpy as jnp
from jax import lax
from jax.experimental import pallas as pl
from jax.experimental.pallas import tpu as pltpu
from jax.sharding import PartitionSpec as P

D = 768
HEADS = 12
HEAD_DIM = 64
FF = 3072
TDIM = 128
TFF = 512
CAP = 256
ROWS = 2 * CAP

f32 = jnp.float32
bf16 = jnp.bfloat16
highest = lax.Precision.HIGHEST
norm_epsilon = 1e-12
masked_score = -1000000000.0
root_half = 0.7071067811865476
density_scale = 0.3989422804014327


core, near, side = ("c", 0), ("x", 0), ("y", 0)


def swapped(value, stage):
    axis, bit = stage
    return lax.ppermute(value, axis, [(i, i ^ (1 << bit)) for i in range(lax.axis_size(axis))])


def own_bit(stage):
    axis, bit = stage
    return (lax.axis_index(axis) >> bit) & 1


def stage_lists():
    bits = lax.axis_size("z").bit_length() - 1
    far = [("z", k) for k in range(bits)]
    return [side] + far[::-1] + [near, core], far


def added(kept, received):
    return lax.reduce_precision(kept.astype(f32) + received.astype(f32), 8, 7).astype(bf16)


def halves(buffer, labels, stage):
    at = labels.index(stage)
    bit = own_bit(stage)
    kept = lax.dynamic_index_in_dim(buffer, bit, axis=at, keepdims=False)
    sent = lax.dynamic_index_in_dim(buffer, 1 - bit, axis=at, keepdims=False)
    return kept, sent, labels[:at] + labels[at + 1 :]


def exchange(buffer, labels, stage, riders=None):
    kept, sent, labels = halves(buffer, labels, stage)
    rows = sent.reshape(-1, D)
    if riders is None:
        return added(kept, swapped(rows, stage).reshape(kept.shape)), labels, None
    received = swapped(jnp.concatenate([rows, riders], axis=0), stage)
    return (
        added(kept, received[: rows.shape[0]].reshape(kept.shape)),
        labels,
        added(riders, received[rows.shape[0] :]),
    )


def scattered_sum(shares, riders=None):
    slow_first, far = stage_lists()
    rows = shares.shape[1]
    buffer = shares.reshape((2,) * len(slow_first) + (rows, D))
    buffer, labels, riders = exchange(buffer, slow_first, core, riders)
    cut = rows // 2
    first, first_labels, riders = exchange(buffer[..., :cut, :], labels, near, riders)
    second, second_labels, _ = exchange(buffer[..., cut:, :], labels, side)
    first, first_labels, riders = exchange(first, first_labels, side, riders)
    second, second_labels, _ = exchange(second, second_labels, near)
    buffer = jnp.concatenate([first, second], axis=-2)
    labels = first_labels
    for stage in far:
        buffer, labels, riders = exchange(buffer, labels, stage, riders)
    return buffer, riders


def gathered(share):
    slow_first, far = stage_lists()
    order = [core, near, side] + far
    buffer = share[None]
    done = []
    for stage in reversed(order):
        buffer = jnp.concatenate([buffer, swapped(buffer, stage)], axis=0)
        done.append(stage)
    bits = len(order)
    buffer = buffer.reshape((2,) * bits + share.shape)
    current = list(reversed(done))
    return jnp.transpose(buffer, [current.index(stage) for stage in slow_first] + [bits, bits + 1]).reshape(
        (1 << bits,) + share.shape
    )


def matmul(left, right):
    return jnp.dot(left, right, preferred_element_type=f32)


def column_sum(values):
    return jnp.sum(values.astype(f32), axis=0)


def dot(left, right, dims):
    return lax.dot_general(left, right, (((dims[0],), (dims[1],)), ((), ())), preferred_element_type=f32)


def nn(left, right):
    return dot(left, right, (1, 0))


def nt(left, right):
    return dot(left, right, (1, 1))


def tn(left, right):
    return dot(left, right, (0, 0))


def whole(*shape):
    return pl.BlockSpec(shape, lambda *at: (0,) * len(shape))


def vector(size):
    return pl.BlockSpec((size,), lambda *at: (0,))


def vector_tile(width):
    return pl.BlockSpec((width,), lambda j, *at: (j,))


def row(ref):
    return ref[...].reshape(1, -1)


def column_tile(rows, width):
    return pl.BlockSpec((rows, width), lambda j, *at: (0, j))


def row_tile(height, width):
    return pl.BlockSpec((height, width), lambda j, *at: (j, 0))


def run(body, grid, operands, in_specs, outs, out_specs, flops, scratch=(), scalars=(), after=(), aliases=None):
    shapes = [jax.ShapeDtypeStruct(shape, dtype) for shape, dtype in outs]
    sizes = [x.size * x.dtype.itemsize for x in list(operands) + shapes]
    used = len(scalars) + len(operands)

    def wrapped(*refs):
        body(*refs[:used], *refs[used + len(after) :])

    return pl.pallas_call(
        wrapped,
        grid_spec=pltpu.PrefetchScalarGridSpec(
            num_scalar_prefetch=len(scalars),
            grid=grid,
            in_specs=in_specs + [pl.BlockSpec(memory_space=pl.ANY)] * len(after),
            out_specs=out_specs,
            scratch_shapes=scratch,
        ),
        out_shape=shapes,
        input_output_aliases=aliases or {},
        compiler_params=pltpu.CompilerParams(vmem_limit_bytes=63 << 20),
        cost_estimate=pl.CostEstimate(flops=int(flops), bytes_accessed=sum(sizes), transcendentals=0),
    )(*scalars, *operands, *after)


def nothing(*refs):
    pass


def tie(values, after):
    anywhere = pl.BlockSpec(memory_space=pl.ANY)
    return pl.pallas_call(
        nothing,
        in_specs=[anywhere] * (len(values) + len(after)),
        out_specs=[anywhere] * len(values),
        out_shape=[jax.ShapeDtypeStruct(value.shape, value.dtype) for value in values],
        input_output_aliases={k: k for k in range(len(values))},
    )(*values, *after)


def normalized(values):
    center = values - jnp.mean(values, axis=-1, keepdims=True)
    spread = jnp.mean(center * center, axis=-1, keepdims=True)
    inverse = lax.rsqrt(spread + norm_epsilon)
    return center * inverse, inverse


def norm_backward(upstream, normed, inverse):
    first_mean = jnp.mean(upstream, axis=-1, keepdims=True)
    second_mean = jnp.mean(upstream * normed, axis=-1, keepdims=True)
    return inverse * (upstream - first_mean - normed * second_mean)


def row_sum(values):
    return jnp.sum(values, axis=0, keepdims=True)


def prepare_body(bits, stamps, src_len, seq_len, flags, inner, inner_bias, outer, outer_bias, *outs):
    features, inner_sum, middle, stamp, allowed, valid, masked = outs
    y = bits[2]
    lane = lax.broadcasted_iota(jnp.int32, (1, TDIM), 1)
    half = TDIM // 2
    frequency = jnp.exp(-math.log(10000.0) * lax.rem(lane, half).astype(f32) / half)
    angles = jnp.broadcast_to(stamps[y].astype(f32), (1, TDIM)) * frequency
    waves = jnp.where(lane < half, jnp.cos(angles), jnp.sin(angles))
    features[...] = waves
    total = jnp.dot(waves, inner[...].astype(f32), precision=highest) + row(inner_bias)
    inner_sum[...] = total
    gated = total * (1.0 / (1.0 + jnp.exp(-total)))
    middle[...] = gated
    stamp[...] = jnp.dot(gated, outer[...].astype(f32), precision=highest) + row(outer_bias)
    source, target = src_len[y], seq_len[y] - src_len[y]
    slots = lax.broadcasted_iota(jnp.int32, (CAP, 1), 0)
    lengths = jnp.where(y == 0, source, target), jnp.where(y == 0, target, source)
    for at, (length, stream) in enumerate(zip(lengths, (y, 1 - y))):
        inside = jnp.where(slots < length, 1.0, 0.0)
        kept = jnp.where(flags[y, pl.ds(stream, 1)] == 1, 1.0, 0.0)
        kept = jnp.broadcast_to(kept, (8, CAP)).T[:, :1]
        here = slice(at * CAP, (at + 1) * CAP)
        valid[here] = inside
        allowed[here] = inside * kept
        masked[here] = (1.0 - inside * kept) * masked_score


def prepare(bits, stamps, src_len, seq_len, flags, inner, inner_bias, outer, outer_bias):
    return run(
        prepare_body,
        (1,),
        (flags, inner, inner_bias, outer, outer_bias),
        [whole(2, 2, CAP), whole(TDIM, TFF), vector(TFF), whole(TFF, D), vector(D)],
        [((1, size), f32) for size in (TDIM, TFF, TFF, D)] + [((ROWS, 1), f32)] * 3,
        [whole(1, size) for size in (TDIM, TFF, TFF, D)] + [whole(ROWS, 1)] * 3,
        0,
        scalars=(bits, stamps, src_len, seq_len),
    )


def project_body(rows, stamp, keep, qw, qb, kw, vw, vb, q, k, v, low_out):
    low = (rows[...].astype(f32) + stamp[...]).astype(bf16)
    low_out[...] = low
    q[...] = ((nn(low, qw[...]) + row(qb)).astype(bf16).astype(f32) * 0.125).astype(bf16)
    k[...] = (nn(low, kw[...]) * keep[...]).astype(bf16)
    v[...] = (nn(low, vw[...]) + row(vb)).astype(bf16)


def project(rows, half, stamp, keep, qw, qb, kw, vw, vb):
    tile = 256
    return run(
        project_body,
        (D // tile,),
        (rows, stamp, keep, qw, qb, kw, vw, vb),
        [whole(CAP, D), whole(1, D), pl.BlockSpec((CAP, 1), lambda *at: (half, 0))]
        + [column_tile(D, tile), vector_tile(tile), column_tile(D, tile), column_tile(D, tile), vector_tile(tile)],
        [((CAP, D), bf16)] * 4,
        [column_tile(CAP, tile)] * 3 + [whole(CAP, D)],
        6 * CAP * D * D,
    )


def lanes_of(shape):
    return lax.broadcasted_iota(jnp.int32, shape, 1)


def both(own, far):
    return jnp.concatenate([own[...], far[...]], axis=0)


def attend_body(qo, qf, ko, kf, vo, vf, lo, lf, masked, attended, for_core, probs):
    q, k, v = both(qo, qf), both(ko, kf), both(vo, vf)
    lane = lanes_of(q.shape)
    flag = jnp.broadcast_to(masked[...], q.shape).astype(bf16)
    v_turned = v.T
    pieces = []
    for head in range(2):
        mine = (lane // HEAD_DIM) == head
        spare = lane == (1 - head) * HEAD_DIM
        k_head = jnp.where(mine, k, jnp.where(spare, flag, 0))
        q_head = jnp.where(mine, q, jnp.where(spare, 1, 0).astype(bf16))
        scores = nt(k_head, q_head)
        top = jnp.max(scores, axis=0, keepdims=True)
        exponent = jnp.exp(scores - top)
        inverse = 1.0 / jnp.sum(exponent, axis=0, keepdims=True)
        low = (exponent * inverse).astype(bf16)
        probs[head] = low
        pieces.append(nn(v_turned[head * HEAD_DIM : (head + 1) * HEAD_DIM], low))
    low = jnp.concatenate(pieces, axis=0).T.astype(bf16)
    attended[...] = low
    for_core[0], for_core[1] = both(lo, lf), low


def attend(q, k, v, low, masked):
    pair = 2 * HEAD_DIM
    return run(
        attend_body,
        (D // pair,),
        (*q, *k, *v, *low, masked),
        [column_tile(CAP, pair)] * 8 + [whole(ROWS, 1)],
        [((ROWS, D), bf16), ((2, ROWS, D), bf16), ((HEADS, ROWS, ROWS), bf16)],
        [column_tile(ROWS, pair), pl.BlockSpec((2, ROWS, pair), lambda j: (0, 0, j))]
        + [pl.BlockSpec((2, ROWS, ROWS), lambda j: (j, 0, 0))],
        4 * HEADS * ROWS * ROWS * 256,
    )


SHARE = 96
COLOUR = 48


half_tile = pl.BlockSpec((ROWS, D // 2), lambda j, *at: (0, j))


FOR_CORE = (ROWS, FF + 2 * D)


def by_core(values):
    return [
        jnp.concatenate([values[:, at : at + SHARE] for at in range(start, D, 2 * SHARE)], axis=1) for start in (0, SHARE)
    ]


SUB = 256


def feed_forward_body(
    bits, attended, own, far, stamp, ow, ob, gain, shift, ew, eb, rw, rb, gain2, shift2, valid, cot_own, cot_far,
    output, for_core, activated_own, expanded_own, mixed_low, d_reduced, bias_grad, d_first, d_branch, sums,
    total, normed, inverse, slope, columns,
):
    step = pl.program_id(0)
    tiles = FF // D

    def store(own_out, offset):
        zero, one = by_core(columns[...])
        here = pl.ds(pl.multiple_of(offset, D // 2), D // 2)

        @pl.when(bits[0] == 0)
        def _():
            own_out[...], for_core[:, here] = zero, one

        @pl.when(bits[0] == 1)
        def _():
            own_out[...], for_core[:, here] = one, zero

    @pl.when(step == 0)
    def _():
        hidden = both(own, far).astype(f32) + stamp[...]
        n1, inv = normalized(hidden + nn(attended[...], ow[...]) + row(ob))
        value = n1 * row(gain) + row(shift)
        normed[...] = n1
        inverse[...] = inv
        mixed_low[...] = value.astype(bf16)
        total[...] = value + row(rb)

    @pl.when(step < tiles)
    def _():
        added_up = None
        bias = eb[pl.ds(pl.multiple_of(step * D, D), D)].reshape(1, -1)
        for part in range(D // SUB):
            cut = slice(part * SUB, (part + 1) * SUB)
            expanded = nn(mixed_low[...], ew[:, cut]) + bias[:, cut]
            chance = 0.5 * (1.0 + lax.erf(expanded * root_half))
            slope[step, :, cut] = chance + expanded * jnp.exp(-0.5 * expanded * expanded) * density_scale
            low = (expanded * chance).astype(bf16)
            columns[:, cut] = low
            product = nn(low, rw[cut, :])
            added_up = product if added_up is None else added_up + product
        total[...] += added_up
        store(activated_own, step * (D // 2))

    @pl.when(step == tiles - 1)
    def _():
        n2, inv = normalized(total[...])
        weight = valid[...]
        output[...] = ((n2 * row(gain2) + row(shift2)) * weight).astype(bf16)
        d_out = both(cot_own, cot_far).astype(f32) * weight
        back = norm_backward(d_out * row(gain2), n2, inv)
        low = back.astype(bf16)
        total[...] = back
        d_reduced[...] = low
        for_core[:, 2 * D : 3 * D] = low
        for_core[:, 3 * D : 4 * D] = mixed_low[...]
        sums[...] = jnp.concatenate(
            [jnp.zeros((5, D), f32), row_sum(low.astype(f32)), row_sum(d_out * n2), row_sum(d_out)], axis=0
        )

    @pl.when(step >= tiles)
    def _():
        d_expanded = (nt(d_reduced[...], rw[...]) * slope[step - tiles]).astype(bf16)
        columns[...] = d_expanded
        bias_grad[0] = row_sum(d_expanded.astype(f32))
        total[...] += nt(d_expanded, ew[...])
        store(expanded_own, 4 * D + (step - tiles) * (D // 2))

    @pl.when(step == 2 * tiles - 1)
    def _():
        d_mixed = total[...]
        n1 = normed[...]
        back = norm_backward(d_mixed * row(gain), n1, inverse[...])
        low = back.astype(bf16)
        d_first[...] = back
        d_branch[...] = low
        sums[2:5] = jnp.concatenate([row_sum(low.astype(f32)), row_sum(d_mixed * n1), row_sum(d_mixed)], axis=0)


def feed_forward(
    bits, attended, own, far, stamp, ow, ob, gain, shift, ew, eb, rw, rb, gain2, shift2, valid, cot_own, cot_far
):
    tiles = FF // D
    line, square, half = vector(D), whole(ROWS, D), whole(CAP, D)
    forward = pl.BlockSpec((ROWS, D // 2), lambda j, *at: (0, jnp.minimum(j, tiles - 1)))
    backward = pl.BlockSpec((ROWS, D // 2), lambda j, *at: (0, jnp.maximum(j - tiles, 0)))
    return run(
        feed_forward_body,
        (2 * tiles,),
        (attended, own, far, stamp, ow, ob, gain, shift, ew, eb, rw, rb, gain2, shift2, valid, cot_own, cot_far),
        [square, half, half, whole(1, D), whole(D, D), line, line, line]
        + [pl.BlockSpec((D, D), lambda j, *at: (0, j % tiles)), vector(FF), pl.BlockSpec((D, D), lambda j, *at: (j % tiles, 0))]
        + [line, line, line, whole(ROWS, 1), half, half],
        [((ROWS, D), bf16), (FOR_CORE, bf16), ((ROWS, FF // 2), bf16), ((ROWS, FF // 2), bf16), ((ROWS, D), bf16)]
        + [((ROWS, D), bf16), ((tiles, 1, D), f32), ((ROWS, D), f32), ((ROWS, D), bf16), ((8, D), f32)],
        [square, whole(*FOR_CORE), forward, backward, square, square]
        + [pl.BlockSpec((1, 1, D), lambda j, *at: (jnp.maximum(j - tiles, 0), 0, 0)), square, square, whole(8, D)],
        2 * ROWS * D * (D + 4 * FF),
        scratch=[pltpu.VMEM((ROWS, D), f32)] * 2
        + [pltpu.VMEM((ROWS, 1), f32), pltpu.VMEM((tiles, ROWS, D), f32), pltpu.VMEM((ROWS, D), bf16)],
        scalars=(bits,),
    )


def hidden_grad_body(bits, activated, d_reduced, d_expanded, mixed, activated_got, reduced_got, mixed_got, expanded_got, kept, sent):
    step = pl.program_id(0)
    tile = step % 2

    def store(kind, grad):
        low = grad.astype(bf16)
        for at in range(8):
            x, z = at % 2, at // 2
            here = jnp.where(bits[0] == 0, tile * 4 + (z % 2 * 2 + z // 2), x * 4 + z)
            block = low[at * SHARE : (at + 1) * SHARE]
            mine = jnp.where(bits[0] == 0, x, tile) == bits[5]

            @pl.when(mine)
            def _():
                kept[here, kind] = block

            @pl.when(jnp.logical_not(mine))
            def _():
                sent[here, kind] = block

    @pl.when(step < 2)
    def _():
        store(0, tn(activated[...], d_reduced[...]) + tn(activated_got[...], reduced_got[...]))

    @pl.when(step >= 2)
    def _():
        store(1, tn(d_expanded[...], mixed[...]) + tn(expanded_got[...], mixed_got[...]))


def hidden_grad(bits, activated, d_reduced, d_expanded, mixed, got, after):
    first = lambda start: pl.BlockSpec((ROWS, D), lambda j, bits: (0, start + jnp.minimum(j, 1)))
    second = lambda start: pl.BlockSpec((ROWS, D), lambda j, bits: (0, start + jnp.maximum(j - 2, 0)))
    square = lambda at: pl.BlockSpec((ROWS, D), lambda j, bits: (0, at))
    return run(
        hidden_grad_body,
        (4,),
        (activated, d_reduced, d_expanded, mixed, got, got, got, got),
        [first(0), square(0), second(0), square(0), first(0), square(2), square(3), second(4)],
        [((8, 2, SHARE, D), bf16)] * 2,
        [whole(8, 2, SHARE, D)] * 2,
        4 * ROWS * D * FF,
        scalars=(bits,),
        after=after,
    )


def attend_back_body(bits, d_branch, branch, ow, probs, qo, qf, ko, kf, vo, vf, keep, grads, kept, sent, sums):
    q, k, v = both(qo, qf), both(ko, kf), both(vo, vf)
    lane = lanes_of(q.shape)
    low_half = lane < HEAD_DIM
    upstream = nt(d_branch[...], ow[...]).astype(bf16)
    k_turned = k.T
    d_q, d_k, d_v = [], [], []
    for head in range(2):
        rows = slice(head * HEAD_DIM, (head + 1) * HEAD_DIM)
        mine = low_half if head == 0 else jnp.logical_not(low_half)
        low = probs[head]
        wide = low.astype(f32)
        weighted = wide * nt(jnp.where(mine, v, 0), upstream)
        d_scores = (weighted - wide * row_sum(weighted)).astype(bf16)
        d_v.append(nn(low, upstream))
        d_k.append(nn(d_scores, q))
        d_q.append(nn(k_turned[rows], d_scores))
    q_low = (jnp.concatenate(d_q, axis=0).T * 0.125).astype(bf16)
    v_low = jnp.where(low_half, d_v[0], d_v[1]).astype(bf16)
    k_low = (jnp.where(low_half, d_k[0], d_k[1]) * keep[...]).astype(bf16)
    grads[0], grads[1], grads[2] = q_low, k_low, v_low

    def share(first, second):
        first[0], first[1] = q_low, k_low
        second[0], second[1] = v_low, branch[...]

    @pl.when(bits[0] == 0)
    def _():
        share(kept, sent)

    @pl.when(bits[0] == 1)
    def _():
        share(sent, kept)

    sums[...] = jnp.concatenate(
        [row_sum(q_low.astype(f32)), row_sum(v_low.astype(f32)), jnp.zeros((6, q.shape[1]), f32)], axis=0
    )


def attend_back(bits, d_branch, ow, probs, q, k, v, keep, after):
    pair = 2 * HEAD_DIM
    return run(
        attend_back_body,
        (D // pair,),
        (d_branch, d_branch, ow, probs, *q, *k, *v, keep),
        [whole(ROWS, D), column_tile(ROWS, pair), row_tile(pair, D), pl.BlockSpec((2, ROWS, ROWS), lambda j, *at: (j, 0, 0))]
        + [column_tile(CAP, pair)] * 6
        + [whole(ROWS, 1)],
        [((count, ROWS, D), bf16) for count in (3, 2, 2)] + [((8, D), f32)],
        [pl.BlockSpec((count, ROWS, pair), lambda j, *at: (0, 0, j)) for count in (3, 2, 2)] + [column_tile(8, pair)],
        10 * HEADS * ROWS * ROWS * 256,
        scalars=(bits,),
        after=after,
    )


def pair_grad_body(bits, left, right, left_got, right_got, kept, sent):
    low = (tn(left[0], right[0]) + tn(left_got[0], right_got[0])).astype(bf16)
    zero, one = [low[at * D // 2 : (at + 1) * D // 2].reshape(8, COLOUR, D) for at in range(2)]
    kept[:, 0] = jnp.where(bits[5] == 0, zero, one)
    sent[:, 0] = jnp.where(bits[5] == 0, one, zero)


def pair_grad(bits, left, right, left_got, right_got, after):
    lefts = pl.BlockSpec((1, ROWS, D), lambda j, bits: (j * bits[0], 0, 0))
    rights = pl.BlockSpec((1, ROWS, D), lambda j, bits: (j, 0, 0))
    return run(
        pair_grad_body,
        (2,),
        (left, right, left_got, right_got),
        [lefts, rights] * 2,
        [((8, 2, COLOUR, D), bf16)] * 2,
        [pl.BlockSpec((8, 1, COLOUR, D), lambda j, *at: (0, j, 0, 0))] * 2,
        8 * ROWS * D * D,
        scalars=(bits,),
        after=after,
    )


def input_grad_body(grads, qw, kw, vw, d_first, d_rows, d_time):
    total = d_first[...] + nt(grads[0], qw[...]) + nt(grads[1], kw[...]) + nt(grads[2], vw[...])
    d_rows[...] = total.astype(bf16)
    d_time[...] = row_sum(total)


def input_grad(grads, qw, kw, vw, d_first, after):
    tile = 256
    return run(
        input_grad_body,
        (D // tile,),
        (grads, qw, kw, vw, d_first),
        [whole(3, ROWS, D)] + [row_tile(tile, D)] * 3 + [column_tile(ROWS, tile)],
        [((ROWS, D), bf16), ((1, D), f32)],
        [column_tile(ROWS, tile), column_tile(1, tile)],
        6 * ROWS * D * D,
        after=after,
    )


everywhere = ("y", "z", "x", "c")


def crossed(value, first):
    sizes = [lax.axis_size(axis) for axis in everywhere]
    pairs = []
    for at in range(math.prod(sizes)):
        c, x = at % 2, at // 2 % 2
        along_x = (c == 0) == first
        step = 2 * (1 - 2 * x) if along_x else (math.prod(sizes) // 2) * (1 - 2 * (at // (math.prod(sizes) // 2)))
        pairs.append((at, at + step))
    return lax.ppermute(value, everywhere, pairs)


def lined(value, first):
    sizes = [lax.axis_size(axis) for axis in everywhere]
    turn = lambda c: 1 if (c == 0) == first else 2
    pairs = [(at, at ^ (turn(at % 2) * 4)) for at in range(math.prod(sizes))]
    return lax.ppermute(value, everywhere, pairs)


def plus(left, right):
    return (left.astype(f32) + right.astype(f32)).astype(bf16)


def halved(own, got, bit):
    own, got = [value.reshape((2, -1) + value.shape[1:]) for value in (own, got)]
    at = lambda place: [lax.dynamic_index_in_dim(value, place, 0, keepdims=False) for value in (own, got)]
    return plus(*at(bit)), plus(*at(1 - bit))


BLOCK = 32


def block_body(bits, first, second, bias, d_time, inner_sum, middle, features, outer, out):
    riders = first[...] + second[...]
    total = inner_sum[...]
    gate = 1.0 / (1.0 + jnp.exp(-total))
    d_middle = lax.dot_general(
        d_time[...], outer[...].astype(f32), (((1,), (1,)), ((), ())), precision=highest, preferred_element_type=f32
    )
    d_inner = d_middle * (gate * (1.0 + total * (1.0 - gate)))
    wide = D - TFF
    rows = [jnp.concatenate([d_time[:, at * wide : (at + 1) * wide], middle[...]], axis=1) for at in range(3)]
    rows.append(jnp.concatenate([d_inner, features[...], jnp.zeros((1, wide - TDIM), f32)], axis=1))
    index = lax.broadcasted_iota(jnp.int32, (16, D), 0)
    factors = jnp.zeros((16, D), f32)
    for at, values in enumerate(rows):
        factors = jnp.where(index == 4 * (bits[3] + 2 * bits[4]) + at, values, factors)
    biases = jnp.zeros((8, D), f32)
    index = lax.broadcasted_iota(jnp.int32, (8, D), 0)
    for at in range(4):
        biases = jnp.where(index == at, bias[at], biases)
    out[...] = jnp.concatenate([riders, biases, factors], axis=0).astype(bf16)


def block_rows(bits, *operands):
    return run(
        block_body,
        (1,),
        operands,
        [whole(*operand.shape) for operand in operands],
        [((BLOCK, D), bf16)],
        [whole(BLOCK, D)],
        0,
        scalars=(bits,),
    )[0]


def sum_rows(own, got):
    return lax.reduce_precision(own.astype(f32) + got.astype(f32), 8, 7).astype(bf16)


def longer(data, block, send, join):
    got = send(jnp.concatenate([data, block]))
    size = data.shape[0]
    data, got = jnp.concatenate([data, got[:size]]), got[size:]
    if not join:
        return data, sum_rows(block, got)
    return data, jnp.concatenate([sum_rows(block[:16], got[:16]), block[16:], got[16:]])


def unpack_body(bits, own, got, outs):
    for at in range(4):
        here, there = (bits[6] % 4) ^ at, (bits[7] % 4) ^ at
        for matrix in range(2):
            rows = slice(at * SHARE + matrix * COLOUR, at * SHARE + (matrix + 1) * COLOUR)
            mine, other = own[rows].astype(f32), got[rows].astype(f32)
            outs[matrix][here] = jnp.where(bits[0] == 0, mine, other)
            outs[2 + matrix][there] = jnp.where(bits[0] == 0, other, mine)


def unpack_specs(turn):
    part = pl.BlockSpec((4 * SHARE, D), lambda j, bits: (j, 0))
    spots = [
        pl.BlockSpec((4, COLOUR, D), lambda j, bits, at=at: ((bits[at] // 4) ^ (2 * turn + j), 0, 0)) for at in (6, 6, 7, 7)
    ]
    return part, spots


matrix_shapes = [((16, COLOUR, D), f32)] * 4


def first_unpack(bits, own, got):
    part, spots = unpack_specs(0)
    body = lambda bits, own, got, *outs: unpack_body(bits, own, got, outs)
    return run(body, (2,), (own, got), [part] * 2, matrix_shapes, spots, 0, scalars=(bits,))


def finish_body(bits, turned, turned_far, own, far, turned_last, turned_far_last, *refs):
    outs = refs[-17:]
    unpack_body(bits, turned, turned_far, outs[:4])

    @pl.when(pl.program_id(0) == 0)
    def _():
        vectors_body(own, turned_last, far, turned_far_last, *outs[4:])


def vectors_body(own, turned, own_far, turned_far, *outs):
    blocks = [ref[...].astype(f32) for ref in (own, turned, own_far, turned_far)]
    sums = (blocks[0][:16] + blocks[1][:16]) + (blocks[2][:16] + blocks[3][:16])
    for at in range(8):
        outs[at][...] = sums[at]
    for at in range(4):
        outs[8][at] = sums[8 + at : 9 + at]
    factors = jnp.concatenate([block[16:] for block in blocks], axis=0)
    index = lax.broadcasted_iota(jnp.int32, factors.shape, 0) % 4
    wide = D - TFF
    inner, inner_bias, outer, outer_bias = outs[9:]
    for at in range(3):
        rows = jnp.where(index == at, factors, 0.0)
        d_time = rows[:, :wide]
        here = slice(at * wide, (at + 1) * wide)
        outer[:, here] = tn(rows[:, wide:].astype(bf16), d_time.astype(bf16))
        outer_bias[here] = jnp.sum(d_time, axis=0)
    rows = jnp.where(index == 3, factors, 0.0)
    d_inner = rows[:, :TFF]
    inner[...] = tn(rows[:, TFF : TFF + TDIM].astype(bf16), d_inner.astype(bf16))
    inner_bias[...] = jnp.sum(d_inner, axis=0)


def finish(bits, turned, turned_far, message, message_far, outs):
    part, spots = unpack_specs(1)
    last = pl.BlockSpec((48, D), lambda j, *at: (D // 48, 0))
    shapes = [(D,)] * 8 + [(4, 1, D), (TDIM, TFF), (TFF,), (TFF, D), (D,)]
    return run(
        finish_body,
        (2,),
        (turned, turned_far, message, message_far, turned, turned_far, *outs),
        [part] * 2 + [last] * 4 + [pl.BlockSpec(memory_space=pl.ANY)] * 4,
        matrix_shapes + [(shape, f32) for shape in shapes],
        spots + [whole(*shape) for shape in shapes],
        0,
        scalars=(bits,),
        aliases={7 + k: k for k in range(4)},
    )


def plain_rows(first_class, second_class):
    zero = jnp.concatenate(first_class).reshape(2, 2, 2, 2, SHARE, D)
    one = jnp.concatenate(second_class).reshape(2, 2, 2, 2, SHARE, D)
    classes = jnp.stack([jnp.transpose(zero, (1, 3, 2, 0, 4, 5)), jnp.transpose(one, (0, 2, 3, 1, 4, 5))], axis=4)
    return classes.reshape(FF, D)


def everyones(sums, bias, d_time, inner_sum, middle, features, outer):
    gate = jax.nn.sigmoid(inner_sum)
    d_inner = jnp.dot(d_time, outer.astype(f32).T, precision=highest) * (gate * (1.0 + inner_sum * (1.0 - gate)))
    riders = jnp.concatenate([sums, bias.reshape(4, D), jnp.zeros((4, D), f32)])
    factors = jnp.concatenate([d_time, d_inner, middle, features], axis=1)
    for stage in stage_lists()[0]:
        riders = riders + swapped(riders, stage)
        factors = jnp.concatenate([factors, swapped(factors, stage)])
    cuts = (0, D, D + TFF, D + 2 * TFF, D + 2 * TFF + TDIM)
    d_time, d_inner, middle, features = [factors[:, a:b] for a, b in zip(cuts, cuts[1:])]
    inner, outer = matmul(features.T, d_inner), matmul(middle.T, d_time)
    return list(riders[:8]), riders[8:12], inner, column_sum(d_inner), outer, column_sum(d_time)


def on_device(
    layer_input,
    cotangent,
    timesteps,
    src_len,
    seq_len,
    key_keep,
    query_weight,
    query_bias,
    key_weight,
    value_weight,
    value_bias,
    output_weight,
    output_bias,
    first_gain,
    first_shift,
    expand_weight,
    expand_bias,
    reduce_weight,
    reduce_bias,
    second_gain,
    second_shift,
    time_inner,
    time_inner_bias,
    time_outer,
    time_outer_bias,
):
    stream = lax.axis_index("y")
    sizes = [lax.axis_size(axis) for axis in ("y", "z", "x", "c")]
    devices = math.prod(sizes)
    tuned = sizes == [2, 4, 2, 2]
    c, x, z = lax.axis_index("c") if tuned else 0, lax.axis_index("x"), lax.axis_index("z")
    first, second = jnp.where(c == 0, x, stream), jnp.where(c == 0, stream, x)
    wanted = first if tuned else 0
    near_z, across_z = z & 1, z >> 1
    third, fourth = jnp.where(c == 0, near_z, across_z), jnp.where(c == 0, across_z, near_z)
    places = [x * 8 + stream * 4 + near_z * 2 + across_z, stream * 8 + x * 4 + across_z * 2 + near_z]
    bits = jnp.stack([c, x, stream, z & 1, z >> 1, wanted, *places]).astype(jnp.int32)

    def whole_sequence(rows):
        own = lax.dynamic_index_in_dim(rows[:, 0], stream, axis=0, keepdims=False)
        other = lax.dynamic_index_in_dim(rows[:, 0], 1 - stream, axis=0, keepdims=False)
        return own, swapped(other, side)

    def both_sequences(rows, far):
        own = rows[:CAP]
        return jnp.where(stream == 0, jnp.stack([own, far]), jnp.stack([far, own]))[:, None]

    own, far = whole_sequence(layer_input)
    features, inner_sum, middle, stamp, allowed, valid, masked = prepare(
        bits, timesteps, src_len, seq_len, key_keep, time_inner, time_inner_bias, time_outer, time_outer_bias
    )
    weights = (query_weight, query_bias, key_weight, value_weight, value_bias)
    *first_rows, own_low = project(own, 0, stamp, allowed, *weights)
    (far,) = tie([far], first_rows[:1])
    cotangent, far = lax.optimization_barrier((cotangent, far))
    cot_own, cot_far = whole_sequence(cotangent)
    *other_rows, far_low = project(far, 1, stamp, allowed, *weights)
    q, k, v = zip(first_rows, other_rows)
    low = (own_low, far_low)
    attended, lefts, probs = attend(q, k, v, low, masked)
    (lefts,) = tie([lefts], [cot_far])
    output, for_core, activated, d_expanded, mixed_low, d_reduced, expand_bias_grad, d_first, d_branch, layer_sums = feed_forward(
        bits,
        attended,
        own,
        far,
        stamp,
        output_weight,
        output_bias,
        first_gain,
        first_shift,
        expand_weight,
        expand_bias,
        reduce_weight,
        reduce_bias,
        second_gain,
        second_shift,
        valid,
        cot_own,
        cot_far,
    )
    lefts_got = swapped(lefts, core)
    (output,) = tie([output], [lefts_got])
    output_got = swapped(output[CAP:], side)
    grads, kept, sent, attend_sums = attend_back(bits, d_branch, output_weight, probs, q, k, v, allowed, [output])
    block_parts = (inner_sum, middle, features, time_outer)
    if tuned:
        (sent,) = tie([sent], [output_got])
        sent_got = swapped(sent, core)
        (for_core,) = tie([for_core], [sent_got])
        hidden_got = swapped(for_core, core)
        small, small_sent = pair_grad(bits, lefts, kept, lefts_got, sent_got, [for_core])
        (small_sent,) = tie([small_sent], [hidden_got])
        small_got = crossed(small_sent, True)
        hidden, hidden_sent = hidden_grad(bits, activated, d_reduced, d_expanded, mixed_low, hidden_got, [small_sent])
        (small_got,) = tie([small_got], [hidden])
        hidden_got = crossed(hidden_sent, True)
        small, small_sent = halved(small, small_got, second)
        small_got = crossed(small_sent, False)
        d_rows, d_time = input_grad(grads, query_weight, key_weight, value_weight, d_first, [small_sent])
        (small_got,) = tie([small_got], [d_rows])
        small, small_sent = halved(small, small_got, third)
        small_got = lined(small_sent, True)
        d_rows, d_time = tie([d_rows, d_time], [small_sent])
        input_got = swapped(d_rows[CAP:], side)
        block = block_rows(bits, attend_sums, layer_sums, expand_bias_grad, d_time, *block_parts)
        small, small_sent = halved(small, small_got, fourth)
        small_got = lined(small_sent, False)
        hidden_got, input_got = tie([hidden_got, input_got], [small_sent])
        hidden, hidden_sent = halved(hidden, hidden_got, second)
        hidden_got = crossed(hidden_sent, False)
        (small_got,) = tie([small_got], [hidden_sent])
        share = plus(small, small_got).reshape(SHARE, D)
        data, block = longer(share, block, lambda value: lined(value, False), False)
        (hidden_got,) = tie([hidden_got], [data])
        hidden, hidden_sent = halved(hidden, hidden_got, third)
        hidden_got = lined(hidden_sent, True)
        wait = lambda value: tie([value], [hidden_sent])[0]
        data, block = longer(data, block, lambda value: wait(lined(value, True)), False)
        data, block = longer(data, block, lambda value: crossed(value, False), True)
        message = jnp.concatenate([data, block])
        turned = crossed(message, True)
        message_far = swapped(message, core)
        hidden_got, output, output_got, d_rows, input_got = tie([hidden_got, output, output_got, d_rows, input_got], [message])
        hidden, hidden_sent = halved(hidden, hidden_got, fourth)
        hidden_got = lined(hidden_sent, False)
        outs = first_unpack(bits, message, message_far)
        output, input_grad_rows = both_sequences(output, output_got), both_sequences(d_rows, input_got)
        shares = (hidden.astype(f32) + hidden_got.astype(f32))[0]
        reduce_share, expand_share = shares[0], shares[1]
        (turned,) = tie([turned], [outs[0], output, input_grad_rows, shares])
        turned_far = swapped(turned, core)
        *matrices, expand_bias_grad, inner, inner_bias, outer, outer_bias = finish(
            bits, turned, turned_far, message, message_far, outs
        )
        grad_query, grad_key, grad_value, grad_output = [out.reshape(D, D) for out in matrices[:4]]
        vectors = matrices[4:]
    else:
        d_rows, d_time = input_grad(grads, query_weight, key_weight, value_weight, d_first, ())
        reduce_parts, expand_parts, pairs = [], [], []
        nothing_got = jnp.zeros_like(for_core)
        for core_bit, pair, left, right in (
            (0, kept, activated, d_expanded),
            (1, sent, for_core[:, : 2 * D], for_core[:, 4 * D :]),
        ):
            as_core = bits.at[0].set(core_bit)
            hidden = hidden_grad(as_core, left, d_reduced, right, mixed_low, nothing_got, ())
            reduce_parts.append([part[:, 0] for part in hidden])
            expand_parts.append([part[:, 1] for part in hidden])
            grad = pair_grad(as_core, lefts, pair, lefts, jnp.zeros_like(pair), ())
            pairs.append(jnp.moveaxis(jnp.concatenate(grad), 1, 0).reshape(2, D, D))
        per = FF // devices
        reduce_share, _ = scattered_sum(plain_rows(*reduce_parts).reshape(devices, per, D))
        expand_share, _ = scattered_sum(plain_rows(*expand_parts).reshape(devices, per, D))
        small_share, _ = scattered_sum(jnp.concatenate(pairs).reshape(devices, per, D))
        me = ((stream * sizes[1] + z) * 2 + x) * 2 + lax.axis_index("c")
        small = gathered(small_share)[jnp.arange(devices) ^ me].astype(f32).reshape(4, D, D)
        grad_query, grad_key, grad_value, grad_output = [small[at] for at in range(4)]
        vectors, expand_bias_grad, inner, inner_bias, outer, outer_bias = everyones(
            attend_sums + layer_sums, expand_bias_grad, d_time, *block_parts
        )
        input_grad_rows = both_sequences(d_rows, swapped(d_rows[CAP:], side))
        output = both_sequences(output, output_got)
    return (
        output,
        input_grad_rows,
        grad_query,
        vectors[0],
        grad_key,
        grad_value,
        vectors[1],
        grad_output,
        vectors[2],
        vectors[3],
        vectors[4],
        expand_share.astype(f32).T,
        expand_bias_grad.reshape(FF),
        reduce_share.astype(f32),
        vectors[5],
        vectors[6],
        vectors[7],
        inner,
        inner_bias,
        outer,
        outer_bias,
    )


def solution(mesh):
    seq, batch = mesh.devices.shape
    mesh = jax.sharding.Mesh(mesh.devices.reshape(seq, batch // 4, 2, 2), ("y", "z", "x", "c"))
    sequences, everyone = ("z", "x", "c"), ("y", "z", "x", "c")
    rows = P(sequences, "y", None, None)
    in_specs = (rows, rows) + (P(sequences),) * 3 + (P(sequences, None, None),) + (P(),) * 19
    out_specs = (rows, rows) + (P(),) * 9 + (P(None, everyone), P(), P(everyone, None)) + (P(),) * 7
    return jax.shard_map(on_device, mesh=mesh, in_specs=in_specs, out_specs=out_specs, check_vma=False)
```

```python
import functools
import math

import jax
import jax.numpy as jnp
from jax import lax
from jax.experimental import pallas as pl
from jax.experimental.pallas import tpu as pltpu
from jax.sharding import PartitionSpec as P

D = 768
HEADS = 12
HEAD_DIM = 64
FF = 3072
TDIM = 128
TFF = 512
CAP = 256
ROWS = 2 * CAP

f32 = jnp.float32
bf16 = jnp.bfloat16
highest = lax.Precision.HIGHEST
norm_epsilon = 1e-12
masked_score = -1000000000.0
root_half = 0.7071067811865476
density_scale = 0.3989422804014327


core, near, side = ("c", 0), ("x", 0), ("y", 0)


def swapped(value, stage):
    axis, bit = stage
    return lax.ppermute(value, axis, [(i, i ^ (1 << bit)) for i in range(lax.axis_size(axis))])


def own_bit(stage):
    axis, bit = stage
    return (lax.axis_index(axis) >> bit) & 1


def stage_lists():
    bits = lax.axis_size("z").bit_length() - 1
    far = [("z", k) for k in range(bits)]
    return [side] + far[::-1] + [near, core], far


def added(kept, received):
    return lax.reduce_precision(kept.astype(f32) + received.astype(f32), 8, 7).astype(bf16)


def halves(buffer, labels, stage):
    at = labels.index(stage)
    bit = own_bit(stage)
    kept = lax.dynamic_index_in_dim(buffer, bit, axis=at, keepdims=False)
    sent = lax.dynamic_index_in_dim(buffer, 1 - bit, axis=at, keepdims=False)
    return kept, sent, labels[:at] + labels[at + 1 :]


def exchange(buffer, labels, stage, riders=None):
    kept, sent, labels = halves(buffer, labels, stage)
    rows = sent.reshape(-1, D)
    if riders is None:
        return added(kept, swapped(rows, stage).reshape(kept.shape)), labels, None
    received = swapped(jnp.concatenate([rows, riders], axis=0), stage)
    return (
        added(kept, received[: rows.shape[0]].reshape(kept.shape)),
        labels,
        added(riders, received[rows.shape[0] :]),
    )


def scattered_sum(shares, riders=None):
    slow_first, far = stage_lists()
    rows = shares.shape[1]
    buffer = shares.reshape((2,) * len(slow_first) + (rows, D))
    buffer, labels, riders = exchange(buffer, slow_first, core, riders)
    cut = rows // 2
    first, first_labels, riders = exchange(buffer[..., :cut, :], labels, near, riders)
    second, second_labels, _ = exchange(buffer[..., cut:, :], labels, side)
    first, first_labels, riders = exchange(first, first_labels, side, riders)
    second, second_labels, _ = exchange(second, second_labels, near)
    buffer = jnp.concatenate([first, second], axis=-2)
    labels = first_labels
    for stage in far:
        buffer, labels, riders = exchange(buffer, labels, stage, riders)
    return buffer, riders


def gathered(share):
    slow_first, far = stage_lists()
    order = [core, near, side] + far
    buffer = share[None]
    done = []
    for stage in reversed(order):
        buffer = jnp.concatenate([buffer, swapped(buffer, stage)], axis=0)
        done.append(stage)
    bits = len(order)
    buffer = buffer.reshape((2,) * bits + share.shape)
    current = list(reversed(done))
    return jnp.transpose(buffer, [current.index(stage) for stage in slow_first] + [bits, bits + 1]).reshape(
        (1 << bits,) + share.shape
    )


def matmul(left, right):
    return jnp.dot(left, right, preferred_element_type=f32)


def column_sum(values):
    return jnp.sum(values.astype(f32), axis=0)


def dot(left, right, dims):
    return lax.dot_general(left, right, (((dims[0],), (dims[1],)), ((), ())), preferred_element_type=f32)


def nn(left, right):
    return dot(left, right, (1, 0))


def nt(left, right):
    return dot(left, right, (1, 1))


def tn(left, right):
    return dot(left, right, (0, 0))


def whole(*shape):
    return pl.BlockSpec(shape, lambda *at: (0,) * len(shape))


def vector(size):
    return pl.BlockSpec((size,), lambda *at: (0,))


def vector_tile(width):
    return pl.BlockSpec((width,), lambda j, *at: (j,))


def row(ref):
    return ref[...].reshape(1, -1)


def column_tile(rows, width):
    return pl.BlockSpec((rows, width), lambda j, *at: (0, j))


def row_tile(height, width):
    return pl.BlockSpec((height, width), lambda j, *at: (j, 0))


def run(body, grid, operands, in_specs, outs, out_specs, flops, scratch=(), scalars=(), after=(), aliases=None):
    shapes = [jax.ShapeDtypeStruct(shape, dtype) for shape, dtype in outs]
    sizes = [x.size * x.dtype.itemsize for x in list(operands) + shapes]
    used = len(scalars) + len(operands)

    def wrapped(*refs):
        body(*refs[:used], *refs[used + len(after) :])

    return pl.pallas_call(
        wrapped,
        grid_spec=pltpu.PrefetchScalarGridSpec(
            num_scalar_prefetch=len(scalars),
            grid=grid,
            in_specs=in_specs + [pl.BlockSpec(memory_space=pl.ANY)] * len(after),
            out_specs=out_specs,
            scratch_shapes=scratch,
        ),
        out_shape=shapes,
        input_output_aliases=aliases or {},
        compiler_params=pltpu.CompilerParams(vmem_limit_bytes=(63 << 20) + (960 << 10)),
        cost_estimate=pl.CostEstimate(flops=int(flops), bytes_accessed=sum(sizes), transcendentals=0),
    )(*scalars, *operands, *after)


def nothing(*refs):
    pass


def tie(values, after):
    anywhere = pl.BlockSpec(memory_space=pl.ANY)
    return pl.pallas_call(
        nothing,
        in_specs=[anywhere] * (len(values) + len(after)),
        out_specs=[anywhere] * len(values),
        out_shape=[jax.ShapeDtypeStruct(value.shape, value.dtype) for value in values],
        input_output_aliases={k: k for k in range(len(values))},
        compiler_params=pltpu.CompilerParams(vmem_limit_bytes=(63 << 20) + (960 << 10)),
    )(*values, *after)


def normalized(values):
    center = values - jnp.mean(values, axis=-1, keepdims=True)
    spread = jnp.mean(center * center, axis=-1, keepdims=True)
    inverse = lax.rsqrt(spread + norm_epsilon)
    return center * inverse, inverse


def norm_backward(upstream, normed, inverse):
    first_mean = jnp.mean(upstream, axis=-1, keepdims=True)
    second_mean = jnp.mean(upstream * normed, axis=-1, keepdims=True)
    return inverse * (upstream - first_mean - normed * second_mean)


def row_sum(values):
    return jnp.sum(values, axis=0, keepdims=True)


def prepare_body(bits, stamps, src_len, seq_len, flags, inner, inner_bias, outer, outer_bias, cotangent, *outs):
    features, inner_sum, middle, stamp, allowed, valid, masked, cot_other = outs
    cot_other[...] = cotangent[0]
    y = bits[2]
    lane = lax.broadcasted_iota(jnp.int32, (1, TDIM), 1)
    half = TDIM // 2
    frequency = jnp.exp(-math.log(10000.0) * lax.rem(lane, half).astype(f32) / half)
    angles = jnp.broadcast_to(stamps[y].astype(f32), (1, TDIM)) * frequency
    waves = jnp.where(lane < half, jnp.cos(angles), jnp.sin(angles))
    features[...] = waves
    total = jnp.dot(waves, inner[...].astype(f32), precision=highest) + row(inner_bias)
    inner_sum[...] = total
    gated = total * (1.0 / (1.0 + jnp.exp(-total)))
    middle[...] = gated
    stamp[...] = jnp.dot(gated, outer[...].astype(f32), precision=highest) + row(outer_bias)
    source, target = src_len[y], seq_len[y] - src_len[y]
    slots = lax.broadcasted_iota(jnp.int32, (CAP, 1), 0)
    lengths = jnp.where(y == 0, source, target), jnp.where(y == 0, target, source)
    for at, (length, stream) in enumerate(zip(lengths, (y, 1 - y))):
        inside = jnp.where(slots < length, 1.0, 0.0)
        kept = jnp.where(flags[y, pl.ds(stream, 1)] == 1, 1.0, 0.0)
        kept = jnp.broadcast_to(kept, (8, CAP)).T[:, :1]
        here = slice(at * CAP, (at + 1) * CAP)
        valid[here] = inside
        allowed[here] = inside * kept
        masked[here] = (1.0 - inside * kept) * masked_score


def prepare(bits, stamps, src_len, seq_len, flags, inner, inner_bias, outer, outer_bias, cotangent):
    return run(
        prepare_body,
        (1,),
        (flags, inner, inner_bias, outer, outer_bias, cotangent),
        [whole(2, 2, CAP), whole(TDIM, TFF), vector(TFF), whole(TFF, D), vector(D)]
        + [pl.BlockSpec((1, CAP, D), lambda j, bits, *at: (1 - bits[2], 0, 0))],
        [((1, size), f32) for size in (TDIM, TFF, TFF, D)] + [((ROWS, 1), f32)] * 3 + [((CAP, D), bf16)],
        [whole(1, size) for size in (TDIM, TFF, TFF, D)] + [whole(ROWS, 1)] * 3 + [whole(CAP, D)],
        0,
        scalars=(bits, stamps, src_len, seq_len),
    )


def project_body(rows, stamp, keep, qw, qb, kw, vw, vb, q, k, v, low_out):
    low = (rows[...].astype(f32) + stamp[...]).astype(bf16)
    low_out[...] = low
    q[...] = ((nn(low, qw[...]) + row(qb)).astype(bf16).astype(f32) * 0.125).astype(bf16)
    k[...] = (nn(low, kw[...]) * keep[...]).astype(bf16)
    v[...] = (nn(low, vw[...]) + row(vb)).astype(bf16)


def project(rows, half, stamp, keep, qw, qb, kw, vw, vb):
    tile = 256
    return run(
        project_body,
        (D // tile,),
        (rows, stamp, keep, qw, qb, kw, vw, vb),
        [whole(CAP, D), whole(1, D), pl.BlockSpec((CAP, 1), lambda *at: (half, 0))]
        + [column_tile(D, tile), vector_tile(tile), column_tile(D, tile), column_tile(D, tile), vector_tile(tile)],
        [((CAP, D), bf16)] * 4,
        [column_tile(CAP, tile)] * 3 + [whole(CAP, D)],
        6 * CAP * D * D,
    )


def lanes_of(shape):
    return lax.broadcasted_iota(jnp.int32, shape, 1)


def both(own, far):
    return jnp.concatenate([own[...], far[...]], axis=0)


def attend_body(qo, qf, ko, kf, vo, vf, lo, lf, masked, attended, for_core, probs):
    q, k, v = both(qo, qf), both(ko, kf), both(vo, vf)
    lane = lanes_of(q.shape)
    flag = jnp.broadcast_to(masked[...], q.shape).astype(bf16)
    v_turned = v.T
    pieces = []
    for head in range(2):
        mine = (lane // HEAD_DIM) == head
        spare = lane == (1 - head) * HEAD_DIM
        k_head = jnp.where(mine, k, jnp.where(spare, flag, 0))
        q_head = jnp.where(mine, q, jnp.where(spare, 1, 0).astype(bf16))
        scores = nt(k_head, q_head)
        top = jnp.max(scores, axis=0, keepdims=True)
        exponent = jnp.exp(scores - top)
        inverse = 1.0 / jnp.sum(exponent, axis=0, keepdims=True)
        low = (exponent * inverse).astype(bf16)
        probs[head] = low
        pieces.append(nn(v_turned[head * HEAD_DIM : (head + 1) * HEAD_DIM], low))
    low = jnp.concatenate(pieces, axis=0).T.astype(bf16)
    attended[...] = low
    for_core[0], for_core[1] = both(lo, lf), low


def attend(q, k, v, low, masked):
    pair = 2 * HEAD_DIM
    return run(
        attend_body,
        (D // pair,),
        (*q, *k, *v, *low, masked),
        [column_tile(CAP, pair)] * 8 + [whole(ROWS, 1)],
        [((ROWS, D), bf16), ((2, ROWS, D), bf16), ((HEADS, ROWS, ROWS), bf16)],
        [column_tile(ROWS, pair), pl.BlockSpec((2, ROWS, pair), lambda j: (0, 0, j))]
        + [pl.BlockSpec((2, ROWS, ROWS), lambda j: (j, 0, 0))],
        4 * HEADS * ROWS * ROWS * 256,
    )


SHARE = 96
COLOUR = 48


half_tile = pl.BlockSpec((ROWS, D // 2), lambda j, *at: (0, j))


FOR_CORE = (ROWS, FF + 2 * D)


def by_core(values):
    return [
        jnp.concatenate([values[:, at : at + SHARE] for at in range(start, D, 2 * SHARE)], axis=1) for start in (0, SHARE)
    ]


SUB = 256


def feed_forward_body(
    bits, attended, own, far, stamp, ow, ob, gain, shift, ew, eb, rw, rb, gain2, shift2, valid, cot_own, cot_far,
    output, far_output, for_core, activated_own, expanded_own, mixed_low, d_reduced, bias_grad, d_first, d_branch, sums,
    total, normed, inverse, slope, columns,
):
    step = pl.program_id(0)
    tiles = FF // D

    def store(own_out, offset):
        zero, one = by_core(columns[...])
        here = pl.ds(pl.multiple_of(offset, D // 2), D // 2)

        @pl.when(bits[0] == 0)
        def _():
            own_out[...], for_core[:, here] = zero, one

        @pl.when(bits[0] == 1)
        def _():
            own_out[...], for_core[:, here] = one, zero

    @pl.when(step == 0)
    def _():
        hidden = both(own, far).astype(f32) + stamp[...]
        n1, inv = normalized(hidden + nn(attended[...], ow[...]) + row(ob))
        value = n1 * row(gain) + row(shift)
        normed[...] = n1
        inverse[...] = inv
        mixed_low[...] = value.astype(bf16)
        total[...] = value + row(rb)

    @pl.when(step < tiles)
    def _():
        added_up = None
        bias = eb[pl.ds(pl.multiple_of(step * D, D), D)].reshape(1, -1)
        for part in range(D // SUB):
            cut = slice(part * SUB, (part + 1) * SUB)
            expanded = nn(mixed_low[...], ew[:, cut]) + bias[:, cut]
            chance = 0.5 * (1.0 + lax.erf(expanded * root_half))
            slope[step, :, cut] = chance + expanded * jnp.exp(-0.5 * expanded * expanded) * density_scale
            low = (expanded * chance).astype(bf16)
            columns[:, cut] = low
            product = nn(low, rw[cut, :])
            added_up = product if added_up is None else added_up + product
        total[...] += added_up
        store(activated_own, step * (D // 2))

    @pl.when(step == tiles - 1)
    def _():
        n2, inv = normalized(total[...])
        weight = valid[...]
        rows = ((n2 * row(gain2) + row(shift2)) * weight).astype(bf16)
        output[...], far_output[...] = rows[:CAP], rows[CAP:]
        d_out = jnp.concatenate([cot_own[0], cot_far[...]], axis=0).astype(f32) * weight
        back = norm_backward(d_out * row(gain2), n2, inv)
        low = back.astype(bf16)
        total[...] = back
        d_reduced[...] = low
        for_core[:, 2 * D : 3 * D] = low
        for_core[:, 3 * D : 4 * D] = mixed_low[...]
        sums[...] = jnp.concatenate(
            [jnp.zeros((5, D), f32), row_sum(low.astype(f32)), row_sum(d_out * n2), row_sum(d_out)], axis=0
        )

    @pl.when(step >= tiles)
    def _():
        d_expanded = (nt(d_reduced[...], rw[...]) * slope[step - tiles]).astype(bf16)
        columns[...] = d_expanded
        bias_grad[0] = row_sum(d_expanded.astype(f32))
        total[...] += nt(d_expanded, ew[...])
        store(expanded_own, 4 * D + (step - tiles) * (D // 2))

    @pl.when(step == 2 * tiles - 1)
    def _():
        d_mixed = total[...]
        n1 = normed[...]
        back = norm_backward(d_mixed * row(gain), n1, inverse[...])
        low = back.astype(bf16)
        d_first[...] = back
        d_branch[...] = low
        sums[2:5] = jnp.concatenate([row_sum(low.astype(f32)), row_sum(d_mixed * n1), row_sum(d_mixed)], axis=0)


def feed_forward(
    bits, attended, own, far, stamp, ow, ob, gain, shift, ew, eb, rw, rb, gain2, shift2, valid, cot_own, cot_far
):
    tiles = FF // D
    line, square, half = vector(D), whole(ROWS, D), whole(CAP, D)
    forward = pl.BlockSpec((ROWS, D // 2), lambda j, *at: (0, jnp.minimum(j, tiles - 1)))
    backward = pl.BlockSpec((ROWS, D // 2), lambda j, *at: (0, jnp.maximum(j - tiles, 0)))
    return run(
        feed_forward_body,
        (2 * tiles,),
        (attended, own, far, stamp, ow, ob, gain, shift, ew, eb, rw, rb, gain2, shift2, valid, cot_own, cot_far),
        [square, half, half, whole(1, D), whole(D, D), line, line, line]
        + [pl.BlockSpec((D, D), lambda j, *at: (0, j % tiles)), vector(FF), pl.BlockSpec((D, D), lambda j, *at: (j % tiles, 0))]
        + [line, line, line, whole(ROWS, 1), pl.BlockSpec((1, CAP, D), lambda j, bits: (bits[2], 0, 0)), half],
        [((CAP, D), bf16)] * 2
        + [(FOR_CORE, bf16), ((ROWS, FF // 2), bf16), ((ROWS, FF // 2), bf16), ((ROWS, D), bf16)]
        + [((ROWS, D), bf16), ((tiles, 1, D), f32), ((ROWS, D), f32), ((ROWS, D), bf16), ((8, D), f32)],
        [half, half, whole(*FOR_CORE), forward, backward, square, square]
        + [pl.BlockSpec((1, 1, D), lambda j, *at: (jnp.maximum(j - tiles, 0), 0, 0)), square, square, whole(8, D)],
        2 * ROWS * D * (D + 4 * FF),
        scratch=[pltpu.VMEM((ROWS, D), f32)] * 2
        + [pltpu.VMEM((ROWS, 1), f32), pltpu.VMEM((tiles, ROWS, D), f32), pltpu.VMEM((ROWS, D), bf16)],
        scalars=(bits,),
    )


def hidden_grad_body(bits, activated, d_reduced, d_expanded, mixed, activated_got, reduced_got, mixed_got, expanded_got, kept, sent):
    step = pl.program_id(0)
    tile = step % 2

    def store(kind, grad):
        low = grad.astype(bf16)
        for at in range(8):
            x, z = at % 2, at // 2
            here = jnp.where(bits[0] == 0, tile * 4 + (z % 2 * 2 + z // 2), x * 4 + z)
            block = low[at * SHARE : (at + 1) * SHARE]
            mine = jnp.where(bits[0] == 0, x, tile) == bits[5]

            @pl.when(mine)
            def _():
                kept[here, kind] = block

            @pl.when(jnp.logical_not(mine))
            def _():
                sent[here, kind] = block

    @pl.when(step < 2)
    def _():
        store(0, tn(activated[...], d_reduced[...]) + tn(activated_got[...], reduced_got[...]))

    @pl.when(step >= 2)
    def _():
        store(1, tn(d_expanded[...], mixed[...]) + tn(expanded_got[...], mixed_got[...]))


def hidden_grad(bits, activated, d_reduced, d_expanded, mixed, got, after):
    first = lambda start: pl.BlockSpec((ROWS, D), lambda j, bits: (0, start + jnp.minimum(j, 1)))
    second = lambda start: pl.BlockSpec((ROWS, D), lambda j, bits: (0, start + jnp.maximum(j - 2, 0)))
    square = lambda at: pl.BlockSpec((ROWS, D), lambda j, bits: (0, at))
    return run(
        hidden_grad_body,
        (4,),
        (activated, d_reduced, d_expanded, mixed, got, got, got, got),
        [first(0), square(0), second(0), square(0), first(0), square(2), square(3), second(4)],
        [((8, 2, SHARE, D), bf16)] * 2,
        [whole(8, 2, SHARE, D)] * 2,
        4 * ROWS * D * FF,
        scalars=(bits,),
        after=after,
    )


def attend_back_body(bits, d_branch, branch, ow, probs, qo, qf, ko, kf, vo, vf, keep, grads, kept, sent, sums):
    q, k, v = both(qo, qf), both(ko, kf), both(vo, vf)
    lane = lanes_of(q.shape)
    low_half = lane < HEAD_DIM
    upstream = nt(d_branch[...], ow[...]).astype(bf16)
    k_turned = k.T
    d_q, d_k, d_v = [], [], []
    for head in range(2):
        rows = slice(head * HEAD_DIM, (head + 1) * HEAD_DIM)
        mine = low_half if head == 0 else jnp.logical_not(low_half)
        low = probs[head]
        wide = low.astype(f32)
        weighted = wide * nt(jnp.where(mine, v, 0), upstream)
        d_scores = (weighted - wide * row_sum(weighted)).astype(bf16)
        d_v.append(nn(low, upstream))
        d_k.append(nn(d_scores, q))
        d_q.append(nn(k_turned[rows], d_scores))
    q_low = (jnp.concatenate(d_q, axis=0).T * 0.125).astype(bf16)
    v_low = jnp.where(low_half, d_v[0], d_v[1]).astype(bf16)
    k_low = (jnp.where(low_half, d_k[0], d_k[1]) * keep[...]).astype(bf16)
    grads[0], grads[1], grads[2] = q_low, k_low, v_low

    def share(first, second):
        first[0], first[1] = q_low, k_low
        second[0], second[1] = v_low, branch[...]

    @pl.when(bits[0] == 0)
    def _():
        share(kept, sent)

    @pl.when(bits[0] == 1)
    def _():
        share(sent, kept)

    sums[...] = jnp.concatenate(
        [row_sum(q_low.astype(f32)), row_sum(v_low.astype(f32)), jnp.zeros((6, q.shape[1]), f32)], axis=0
    )


def attend_back(bits, d_branch, ow, probs, q, k, v, keep, after):
    pair = 2 * HEAD_DIM
    return run(
        attend_back_body,
        (D // pair,),
        (d_branch, d_branch, ow, probs, *q, *k, *v, keep),
        [whole(ROWS, D), column_tile(ROWS, pair), row_tile(pair, D), pl.BlockSpec((2, ROWS, ROWS), lambda j, *at: (j, 0, 0))]
        + [column_tile(CAP, pair)] * 6
        + [whole(ROWS, 1)],
        [((count, ROWS, D), bf16) for count in (3, 2, 2)] + [((8, D), f32)],
        [pl.BlockSpec((count, ROWS, pair), lambda j, *at: (0, 0, j)) for count in (3, 2, 2)] + [column_tile(8, pair)],
        10 * HEADS * ROWS * ROWS * 256,
        scalars=(bits,),
        after=after,
    )


def pair_grad_body(bits, left, right, left_got, right_got, kept, sent):
    low = (tn(left[0], right[0]) + tn(left_got[0], right_got[0])).astype(bf16)
    zero, one = [low[at * D // 2 : (at + 1) * D // 2].reshape(8, COLOUR, D) for at in range(2)]
    kept[:, 0] = jnp.where(bits[5] == 0, zero, one)
    sent[:, 0] = jnp.where(bits[5] == 0, one, zero)


def pair_grad(bits, left, right, left_got, right_got, after):
    lefts = pl.BlockSpec((1, ROWS, D), lambda j, bits: (j * bits[0], 0, 0))
    rights = pl.BlockSpec((1, ROWS, D), lambda j, bits: (j, 0, 0))
    return run(
        pair_grad_body,
        (2,),
        (left, right, left_got, right_got),
        [lefts, rights] * 2,
        [((8, 2, COLOUR, D), bf16)] * 2,
        [pl.BlockSpec((8, 1, COLOUR, D), lambda j, *at: (0, j, 0, 0))] * 2,
        8 * ROWS * D * D,
        scalars=(bits,),
        after=after,
    )


def input_grad_body(grads, qw, kw, vw, d_first, own_rows, far_rows, d_time):
    total = d_first[...] + nt(grads[0], qw[...]) + nt(grads[1], kw[...]) + nt(grads[2], vw[...])
    low = total.astype(bf16)
    own_rows[...], far_rows[...] = low[:CAP], low[CAP:]
    d_time[...] = row_sum(total)


def input_grad(grads, qw, kw, vw, d_first, after):
    tile = 256
    return run(
        input_grad_body,
        (D // tile,),
        (grads, qw, kw, vw, d_first),
        [whole(3, ROWS, D)] + [row_tile(tile, D)] * 3 + [column_tile(ROWS, tile)],
        [((CAP, D), bf16)] * 2 + [((1, D), f32)],
        [column_tile(CAP, tile)] * 2 + [column_tile(1, tile)],
        6 * ROWS * D * D,
        after=after,
    )


everywhere = ("y", "z", "x", "c")


def crossed(value, first):
    sizes = [lax.axis_size(axis) for axis in everywhere]
    pairs = []
    for at in range(math.prod(sizes)):
        c, x = at % 2, at // 2 % 2
        along_x = (c == 0) == first
        step = 2 * (1 - 2 * x) if along_x else (math.prod(sizes) // 2) * (1 - 2 * (at // (math.prod(sizes) // 2)))
        pairs.append((at, at + step))
    return lax.ppermute(value, everywhere, pairs)


def lined(value, first):
    sizes = [lax.axis_size(axis) for axis in everywhere]
    turn = lambda c: 1 if (c == 0) == first else 2
    pairs = [(at, at ^ (turn(at % 2) * 4)) for at in range(math.prod(sizes))]
    return lax.ppermute(value, everywhere, pairs)


def plus(left, right):
    return (left.astype(f32) + right.astype(f32)).astype(bf16)


def halved(own, got, bit):
    own, got = [value.reshape((2, -1) + value.shape[1:]) for value in (own, got)]
    at = lambda place: [lax.dynamic_index_in_dim(value, place, 0, keepdims=False) for value in (own, got)]
    return plus(*at(bit)), plus(*at(1 - bit))


BLOCK = 32


def block_body(bits, first, second, bias, d_time, inner_sum, middle, features, outer, out):
    riders = first[...] + second[...]
    total = inner_sum[...]
    gate = 1.0 / (1.0 + jnp.exp(-total))
    d_middle = lax.dot_general(
        d_time[...], outer[...].astype(f32), (((1,), (1,)), ((), ())), precision=highest, preferred_element_type=f32
    )
    d_inner = d_middle * (gate * (1.0 + total * (1.0 - gate)))
    wide = D - TFF
    rows = [jnp.concatenate([d_time[:, at * wide : (at + 1) * wide], middle[...]], axis=1) for at in range(3)]
    rows.append(jnp.concatenate([d_inner, features[...], jnp.zeros((1, wide - TDIM), f32)], axis=1))
    index = lax.broadcasted_iota(jnp.int32, (16, D), 0)
    factors = jnp.zeros((16, D), f32)
    for at, values in enumerate(rows):
        factors = jnp.where(index == 4 * (bits[3] + 2 * bits[4]) + at, values, factors)
    biases = jnp.zeros((8, D), f32)
    index = lax.broadcasted_iota(jnp.int32, (8, D), 0)
    for at in range(4):
        biases = jnp.where(index == at, bias[at], biases)
    out[...] = jnp.concatenate([riders, biases, factors], axis=0).astype(bf16)


def block_rows(bits, *operands):
    return run(
        block_body,
        (1,),
        operands,
        [whole(*operand.shape) for operand in operands],
        [((BLOCK, D), bf16)],
        [whole(BLOCK, D)],
        0,
        scalars=(bits,),
    )[0]


def sum_rows(own, got):
    return lax.reduce_precision(own.astype(f32) + got.astype(f32), 8, 7).astype(bf16)


def longer(data, block, send):
    got = send(jnp.concatenate([data, block]))
    size = data.shape[0]
    return jnp.concatenate([data, got[:size]]), sum_rows(block, got[size:])


def unpack_body(bits, pieces, outs):
    for turn in range(2):

        @pl.when(pl.program_id(0) == turn)
        def _():
            own, got = pieces[turn], pieces[2 + turn]
            for at in range(4):
                here, there = (bits[6] % 4) ^ at, (bits[7] % 4) ^ at
                for matrix in range(2):
                    rows = slice(at * SHARE + matrix * COLOUR, at * SHARE + (matrix + 1) * COLOUR)
                    mine, other = own[rows].astype(f32), got[rows].astype(f32)
                    outs[matrix][here] = jnp.where(bits[0] == 0, mine, other)
                    outs[2 + matrix][there] = jnp.where(bits[0] == 0, other, mine)


def unpack_specs(turn):
    part = whole(4 * SHARE, D)
    spots = [
        pl.BlockSpec((4, COLOUR, D), lambda j, bits, at=at: ((bits[at] // 4) ^ (2 * turn + j), 0, 0)) for at in (6, 6, 7, 7)
    ]
    return part, spots


matrix_shapes = [((16, COLOUR, D), f32)] * 4


def first_unpack(bits, pieces):
    part, spots = unpack_specs(0)
    body = lambda bits, *refs: unpack_body(bits, refs[:4], refs[4:])
    return run(body, (2,), pieces, [part] * 4, matrix_shapes, spots, 0, scalars=(bits,))


def finish_body(bits, *refs):
    unpack_body(bits, refs[:4], refs[16:20])

    @pl.when(pl.program_id(0) == 1)
    def _():
        vectors_body(refs[4:12], *refs[20:])


def vectors_body(refs, *outs):
    blocks = [ref[...].astype(f32) for ref in refs]
    riders = [block[:16] for block in blocks]
    pairs = [riders[at] + riders[at + 1] for at in range(0, 8, 2)]
    sums = (pairs[0] + pairs[1]) + (pairs[2] + pairs[3])
    for at in range(8):
        outs[at][...] = sums[at]
    for at in range(4):
        outs[8][at] = sums[8 + at : 9 + at]
    factors = jnp.concatenate([block[16:] for block in blocks], axis=0)
    index = lax.broadcasted_iota(jnp.int32, factors.shape, 0) % 4
    wide = D - TFF
    inner, inner_bias, outer, outer_bias = outs[9:]
    for at in range(3):
        rows = jnp.where(index == at, factors, 0.0)
        d_time = rows[:, :wide]
        here = slice(at * wide, (at + 1) * wide)
        outer[:, here] = tn(rows[:, wide:].astype(bf16), d_time.astype(bf16))
        outer_bias[here] = jnp.sum(d_time, axis=0)
    rows = jnp.where(index == 3, factors, 0.0)
    d_inner = rows[:, :TFF]
    inner[...] = tn(rows[:, TFF : TFF + TDIM].astype(bf16), d_inner.astype(bf16))
    inner_bias[...] = jnp.sum(d_inner, axis=0)


def finish(bits, turned, turned_far, pieces, pieces_far, outs):
    part, spots = unpack_specs(1)
    last = pl.BlockSpec((BLOCK, D), lambda j, *at: (4 * SHARE // BLOCK, 0))
    shapes = [(D,)] * 8 + [(4, 1, D), (TDIM, TFF), (TFF,), (TFF, D), (D,)]
    return run(
        finish_body,
        (2,),
        (*turned, *turned_far, *pieces, *turned, *pieces_far, *turned_far, *outs),
        [part] * 4 + [last] * 8 + [pl.BlockSpec(memory_space=pl.ANY)] * 4,
        matrix_shapes + [(shape, f32) for shape in shapes],
        spots + [whole(*shape) for shape in shapes],
        0,
        scalars=(bits,),
        aliases={13 + k: k for k in range(4)},
    )


def plain_rows(first_class, second_class):
    zero = jnp.concatenate(first_class).reshape(2, 2, 2, 2, SHARE, D)
    one = jnp.concatenate(second_class).reshape(2, 2, 2, 2, SHARE, D)
    classes = jnp.stack([jnp.transpose(zero, (1, 3, 2, 0, 4, 5)), jnp.transpose(one, (0, 2, 3, 1, 4, 5))], axis=4)
    return classes.reshape(FF, D)


def everyones(sums, bias, d_time, inner_sum, middle, features, outer):
    gate = jax.nn.sigmoid(inner_sum)
    d_inner = jnp.dot(d_time, outer.astype(f32).T, precision=highest) * (gate * (1.0 + inner_sum * (1.0 - gate)))
    riders = jnp.concatenate([sums, bias.reshape(4, D), jnp.zeros((4, D), f32)])
    factors = jnp.concatenate([d_time, d_inner, middle, features], axis=1)
    for stage in stage_lists()[0]:
        riders = riders + swapped(riders, stage)
        factors = jnp.concatenate([factors, swapped(factors, stage)])
    cuts = (0, D, D + TFF, D + 2 * TFF, D + 2 * TFF + TDIM)
    d_time, d_inner, middle, features = [factors[:, a:b] for a, b in zip(cuts, cuts[1:])]
    inner, outer = matmul(features.T, d_inner), matmul(middle.T, d_time)
    return list(riders[:8]), riders[8:12], inner, column_sum(d_inner), outer, column_sum(d_time)


def on_device(
    layer_input,
    cotangent,
    timesteps,
    src_len,
    seq_len,
    key_keep,
    query_weight,
    query_bias,
    key_weight,
    value_weight,
    value_bias,
    output_weight,
    output_bias,
    first_gain,
    first_shift,
    expand_weight,
    expand_bias,
    reduce_weight,
    reduce_bias,
    second_gain,
    second_shift,
    time_inner,
    time_inner_bias,
    time_outer,
    time_outer_bias,
):
    stream = lax.axis_index("y")
    sizes = [lax.axis_size(axis) for axis in ("y", "z", "x", "c")]
    devices = math.prod(sizes)
    tuned = sizes == [2, 4, 2, 2]
    c, x, z = lax.axis_index("c") if tuned else 0, lax.axis_index("x"), lax.axis_index("z")
    first, second = jnp.where(c == 0, x, stream), jnp.where(c == 0, stream, x)
    wanted = first if tuned else 0
    near_z, across_z = z & 1, z >> 1
    third, fourth = jnp.where(c == 0, near_z, across_z), jnp.where(c == 0, across_z, near_z)
    places = [x * 8 + stream * 4 + near_z * 2 + across_z, stream * 8 + x * 4 + across_z * 2 + near_z]
    bits = jnp.stack([c, x, stream, z & 1, z >> 1, wanted, *places]).astype(jnp.int32)

    def whole_sequence(rows):
        own = lax.dynamic_index_in_dim(rows[:, 0], stream, axis=0, keepdims=False)
        other = lax.dynamic_index_in_dim(rows[:, 0], 1 - stream, axis=0, keepdims=False)
        return own, other

    def both_sequences(rows, far):
        own = rows
        return jnp.where(stream == 0, jnp.stack([own, far]), jnp.stack([far, own]))[:, None]

    own, other = whole_sequence(layer_input)
    far = swapped(other, side)
    cotangent = cotangent[:, 0]
    features, inner_sum, middle, stamp, allowed, valid, masked, cot_other = prepare(
        bits, timesteps, src_len, seq_len, key_keep, time_inner, time_inner_bias, time_outer, time_outer_bias, cotangent
    )
    weights = (query_weight, query_bias, key_weight, value_weight, value_bias)
    *first_rows, own_low = project(own, 0, stamp, allowed, *weights)
    (far,) = tie([far], first_rows[:1])
    cot_other, far = lax.optimization_barrier((cot_other, far))
    cot_far = swapped(cot_other, side)
    *other_rows, far_low = project(far, 1, stamp, allowed, *weights)
    q, k, v = zip(first_rows, other_rows)
    low = (own_low, far_low)
    attended, lefts, probs = attend(q, k, v, low, masked)
    (lefts,) = tie([lefts], [cot_far])
    output, far_output, for_core, activated, d_expanded, mixed_low, d_reduced, *others = feed_forward(
        bits,
        attended,
        own,
        far,
        stamp,
        output_weight,
        output_bias,
        first_gain,
        first_shift,
        expand_weight,
        expand_bias,
        reduce_weight,
        reduce_bias,
        second_gain,
        second_shift,
        valid,
        cotangent,
        cot_far,
    )
    expand_bias_grad, d_first, d_branch, layer_sums = others
    lefts_got = swapped(lefts, core)
    (far_output,) = tie([far_output], [lefts_got])
    output_got = swapped(far_output, side)
    grads, kept, sent, attend_sums = attend_back(bits, d_branch, output_weight, probs, q, k, v, allowed, [far_output])
    block_parts = (inner_sum, middle, features, time_outer)
    if tuned:
        (sent,) = tie([sent], [output_got])
        sent_got = swapped(sent, core)
        (for_core,) = tie([for_core], [sent_got])
        hidden_got = swapped(for_core, core)
        small, small_sent = pair_grad(bits, lefts, kept, lefts_got, sent_got, [for_core])
        (small_sent,) = tie([small_sent], [hidden_got])
        small_got = crossed(small_sent, True)
        hidden, hidden_sent = hidden_grad(bits, activated, d_reduced, d_expanded, mixed_low, hidden_got, [small_sent])
        (small_got,) = tie([small_got], [hidden])
        hidden_got = crossed(hidden_sent, True)
        small_sent = halved(small, small_got, second)[1]
        (small_got,) = tie([small_got], [small_sent])
        small = halved(small, small_got, second)[0]
        small_got = crossed(small_sent, False)
        d_rows, far_grad, d_time = input_grad(grads, query_weight, key_weight, value_weight, d_first, [small_sent])
        block = block_rows(bits, attend_sums, layer_sums, expand_bias_grad, d_time, *block_parts)
        (small_got,) = tie([small_got], [block])
        small, small_sent = halved(small, small_got, third)
        small_got = lined(small_sent, True)
        (far_grad,) = tie([far_grad], [small_sent])
        input_got = swapped(far_grad, side)
        small, small_sent = halved(small, small_got, fourth)
        small_got = lined(small_sent, False)
        hidden_got, input_got = tie([hidden_got, input_got], [small_sent])
        hidden, hidden_sent = halved(hidden, hidden_got, second)
        hidden_got = crossed(hidden_sent, False)
        (small_got,) = tie([small_got], [hidden_sent])
        share = plus(small, small_got).reshape(SHARE, D)
        data, block = longer(share, block, lambda value: lined(value, False))
        (hidden_got,) = tie([hidden_got], [data])
        hidden, hidden_sent = halved(hidden, hidden_got, third)
        hidden_got = lined(hidden_sent, True)
        wait = lambda value: tie([value], [hidden_sent])[0]
        data, block = longer(data, block, lambda value: wait(lined(value, True)))
        piece = jnp.concatenate([data, block])
        cross_got = crossed(piece, False)
        turned = crossed(piece, True)
        hidden, hidden_sent = halved(hidden, hidden_got, fourth)
        hidden_got = lined(hidden_sent, False)
        (cross_got,) = tie([cross_got], [hidden_sent, turned])
        pieces, turned = (piece, cross_got), (turned, crossed(cross_got, True))
        pieces_far = [swapped(value, core) for value in pieces]
        output, output_got, d_rows, input_got = tie([output, output_got, d_rows, input_got], [cross_got])
        outs = first_unpack(bits, (*pieces, *pieces_far))
        output, input_grad_rows = both_sequences(output, output_got), both_sequences(d_rows, input_got)
        turned = tie(turned, [outs[0], output, input_grad_rows])
        turned_far = [swapped(value, core) for value in turned]
        (hidden_got,) = tie([hidden_got], turned)
        shares = (hidden.astype(f32) + hidden_got.astype(f32))[0]
        reduce_share, expand_share = shares[0], shares[1]
        *matrices, expand_bias_grad, inner, inner_bias, outer, outer_bias = finish(
            bits, turned, turned_far, pieces, pieces_far, outs
        )
        grad_query, grad_key, grad_value, grad_output = [out.reshape(D, D) for out in matrices[:4]]
        vectors = matrices[4:]
    else:
        d_rows, far_grad, d_time = input_grad(grads, query_weight, key_weight, value_weight, d_first, ())
        reduce_parts, expand_parts, pairs = [], [], []
        nothing_got = jnp.zeros_like(for_core)
        for core_bit, pair, left, right in (
            (0, kept, activated, d_expanded),
            (1, sent, for_core[:, : 2 * D], for_core[:, 4 * D :]),
        ):
            as_core = bits.at[0].set(core_bit)
            hidden = hidden_grad(as_core, left, d_reduced, right, mixed_low, nothing_got, ())
            reduce_parts.append([part[:, 0] for part in hidden])
            expand_parts.append([part[:, 1] for part in hidden])
            grad = pair_grad(as_core, lefts, pair, lefts, jnp.zeros_like(pair), ())
            pairs.append(jnp.moveaxis(jnp.concatenate(grad), 1, 0).reshape(2, D, D))
        per = FF // devices
        reduce_share, _ = scattered_sum(plain_rows(*reduce_parts).reshape(devices, per, D))
        expand_share, _ = scattered_sum(plain_rows(*expand_parts).reshape(devices, per, D))
        small_share, _ = scattered_sum(jnp.concatenate(pairs).reshape(devices, per, D))
        me = ((stream * sizes[1] + z) * 2 + x) * 2 + lax.axis_index("c")
        small = gathered(small_share)[jnp.arange(devices) ^ me].astype(f32).reshape(4, D, D)
        grad_query, grad_key, grad_value, grad_output = [small[at] for at in range(4)]
        vectors, expand_bias_grad, inner, inner_bias, outer, outer_bias = everyones(
            attend_sums + layer_sums, expand_bias_grad, d_time, *block_parts
        )
        input_grad_rows = both_sequences(d_rows, swapped(far_grad, side))
        output = both_sequences(output, output_got)
    return (
        output,
        input_grad_rows,
        grad_query,
        vectors[0],
        grad_key,
        grad_value,
        vectors[1],
        grad_output,
        vectors[2],
        vectors[3],
        vectors[4],
        expand_share.astype(f32).T,
        expand_bias_grad.reshape(FF),
        reduce_share.astype(f32),
        vectors[5],
        vectors[6],
        vectors[7],
        inner,
        inner_bias,
        outer,
        outer_bias,
    )


def solution(mesh):
    seq, batch = mesh.devices.shape
    mesh = jax.sharding.Mesh(mesh.devices.reshape(seq, batch // 4, 2, 2), ("y", "z", "x", "c"))
    sequences, everyone = ("z", "x", "c"), ("y", "z", "x", "c")
    rows = P(sequences, "y", None, None)
    in_specs = (rows, rows) + (P(sequences),) * 3 + (P(sequences, None, None),) + (P(),) * 19
    out_specs = (rows, rows) + (P(),) * 9 + (P(None, everyone), P(), P(everyone, None)) + (P(),) * 7
    return jax.shard_map(on_device, mesh=mesh, in_specs=in_specs, out_specs=out_specs, check_vma=False)
```

```python
import functools
import math

import jax
import jax.numpy as jnp
from jax import lax
from jax.experimental import pallas as pl
from jax.experimental.pallas import tpu as pltpu
from jax.sharding import PartitionSpec as P

D = 768
HEADS = 12
HEAD_DIM = 64
FF = 3072
TDIM = 128
TFF = 512
CAP = 256
ROWS = 2 * CAP

f32 = jnp.float32
bf16 = jnp.bfloat16
highest = lax.Precision.HIGHEST
norm_epsilon = 1e-12
masked_score = -1000000000.0
root_half = 0.7071067811865476
density_scale = 0.3989422804014327


core, near, side = ("c", 0), ("x", 0), ("y", 0)


def swapped(value, stage):
    axis, bit = stage
    return lax.ppermute(value, axis, [(i, i ^ (1 << bit)) for i in range(lax.axis_size(axis))])


def own_bit(stage):
    axis, bit = stage
    return (lax.axis_index(axis) >> bit) & 1


def stage_lists():
    bits = lax.axis_size("z").bit_length() - 1
    far = [("z", k) for k in range(bits)]
    return [side] + far[::-1] + [near, core], far


def added(kept, received):
    return lax.reduce_precision(kept.astype(f32) + received.astype(f32), 8, 7).astype(bf16)


def halves(buffer, labels, stage):
    at = labels.index(stage)
    bit = own_bit(stage)
    kept = lax.dynamic_index_in_dim(buffer, bit, axis=at, keepdims=False)
    sent = lax.dynamic_index_in_dim(buffer, 1 - bit, axis=at, keepdims=False)
    return kept, sent, labels[:at] + labels[at + 1 :]


def exchange(buffer, labels, stage, riders=None):
    kept, sent, labels = halves(buffer, labels, stage)
    rows = sent.reshape(-1, D)
    if riders is None:
        return added(kept, swapped(rows, stage).reshape(kept.shape)), labels, None
    received = swapped(jnp.concatenate([rows, riders], axis=0), stage)
    return (
        added(kept, received[: rows.shape[0]].reshape(kept.shape)),
        labels,
        added(riders, received[rows.shape[0] :]),
    )


def scattered_sum(shares, riders=None):
    slow_first, far = stage_lists()
    rows = shares.shape[1]
    buffer = shares.reshape((2,) * len(slow_first) + (rows, D))
    buffer, labels, riders = exchange(buffer, slow_first, core, riders)
    cut = rows // 2
    first, first_labels, riders = exchange(buffer[..., :cut, :], labels, near, riders)
    second, second_labels, _ = exchange(buffer[..., cut:, :], labels, side)
    first, first_labels, riders = exchange(first, first_labels, side, riders)
    second, second_labels, _ = exchange(second, second_labels, near)
    buffer = jnp.concatenate([first, second], axis=-2)
    labels = first_labels
    for stage in far:
        buffer, labels, riders = exchange(buffer, labels, stage, riders)
    return buffer, riders


def gathered(share):
    slow_first, far = stage_lists()
    order = [core, near, side] + far
    buffer = share[None]
    done = []
    for stage in reversed(order):
        buffer = jnp.concatenate([buffer, swapped(buffer, stage)], axis=0)
        done.append(stage)
    bits = len(order)
    buffer = buffer.reshape((2,) * bits + share.shape)
    current = list(reversed(done))
    return jnp.transpose(buffer, [current.index(stage) for stage in slow_first] + [bits, bits + 1]).reshape(
        (1 << bits,) + share.shape
    )


def matmul(left, right):
    return jnp.dot(left, right, preferred_element_type=f32)


def column_sum(values):
    return jnp.sum(values.astype(f32), axis=0)


def dot(left, right, dims):
    return lax.dot_general(left, right, (((dims[0],), (dims[1],)), ((), ())), preferred_element_type=f32)


def nn(left, right):
    return dot(left, right, (1, 0))


def nt(left, right):
    return dot(left, right, (1, 1))


def tn(left, right):
    return dot(left, right, (0, 0))


def whole(*shape):
    return pl.BlockSpec(shape, lambda *at: (0,) * len(shape))


def vector(size):
    return pl.BlockSpec((size,), lambda *at: (0,))


def vector_tile(width):
    return pl.BlockSpec((width,), lambda j, *at: (j,))


def row(ref):
    return ref[...].reshape(1, -1)


def column_tile(rows, width):
    return pl.BlockSpec((rows, width), lambda j, *at: (0, j))


def row_tile(height, width):
    return pl.BlockSpec((height, width), lambda j, *at: (j, 0))


def run(body, grid, operands, in_specs, outs, out_specs, flops, scratch=(), scalars=(), after=(), aliases=None):
    shapes = [jax.ShapeDtypeStruct(shape, dtype) for shape, dtype in outs]
    sizes = [x.size * x.dtype.itemsize for x in list(operands) + shapes]
    used = len(scalars) + len(operands)

    def wrapped(*refs):
        body(*refs[:used], *refs[used + len(after) :])

    return pl.pallas_call(
        wrapped,
        grid_spec=pltpu.PrefetchScalarGridSpec(
            num_scalar_prefetch=len(scalars),
            grid=grid,
            in_specs=in_specs + [pl.BlockSpec(memory_space=pl.ANY)] * len(after),
            out_specs=out_specs,
            scratch_shapes=scratch,
        ),
        out_shape=shapes,
        input_output_aliases=aliases or {},
        compiler_params=pltpu.CompilerParams(vmem_limit_bytes=(63 << 20) + (960 << 10)),
        cost_estimate=pl.CostEstimate(flops=int(flops), bytes_accessed=sum(sizes), transcendentals=0),
    )(*scalars, *operands, *after)


def nothing(*refs):
    pass


def tie(values, after):
    anywhere = pl.BlockSpec(memory_space=pl.ANY)
    return pl.pallas_call(
        nothing,
        in_specs=[anywhere] * (len(values) + len(after)),
        out_specs=[anywhere] * len(values),
        out_shape=[jax.ShapeDtypeStruct(value.shape, value.dtype) for value in values],
        input_output_aliases={k: k for k in range(len(values))},
        compiler_params=pltpu.CompilerParams(vmem_limit_bytes=(63 << 20) + (960 << 10)),
    )(*values, *after)


def normalized(values):
    center = values - jnp.mean(values, axis=-1, keepdims=True)
    spread = jnp.mean(center * center, axis=-1, keepdims=True)
    inverse = lax.rsqrt(spread + norm_epsilon)
    return center * inverse, inverse


def norm_backward(upstream, normed, inverse):
    first_mean = jnp.mean(upstream, axis=-1, keepdims=True)
    second_mean = jnp.mean(upstream * normed, axis=-1, keepdims=True)
    return inverse * (upstream - first_mean - normed * second_mean)


def row_sum(values):
    return jnp.sum(values, axis=0, keepdims=True)


def prepare_body(bits, stamps, src_len, seq_len, flags, inner, inner_bias, outer, outer_bias, cotangent, *outs):
    features, inner_sum, middle, stamp, allowed, valid, masked, cot_other = outs
    cot_other[...] = cotangent[0]
    y = bits[2]
    lane = lax.broadcasted_iota(jnp.int32, (1, TDIM), 1)
    half = TDIM // 2
    frequency = jnp.exp(-math.log(10000.0) * lax.rem(lane, half).astype(f32) / half)
    angles = jnp.broadcast_to(stamps[y].astype(f32), (1, TDIM)) * frequency
    waves = jnp.where(lane < half, jnp.cos(angles), jnp.sin(angles))
    features[...] = waves
    total = jnp.dot(waves, inner[...].astype(f32), precision=highest) + row(inner_bias)
    inner_sum[...] = total
    gated = total * (1.0 / (1.0 + jnp.exp(-total)))
    middle[...] = gated
    stamp[...] = jnp.dot(gated, outer[...].astype(f32), precision=highest) + row(outer_bias)
    source, target = src_len[y], seq_len[y] - src_len[y]
    slots = lax.broadcasted_iota(jnp.int32, (CAP, 1), 0)
    lengths = jnp.where(y == 0, source, target), jnp.where(y == 0, target, source)
    for at, (length, stream) in enumerate(zip(lengths, (y, 1 - y))):
        inside = jnp.where(slots < length, 1.0, 0.0)
        kept = jnp.where(flags[y, pl.ds(stream, 1)] == 1, 1.0, 0.0)
        kept = jnp.broadcast_to(kept, (8, CAP)).T[:, :1]
        here = slice(at * CAP, (at + 1) * CAP)
        valid[here] = inside
        allowed[here] = inside * kept
        masked[here] = (1.0 - inside * kept) * masked_score


def prepare(bits, stamps, src_len, seq_len, flags, inner, inner_bias, outer, outer_bias, cotangent):
    return run(
        prepare_body,
        (1,),
        (flags, inner, inner_bias, outer, outer_bias, cotangent),
        [whole(2, 2, CAP), whole(TDIM, TFF), vector(TFF), whole(TFF, D), vector(D)]
        + [pl.BlockSpec((1, CAP, D), lambda j, bits, *at: (1 - bits[2], 0, 0))],
        [((1, size), f32) for size in (TDIM, TFF, TFF, D)] + [((ROWS, 1), f32)] * 3 + [((CAP, D), bf16)],
        [whole(1, size) for size in (TDIM, TFF, TFF, D)] + [whole(ROWS, 1)] * 3 + [whole(CAP, D)],
        0,
        scalars=(bits, stamps, src_len, seq_len),
    )


def project_body(rows, stamp, keep, qw, qb, kw, vw, vb, q, k, v, low_out):
    low = (rows[...].astype(f32) + stamp[...]).astype(bf16)
    low_out[...] = low
    q[...] = ((nn(low, qw[...]) + row(qb)).astype(bf16).astype(f32) * 0.125).astype(bf16)
    k[...] = (nn(low, kw[...]) * keep[...]).astype(bf16)
    v[...] = (nn(low, vw[...]) + row(vb)).astype(bf16)


def project(rows, half, stamp, keep, qw, qb, kw, vw, vb):
    tile = 256
    return run(
        project_body,
        (D // tile,),
        (rows, stamp, keep, qw, qb, kw, vw, vb),
        [whole(CAP, D), whole(1, D), pl.BlockSpec((CAP, 1), lambda *at: (half, 0))]
        + [column_tile(D, tile), vector_tile(tile), column_tile(D, tile), column_tile(D, tile), vector_tile(tile)],
        [((CAP, D), bf16)] * 4,
        [column_tile(CAP, tile)] * 3 + [whole(CAP, D)],
        6 * CAP * D * D,
    )


def lanes_of(shape):
    return lax.broadcasted_iota(jnp.int32, shape, 1)


def both(own, far):
    return jnp.concatenate([own[...], far[...]], axis=0)


def attend_body(qo, qf, ko, kf, vo, vf, lo, lf, masked, attended, for_core, probs):
    q, k, v = both(qo, qf), both(ko, kf), both(vo, vf)
    lane = lanes_of(q.shape)
    flag = jnp.broadcast_to(masked[...], q.shape).astype(bf16)
    v_turned = v.T
    pieces = []
    for head in range(2):
        mine = (lane // HEAD_DIM) == head
        spare = lane == (1 - head) * HEAD_DIM
        k_head = jnp.where(mine, k, jnp.where(spare, flag, 0))
        q_head = jnp.where(mine, q, jnp.where(spare, 1, 0).astype(bf16))
        scores = nt(k_head, q_head)
        top = jnp.max(scores, axis=0, keepdims=True)
        exponent = jnp.exp(scores - top)
        inverse = 1.0 / jnp.sum(exponent, axis=0, keepdims=True)
        low = (exponent * inverse).astype(bf16)
        probs[head] = low
        pieces.append(nn(v_turned[head * HEAD_DIM : (head + 1) * HEAD_DIM], low))
    low = jnp.concatenate(pieces, axis=0).T.astype(bf16)
    attended[...] = low
    for_core[0], for_core[1] = both(lo, lf), low


def attend(q, k, v, low, masked):
    pair = 2 * HEAD_DIM
    return run(
        attend_body,
        (D // pair,),
        (*q, *k, *v, *low, masked),
        [column_tile(CAP, pair)] * 8 + [whole(ROWS, 1)],
        [((ROWS, D), bf16), ((2, ROWS, D), bf16), ((HEADS, ROWS, ROWS), bf16)],
        [column_tile(ROWS, pair), pl.BlockSpec((2, ROWS, pair), lambda j: (0, 0, j))]
        + [pl.BlockSpec((2, ROWS, ROWS), lambda j: (j, 0, 0))],
        4 * HEADS * ROWS * ROWS * 256,
    )


SHARE = 96
COLOUR = 48


half_tile = pl.BlockSpec((ROWS, D // 2), lambda j, *at: (0, j))


FOR_CORE = (ROWS, FF + 2 * D)


def by_core(values):
    return [
        jnp.concatenate([values[:, at : at + SHARE] for at in range(start, D, 2 * SHARE)], axis=1) for start in (0, SHARE)
    ]


SUB = 256


def feed_forward_body(
    bits, attended, own, far, stamp, ow, ob, gain, shift, ew, eb, rw, rb, gain2, shift2, valid, cot_own, cot_far,
    output, far_output, for_core, activated_own, expanded_own, mixed_low, d_reduced, bias_grad, d_first, d_branch, sums,
    total, normed, inverse, slope, columns,
):
    step = pl.program_id(0)
    tiles = FF // D

    def store(own_out, offset):
        zero, one = by_core(columns[...])
        here = pl.ds(pl.multiple_of(offset, D // 2), D // 2)

        @pl.when(bits[0] == 0)
        def _():
            own_out[...], for_core[:, here] = zero, one

        @pl.when(bits[0] == 1)
        def _():
            own_out[...], for_core[:, here] = one, zero

    @pl.when(step == 0)
    def _():
        hidden = both(own, far).astype(f32) + stamp[...]
        n1, inv = normalized(hidden + nn(attended[...], ow[...]) + row(ob))
        value = n1 * row(gain) + row(shift)
        normed[...] = n1
        inverse[...] = inv
        mixed_low[...] = value.astype(bf16)
        total[...] = value + row(rb)

    @pl.when(step < tiles)
    def _():
        added_up = None
        bias = eb[pl.ds(pl.multiple_of(step * D, D), D)].reshape(1, -1)
        for part in range(D // SUB):
            cut = slice(part * SUB, (part + 1) * SUB)
            expanded = nn(mixed_low[...], ew[:, cut]) + bias[:, cut]
            chance = 0.5 * (1.0 + lax.erf(expanded * root_half))
            slope[step, :, cut] = chance + expanded * jnp.exp(-0.5 * expanded * expanded) * density_scale
            low = (expanded * chance).astype(bf16)
            columns[:, cut] = low
            product = nn(low, rw[cut, :])
            added_up = product if added_up is None else added_up + product
        total[...] += added_up
        store(activated_own, step % 2 * (D // 2))

    @pl.when(step == tiles - 1)
    def _():
        n2, inv = normalized(total[...])
        weight = valid[...]
        rows = ((n2 * row(gain2) + row(shift2)) * weight).astype(bf16)
        output[...], far_output[...] = rows[:CAP], rows[CAP:]
        d_out = jnp.concatenate([cot_own[0], cot_far[...]], axis=0).astype(f32) * weight
        back = norm_backward(d_out * row(gain2), n2, inv)
        low = back.astype(bf16)
        total[...] = back
        d_reduced[...] = low
        sums[...] = jnp.concatenate(
            [jnp.zeros((5, D), f32), row_sum(low.astype(f32)), row_sum(d_out * n2), row_sum(d_out)], axis=0
        )

    @pl.when(step >= tiles)
    def _():
        d_expanded = (nt(d_reduced[...], rw[...]) * slope[step - tiles]).astype(bf16)
        columns[...] = d_expanded
        bias_grad[0] = row_sum(d_expanded.astype(f32))
        total[...] += nt(d_expanded, ew[...])
        store(expanded_own, 0)
        for at in range(tiles):

            @pl.when(step == tiles + at)
            def _():
                source = d_reduced if at < 2 else mixed_low
                for_core[:, D // 2 :] = source[:, at % 2 * (D // 2) : (at % 2 + 1) * (D // 2)]

    @pl.when(step == 2 * tiles - 1)
    def _():
        d_mixed = total[...]
        n1 = normed[...]
        back = norm_backward(d_mixed * row(gain), n1, inverse[...])
        low = back.astype(bf16)
        d_first[...] = back
        d_branch[...] = low
        sums[2:5] = jnp.concatenate([row_sum(low.astype(f32)), row_sum(d_mixed * n1), row_sum(d_mixed)], axis=0)


def feed_forward(
    bits, attended, own, far, stamp, ow, ob, gain, shift, ew, eb, rw, rb, gain2, shift2, valid, cot_own, cot_far
):
    tiles = FF // D
    line, square, half = vector(D), whole(ROWS, D), whole(CAP, D)
    forward = pl.BlockSpec((ROWS, D // 2), lambda j, *at: (0, jnp.minimum(j, tiles - 1)))
    backward = pl.BlockSpec((ROWS, D // 2), lambda j, *at: (0, jnp.maximum(j - tiles, 0)))
    return run(
        feed_forward_body,
        (2 * tiles,),
        (attended, own, far, stamp, ow, ob, gain, shift, ew, eb, rw, rb, gain2, shift2, valid, cot_own, cot_far),
        [square, half, half, whole(1, D), whole(D, D), line, line, line]
        + [pl.BlockSpec((D, D), lambda j, *at: (0, j % tiles)), vector(FF), pl.BlockSpec((D, D), lambda j, *at: (j % tiles, 0))]
        + [line, line, line, whole(ROWS, 1), pl.BlockSpec((1, CAP, D), lambda j, bits: (bits[2], 0, 0)), half],
        [((CAP, D), bf16)] * 2
        + [(FOR_CORE, bf16), ((ROWS, FF // 2), bf16), ((ROWS, FF // 2), bf16), ((ROWS, D), bf16)]
        + [((ROWS, D), bf16), ((tiles, 1, D), f32), ((ROWS, D), f32), ((ROWS, D), bf16), ((8, D), f32)],
        [half, half, pl.BlockSpec((ROWS, D), lambda j, *at: (0, jnp.where(j < tiles, j // 2, j - tiles // 2)))]
        + [forward, backward, square, square]
        + [pl.BlockSpec((1, 1, D), lambda j, *at: (jnp.maximum(j - tiles, 0), 0, 0)), square, square, whole(8, D)],
        2 * ROWS * D * (D + 4 * FF),
        scratch=[pltpu.VMEM((ROWS, D), f32)] * 2
        + [pltpu.VMEM((ROWS, 1), f32), pltpu.VMEM((tiles, ROWS, D), f32), pltpu.VMEM((ROWS, D), bf16)],
        scalars=(bits,),
    )


def hidden_grad_body(bits, activated, d_reduced, d_expanded, mixed, activated_got, *refs):
    halves, (kept, sent) = refs[:6], refs[6:]
    reduced_got, mixed_got, expanded_got = [lambda at=at: jnp.concatenate([halves[at][...], halves[at + 1][...]], axis=1) for at in (0, 2, 4)]
    step = pl.program_id(0)
    tile = step % 2

    def store(kind, grad):
        low = grad.astype(bf16)
        for at in range(8):
            x, z = at % 2, at // 2
            here = jnp.where(bits[0] == 0, tile * 4 + (z % 2 * 2 + z // 2), x * 4 + z)
            block = low[at * SHARE : (at + 1) * SHARE]
            mine = jnp.where(bits[0] == 0, x, tile) == bits[5]

            @pl.when(mine)
            def _():
                kept[here, kind] = block

            @pl.when(jnp.logical_not(mine))
            def _():
                sent[here, kind] = block

    @pl.when(step < 2)
    def _():
        store(0, tn(activated[...], d_reduced[...]) + tn(activated_got[...], reduced_got()))

    @pl.when(step >= 2)
    def _():
        store(1, tn(d_expanded[...], mixed[...]) + tn(expanded_got(), mixed_got()))


def hidden_grad(bits, activated, d_reduced, d_expanded, mixed, got, after):
    first = lambda start: pl.BlockSpec((ROWS, D), lambda j, bits: (0, start + jnp.minimum(j, 1)))
    second = lambda start: pl.BlockSpec((ROWS, D), lambda j, bits: (0, start + jnp.maximum(j - 2, 0)))
    square = lambda at: pl.BlockSpec((ROWS, D), lambda j, bits: (0, at))
    unit = lambda at: pl.BlockSpec((ROWS, D // 2), lambda j, bits: (0, at))
    turn = lambda start: pl.BlockSpec((ROWS, D // 2), lambda j, bits: (0, start + 4 * jnp.maximum(j - 2, 0)))
    return run(
        hidden_grad_body,
        (4,),
        (activated, d_reduced, d_expanded, mixed) + (got,) * 7,
        [first(0), square(0), second(0), square(0), first(0)] + [unit(at) for at in (5, 7, 9, 11)] + [turn(4), turn(6)],
        [((8, 2, SHARE, D), bf16)] * 2,
        [whole(8, 2, SHARE, D)] * 2,
        4 * ROWS * D * FF,
        scalars=(bits,),
        after=after,
    )


def attend_back_body(bits, d_branch, branch, ow, probs, qo, qf, ko, kf, vo, vf, keep, grads, kept, sent, sums):
    q, k, v = both(qo, qf), both(ko, kf), both(vo, vf)
    lane = lanes_of(q.shape)
    low_half = lane < HEAD_DIM
    upstream = nt(d_branch[...], ow[...]).astype(bf16)
    k_turned = k.T
    d_q, d_k, d_v = [], [], []
    for head in range(2):
        rows = slice(head * HEAD_DIM, (head + 1) * HEAD_DIM)
        mine = low_half if head == 0 else jnp.logical_not(low_half)
        low = probs[head]
        wide = low.astype(f32)
        weighted = wide * nt(jnp.where(mine, v, 0), upstream)
        d_scores = (weighted - wide * row_sum(weighted)).astype(bf16)
        d_v.append(nn(low, upstream))
        d_k.append(nn(d_scores, q))
        d_q.append(nn(k_turned[rows], d_scores))
    q_low = (jnp.concatenate(d_q, axis=0).T * 0.125).astype(bf16)
    v_low = jnp.where(low_half, d_v[0], d_v[1]).astype(bf16)
    k_low = (jnp.where(low_half, d_k[0], d_k[1]) * keep[...]).astype(bf16)
    grads[0], grads[1], grads[2] = q_low, k_low, v_low

    def share(first, second):
        first[0], first[1] = q_low, k_low
        second[0], second[1] = v_low, branch[...]

    @pl.when(bits[0] == 0)
    def _():
        share(kept, sent)

    @pl.when(bits[0] == 1)
    def _():
        share(sent, kept)

    sums[...] = jnp.concatenate(
        [row_sum(q_low.astype(f32)), row_sum(v_low.astype(f32)), jnp.zeros((6, q.shape[1]), f32)], axis=0
    )


def attend_back(bits, d_branch, ow, probs, q, k, v, keep, after):
    pair = 2 * HEAD_DIM
    return run(
        attend_back_body,
        (D // pair,),
        (d_branch, d_branch, ow, probs, *q, *k, *v, keep),
        [whole(ROWS, D), column_tile(ROWS, pair), row_tile(pair, D), pl.BlockSpec((2, ROWS, ROWS), lambda j, *at: (j, 0, 0))]
        + [column_tile(CAP, pair)] * 6
        + [whole(ROWS, 1)],
        [((count, ROWS, D), bf16) for count in (3, 2, 2)] + [((8, D), f32)],
        [pl.BlockSpec((count, ROWS, pair), lambda j, *at: (0, 0, j)) for count in (3, 2, 2)] + [column_tile(8, pair)],
        10 * HEADS * ROWS * ROWS * 256,
        scalars=(bits,),
        after=after,
    )


def pair_grad_body(bits, left, right, left_got, right_got, kept, sent):
    low = (tn(left[0], right[0]) + tn(left_got[0], right_got[0])).astype(bf16)
    zero, one = [low[at * D // 2 : (at + 1) * D // 2].reshape(8, COLOUR, D) for at in range(2)]
    kept[:, 0] = jnp.where(bits[5] == 0, zero, one)
    sent[:, 0] = jnp.where(bits[5] == 0, one, zero)


def pair_grad(bits, left, right, left_got, right_got, after):
    lefts = pl.BlockSpec((1, ROWS, D), lambda j, bits: (j * bits[0], 0, 0))
    rights = pl.BlockSpec((1, ROWS, D), lambda j, bits: (j, 0, 0))
    return run(
        pair_grad_body,
        (2,),
        (left, right, left_got, right_got),
        [lefts, rights] * 2,
        [((8, 2, COLOUR, D), bf16)] * 2,
        [pl.BlockSpec((8, 1, COLOUR, D), lambda j, *at: (0, j, 0, 0))] * 2,
        8 * ROWS * D * D,
        scalars=(bits,),
        after=after,
    )


def input_grad_body(grads, qw, kw, vw, d_first, own_rows, far_rows, d_time):
    total = d_first[...] + nt(grads[0], qw[...]) + nt(grads[1], kw[...]) + nt(grads[2], vw[...])
    low = total.astype(bf16)
    own_rows[...], far_rows[...] = low[:CAP], low[CAP:]
    d_time[...] = row_sum(total)


def input_grad(grads, qw, kw, vw, d_first, after):
    tile = 256
    return run(
        input_grad_body,
        (D // tile,),
        (grads, qw, kw, vw, d_first),
        [whole(3, ROWS, D)] + [row_tile(tile, D)] * 3 + [column_tile(ROWS, tile)],
        [((CAP, D), bf16)] * 2 + [((1, D), f32)],
        [column_tile(CAP, tile)] * 2 + [column_tile(1, tile)],
        6 * ROWS * D * D,
        after=after,
    )


everywhere = ("y", "z", "x", "c")


def crossed(value, first):
    sizes = [lax.axis_size(axis) for axis in everywhere]
    pairs = []
    for at in range(math.prod(sizes)):
        c, x = at % 2, at // 2 % 2
        along_x = (c == 0) == first
        step = 2 * (1 - 2 * x) if along_x else (math.prod(sizes) // 2) * (1 - 2 * (at // (math.prod(sizes) // 2)))
        pairs.append((at, at + step))
    return lax.ppermute(value, everywhere, pairs)


def lined(value, first):
    sizes = [lax.axis_size(axis) for axis in everywhere]
    turn = lambda c: 1 if (c == 0) == first else 2
    pairs = [(at, at ^ (turn(at % 2) * 4)) for at in range(math.prod(sizes))]
    return lax.ppermute(value, everywhere, pairs)


def plus(left, right):
    return (left.astype(f32) + right.astype(f32)).astype(bf16)


def halved(own, got, bit):
    own, got = [value.reshape((2, -1) + value.shape[1:]) for value in (own, got)]
    at = lambda place: [lax.dynamic_index_in_dim(value, place, 0, keepdims=False) for value in (own, got)]
    return plus(*at(bit)), plus(*at(1 - bit))


BLOCK = 32


def block_body(bits, first, second, bias, d_time, inner_sum, middle, features, outer, out):
    riders = first[...] + second[...]
    total = inner_sum[...]
    gate = 1.0 / (1.0 + jnp.exp(-total))
    d_middle = lax.dot_general(
        d_time[...], outer[...].astype(f32), (((1,), (1,)), ((), ())), precision=highest, preferred_element_type=f32
    )
    d_inner = d_middle * (gate * (1.0 + total * (1.0 - gate)))
    wide = D - TFF
    rows = [jnp.concatenate([d_time[:, at * wide : (at + 1) * wide], middle[...]], axis=1) for at in range(3)]
    rows.append(jnp.concatenate([d_inner, features[...], jnp.zeros((1, wide - TDIM), f32)], axis=1))
    index = lax.broadcasted_iota(jnp.int32, (16, D), 0)
    factors = jnp.zeros((16, D), f32)
    for at, values in enumerate(rows):
        factors = jnp.where(index == 4 * (bits[3] + 2 * bits[4]) + at, values, factors)
    biases = jnp.zeros((8, D), f32)
    index = lax.broadcasted_iota(jnp.int32, (8, D), 0)
    for at in range(4):
        biases = jnp.where(index == at, bias[at], biases)
    out[...] = jnp.concatenate([riders, biases, factors], axis=0).astype(bf16)


def block_rows(bits, *operands):
    return run(
        block_body,
        (1,),
        operands,
        [whole(*operand.shape) for operand in operands],
        [((BLOCK, D), bf16)],
        [whole(BLOCK, D)],
        0,
        scalars=(bits,),
    )[0]


def sum_rows(own, got):
    return lax.reduce_precision(own.astype(f32) + got.astype(f32), 8, 7).astype(bf16)


def longer(data, block, send):
    got = send(jnp.concatenate([data, block]))
    size = data.shape[0]
    return jnp.concatenate([data, got[:size]]), sum_rows(block, got[size:])


def unpack_body(bits, pieces, outs):
    for turn in range(2):

        @pl.when(pl.program_id(0) == turn)
        def _():
            own, got = pieces[turn], pieces[2 + turn]
            for at in range(4):
                here, there = (bits[6] % 4) ^ at, (bits[7] % 4) ^ at
                for matrix in range(2):
                    rows = slice(at * SHARE + matrix * COLOUR, at * SHARE + (matrix + 1) * COLOUR)
                    mine, other = own[rows].astype(f32), got[rows].astype(f32)
                    outs[matrix][here] = jnp.where(bits[0] == 0, mine, other)
                    outs[2 + matrix][there] = jnp.where(bits[0] == 0, other, mine)


def unpack_specs(turn):
    part = whole(4 * SHARE, D)
    spots = [
        pl.BlockSpec((4, COLOUR, D), lambda j, bits, at=at: ((bits[at] // 4) ^ (2 * turn + j), 0, 0)) for at in (6, 6, 7, 7)
    ]
    return part, spots


matrix_shapes = [((16, COLOUR, D), f32)] * 4


def first_unpack(bits, pieces):
    part, spots = unpack_specs(0)
    body = lambda bits, *refs: unpack_body(bits, refs[:4], refs[4:])
    return run(body, (2,), pieces, [part] * 4, matrix_shapes, spots, 0, scalars=(bits,))


def finish_body(bits, *refs):
    unpack_body(bits, refs[:4], refs[16:20])

    @pl.when(pl.program_id(0) == 1)
    def _():
        vectors_body(refs[4:12], *refs[20:])


def vectors_body(refs, *outs):
    blocks = [ref[...].astype(f32) for ref in refs]
    riders = [block[:16] for block in blocks]
    pairs = [riders[at] + riders[at + 1] for at in range(0, 8, 2)]
    sums = (pairs[0] + pairs[1]) + (pairs[2] + pairs[3])
    for at in range(8):
        outs[at][...] = sums[at]
    for at in range(4):
        outs[8][at] = sums[8 + at : 9 + at]
    factors = jnp.concatenate([block[16:] for block in blocks], axis=0)
    index = lax.broadcasted_iota(jnp.int32, factors.shape, 0) % 4
    wide = D - TFF
    inner, inner_bias, outer, outer_bias = outs[9:]
    for at in range(3):
        rows = jnp.where(index == at, factors, 0.0)
        d_time = rows[:, :wide]
        here = slice(at * wide, (at + 1) * wide)
        outer[:, here] = tn(rows[:, wide:].astype(bf16), d_time.astype(bf16))
        outer_bias[here] = jnp.sum(d_time, axis=0)
    rows = jnp.where(index == 3, factors, 0.0)
    d_inner = rows[:, :TFF]
    inner[...] = tn(rows[:, TFF : TFF + TDIM].astype(bf16), d_inner.astype(bf16))
    inner_bias[...] = jnp.sum(d_inner, axis=0)


def finish(bits, turned, turned_far, pieces, pieces_far, outs):
    part, spots = unpack_specs(1)
    last = pl.BlockSpec((BLOCK, D), lambda j, *at: (4 * SHARE // BLOCK, 0))
    shapes = [(D,)] * 8 + [(4, 1, D), (TDIM, TFF), (TFF,), (TFF, D), (D,)]
    return run(
        finish_body,
        (2,),
        (*turned, *turned_far, *pieces, *turned, *pieces_far, *turned_far, *outs),
        [part] * 4 + [last] * 8 + [pl.BlockSpec(memory_space=pl.ANY)] * 4,
        matrix_shapes + [(shape, f32) for shape in shapes],
        spots + [whole(*shape) for shape in shapes],
        0,
        scalars=(bits,),
        aliases={13 + k: k for k in range(4)},
    )


def plain_rows(first_class, second_class):
    zero = jnp.concatenate(first_class).reshape(2, 2, 2, 2, SHARE, D)
    one = jnp.concatenate(second_class).reshape(2, 2, 2, 2, SHARE, D)
    classes = jnp.stack([jnp.transpose(zero, (1, 3, 2, 0, 4, 5)), jnp.transpose(one, (0, 2, 3, 1, 4, 5))], axis=4)
    return classes.reshape(FF, D)


def everyones(sums, bias, d_time, inner_sum, middle, features, outer):
    gate = jax.nn.sigmoid(inner_sum)
    d_inner = jnp.dot(d_time, outer.astype(f32).T, precision=highest) * (gate * (1.0 + inner_sum * (1.0 - gate)))
    riders = jnp.concatenate([sums, bias.reshape(4, D), jnp.zeros((4, D), f32)])
    factors = jnp.concatenate([d_time, d_inner, middle, features], axis=1)
    for stage in stage_lists()[0]:
        riders = riders + swapped(riders, stage)
        factors = jnp.concatenate([factors, swapped(factors, stage)])
    cuts = (0, D, D + TFF, D + 2 * TFF, D + 2 * TFF + TDIM)
    d_time, d_inner, middle, features = [factors[:, a:b] for a, b in zip(cuts, cuts[1:])]
    inner, outer = matmul(features.T, d_inner), matmul(middle.T, d_time)
    return list(riders[:8]), riders[8:12], inner, column_sum(d_inner), outer, column_sum(d_time)


def on_device(
    layer_input,
    cotangent,
    timesteps,
    src_len,
    seq_len,
    key_keep,
    query_weight,
    query_bias,
    key_weight,
    value_weight,
    value_bias,
    output_weight,
    output_bias,
    first_gain,
    first_shift,
    expand_weight,
    expand_bias,
    reduce_weight,
    reduce_bias,
    second_gain,
    second_shift,
    time_inner,
    time_inner_bias,
    time_outer,
    time_outer_bias,
):
    stream = lax.axis_index("y")
    sizes = [lax.axis_size(axis) for axis in ("y", "z", "x", "c")]
    devices = math.prod(sizes)
    tuned = sizes == [2, 4, 2, 2]
    c, x, z = lax.axis_index("c") if tuned else 0, lax.axis_index("x"), lax.axis_index("z")
    first, second = jnp.where(c == 0, x, stream), jnp.where(c == 0, stream, x)
    wanted = first if tuned else 0
    near_z, across_z = z & 1, z >> 1
    third, fourth = jnp.where(c == 0, near_z, across_z), jnp.where(c == 0, across_z, near_z)
    places = [x * 8 + stream * 4 + near_z * 2 + across_z, stream * 8 + x * 4 + across_z * 2 + near_z]
    bits = jnp.stack([c, x, stream, z & 1, z >> 1, wanted, *places]).astype(jnp.int32)

    def whole_sequence(rows):
        own = lax.dynamic_index_in_dim(rows[:, 0], stream, axis=0, keepdims=False)
        other = lax.dynamic_index_in_dim(rows[:, 0], 1 - stream, axis=0, keepdims=False)
        return own, other

    def both_sequences(rows, far):
        own = rows
        return jnp.where(stream == 0, jnp.stack([own, far]), jnp.stack([far, own]))[:, None]

    own, other = whole_sequence(layer_input)
    far = swapped(other, side)
    cotangent = cotangent[:, 0]
    features, inner_sum, middle, stamp, allowed, valid, masked, cot_other = prepare(
        bits, timesteps, src_len, seq_len, key_keep, time_inner, time_inner_bias, time_outer, time_outer_bias, cotangent
    )
    weights = (query_weight, query_bias, key_weight, value_weight, value_bias)
    *first_rows, own_low = project(own, 0, stamp, allowed, *weights)
    (far,) = tie([far], first_rows[:1])
    cot_other, far = lax.optimization_barrier((cot_other, far))
    cot_far = swapped(cot_other, side)
    *other_rows, far_low = project(far, 1, stamp, allowed, *weights)
    q, k, v = zip(first_rows, other_rows)
    low = (own_low, far_low)
    attended, lefts, probs = attend(q, k, v, low, masked)
    (lefts,) = tie([lefts], [cot_far])
    output, far_output, for_core, activated, d_expanded, mixed_low, d_reduced, *others = feed_forward(
        bits,
        attended,
        own,
        far,
        stamp,
        output_weight,
        output_bias,
        first_gain,
        first_shift,
        expand_weight,
        expand_bias,
        reduce_weight,
        reduce_bias,
        second_gain,
        second_shift,
        valid,
        cotangent,
        cot_far,
    )
    expand_bias_grad, d_first, d_branch, layer_sums = others
    lefts_got = swapped(lefts, core)
    (far_output,) = tie([far_output], [lefts_got])
    output_got = swapped(far_output, side)
    grads, kept, sent, attend_sums = attend_back(bits, d_branch, output_weight, probs, q, k, v, allowed, [far_output])
    block_parts = (inner_sum, middle, features, time_outer)
    if tuned:
        (sent,) = tie([sent], [output_got])
        sent_got = swapped(sent, core)
        (for_core,) = tie([for_core], [sent_got])
        hidden_got = swapped(for_core, core)
        small, small_sent = pair_grad(bits, lefts, kept, lefts_got, sent_got, [for_core])
        (small_sent,) = tie([small_sent], [hidden_got])
        small_got = crossed(small_sent, True)
        hidden, hidden_sent = hidden_grad(bits, activated, d_reduced, d_expanded, mixed_low, hidden_got, [small_sent])
        (small_got,) = tie([small_got], [hidden])
        hidden_got = crossed(hidden_sent, True)
        small_sent = halved(small, small_got, second)[1]
        (small_got,) = tie([small_got], [small_sent])
        small = halved(small, small_got, second)[0]
        small_got = crossed(small_sent, False)
        d_rows, far_grad, d_time = input_grad(grads, query_weight, key_weight, value_weight, d_first, [small_sent])
        block = block_rows(bits, attend_sums, layer_sums, expand_bias_grad, d_time, *block_parts)
        (small_got,) = tie([small_got], [block])
        small, small_sent = halved(small, small_got, third)
        small_got = lined(small_sent, True)
        (far_grad,) = tie([far_grad], [small_sent])
        input_got = swapped(far_grad, side)
        small, small_sent = halved(small, small_got, fourth)
        small_got = lined(small_sent, False)
        hidden_got, input_got = tie([hidden_got, input_got], [small_sent])
        hidden, hidden_sent = halved(hidden, hidden_got, second)
        hidden_got = crossed(hidden_sent, False)
        (small_got,) = tie([small_got], [hidden_sent])
        share = plus(small, small_got).reshape(SHARE, D)
        data, block = longer(share, block, lambda value: lined(value, False))
        (hidden_got,) = tie([hidden_got], [data])
        hidden, hidden_sent = halved(hidden, hidden_got, third)
        hidden_got = lined(hidden_sent, True)
        wait = lambda value: tie([value], [hidden_sent])[0]
        data, block = longer(data, block, lambda value: wait(lined(value, True)))
        piece = jnp.concatenate([data, block])
        cross_got = crossed(piece, False)
        turned = crossed(piece, True)
        hidden, hidden_sent = halved(hidden, hidden_got, fourth)
        hidden_got = lined(hidden_sent, False)
        (cross_got,) = tie([cross_got], [hidden_sent, turned])
        pieces, turned = (piece, cross_got), (turned, crossed(cross_got, True))
        pieces_far = [swapped(value, core) for value in pieces]
        output, output_got, d_rows, input_got = tie([output, output_got, d_rows, input_got], [cross_got])
        outs = first_unpack(bits, (*pieces, *pieces_far))
        output, input_grad_rows = both_sequences(output, output_got), both_sequences(d_rows, input_got)
        turned = tie(turned, [outs[0], output, input_grad_rows])
        turned_far = [swapped(value, core) for value in turned]
        (hidden_got,) = tie([hidden_got], turned)
        shares = (hidden.astype(f32) + hidden_got.astype(f32))[0]
        reduce_share, expand_share = shares[0], shares[1]
        *matrices, expand_bias_grad, inner, inner_bias, outer, outer_bias = finish(
            bits, turned, turned_far, pieces, pieces_far, outs
        )
        grad_query, grad_key, grad_value, grad_output = [out.reshape(D, D) for out in matrices[:4]]
        vectors = matrices[4:]
    else:
        d_rows, far_grad, d_time = input_grad(grads, query_weight, key_weight, value_weight, d_first, ())
        reduce_parts, expand_parts, pairs = [], [], []
        nothing_got = jnp.zeros_like(for_core)
        expanded_other = jnp.concatenate([for_core[:, at * D // 2 : (at + 1) * D // 2] for at in (4, 6, 8, 10)], axis=1)
        for core_bit, pair, left, right in (
            (0, kept, activated, d_expanded),
            (1, sent, for_core[:, : 2 * D], expanded_other),
        ):
            as_core = bits.at[0].set(core_bit)
            hidden = hidden_grad(as_core, left, d_reduced, right, mixed_low, nothing_got, ())
            reduce_parts.append([part[:, 0] for part in hidden])
            expand_parts.append([part[:, 1] for part in hidden])
            grad = pair_grad(as_core, lefts, pair, lefts, jnp.zeros_like(pair), ())
            pairs.append(jnp.moveaxis(jnp.concatenate(grad), 1, 0).reshape(2, D, D))
        per = FF // devices
        reduce_share, _ = scattered_sum(plain_rows(*reduce_parts).reshape(devices, per, D))
        expand_share, _ = scattered_sum(plain_rows(*expand_parts).reshape(devices, per, D))
        small_share, _ = scattered_sum(jnp.concatenate(pairs).reshape(devices, per, D))
        me = ((stream * sizes[1] + z) * 2 + x) * 2 + lax.axis_index("c")
        small = gathered(small_share)[jnp.arange(devices) ^ me].astype(f32).reshape(4, D, D)
        grad_query, grad_key, grad_value, grad_output = [small[at] for at in range(4)]
        vectors, expand_bias_grad, inner, inner_bias, outer, outer_bias = everyones(
            attend_sums + layer_sums, expand_bias_grad, d_time, *block_parts
        )
        input_grad_rows = both_sequences(d_rows, swapped(far_grad, side))
        output = both_sequences(output, output_got)
    return (
        output,
        input_grad_rows,
        grad_query,
        vectors[0],
        grad_key,
        grad_value,
        vectors[1],
        grad_output,
        vectors[2],
        vectors[3],
        vectors[4],
        expand_share.astype(f32).T,
        expand_bias_grad.reshape(FF),
        reduce_share.astype(f32),
        vectors[5],
        vectors[6],
        vectors[7],
        inner,
        inner_bias,
        outer,
        outer_bias,
    )


def solution(mesh):
    seq, batch = mesh.devices.shape
    mesh = jax.sharding.Mesh(mesh.devices.reshape(seq, batch // 4, 2, 2), ("y", "z", "x", "c"))
    sequences, everyone = ("z", "x", "c"), ("y", "z", "x", "c")
    rows = P(sequences, "y", None, None)
    in_specs = (rows, rows) + (P(sequences),) * 3 + (P(sequences, None, None),) + (P(),) * 19
    out_specs = (rows, rows) + (P(),) * 9 + (P(None, everyone), P(), P(everyone, None)) + (P(),) * 7
    return jax.shard_map(on_device, mesh=mesh, in_specs=in_specs, out_specs=out_specs, check_vma=False)
```

```python
import functools
import math

import jax
import jax.numpy as jnp
from jax import lax
from jax.experimental import pallas as pl
from jax.experimental.pallas import tpu as pltpu
from jax.sharding import PartitionSpec as P

D = 768
HEADS = 12
HEAD_DIM = 64
FF = 3072
TDIM = 128
TFF = 512
CAP = 256
ROWS = 2 * CAP

f32 = jnp.float32
bf16 = jnp.bfloat16
highest = lax.Precision.HIGHEST
norm_epsilon = 1e-12
masked_score = -1000000000.0
root_half = 0.7071067811865476
density_scale = 0.3989422804014327


core, near, side = ("c", 0), ("x", 0), ("y", 0)


def swapped(value, stage):
    axis, bit = stage
    return lax.ppermute(value, axis, [(i, i ^ (1 << bit)) for i in range(lax.axis_size(axis))])


def own_bit(stage):
    axis, bit = stage
    return (lax.axis_index(axis) >> bit) & 1


def stage_lists():
    bits = lax.axis_size("z").bit_length() - 1
    far = [("z", k) for k in range(bits)]
    return [side] + far[::-1] + [near, core], far


def added(kept, received):
    return lax.reduce_precision(kept.astype(f32) + received.astype(f32), 8, 7).astype(bf16)


def halves(buffer, labels, stage):
    at = labels.index(stage)
    bit = own_bit(stage)
    kept = lax.dynamic_index_in_dim(buffer, bit, axis=at, keepdims=False)
    sent = lax.dynamic_index_in_dim(buffer, 1 - bit, axis=at, keepdims=False)
    return kept, sent, labels[:at] + labels[at + 1 :]


def exchange(buffer, labels, stage, riders=None):
    kept, sent, labels = halves(buffer, labels, stage)
    rows = sent.reshape(-1, D)
    if riders is None:
        return added(kept, swapped(rows, stage).reshape(kept.shape)), labels, None
    received = swapped(jnp.concatenate([rows, riders], axis=0), stage)
    return (
        added(kept, received[: rows.shape[0]].reshape(kept.shape)),
        labels,
        added(riders, received[rows.shape[0] :]),
    )


def scattered_sum(shares, riders=None):
    slow_first, far = stage_lists()
    rows = shares.shape[1]
    buffer = shares.reshape((2,) * len(slow_first) + (rows, D))
    buffer, labels, riders = exchange(buffer, slow_first, core, riders)
    cut = rows // 2
    first, first_labels, riders = exchange(buffer[..., :cut, :], labels, near, riders)
    second, second_labels, _ = exchange(buffer[..., cut:, :], labels, side)
    first, first_labels, riders = exchange(first, first_labels, side, riders)
    second, second_labels, _ = exchange(second, second_labels, near)
    buffer = jnp.concatenate([first, second], axis=-2)
    labels = first_labels
    for stage in far:
        buffer, labels, riders = exchange(buffer, labels, stage, riders)
    return buffer, riders


def gathered(share):
    slow_first, far = stage_lists()
    order = [core, near, side] + far
    buffer = share[None]
    done = []
    for stage in reversed(order):
        buffer = jnp.concatenate([buffer, swapped(buffer, stage)], axis=0)
        done.append(stage)
    bits = len(order)
    buffer = buffer.reshape((2,) * bits + share.shape)
    current = list(reversed(done))
    return jnp.transpose(buffer, [current.index(stage) for stage in slow_first] + [bits, bits + 1]).reshape(
        (1 << bits,) + share.shape
    )


def matmul(left, right):
    return jnp.dot(left, right, preferred_element_type=f32)


def column_sum(values):
    return jnp.sum(values.astype(f32), axis=0)


def dot(left, right, dims):
    return lax.dot_general(left, right, (((dims[0],), (dims[1],)), ((), ())), preferred_element_type=f32)


def nn(left, right):
    return dot(left, right, (1, 0))


def nt(left, right):
    return dot(left, right, (1, 1))


def tn(left, right):
    return dot(left, right, (0, 0))


def whole(*shape):
    return pl.BlockSpec(shape, lambda *at: (0,) * len(shape))


def vector(size):
    return pl.BlockSpec((size,), lambda *at: (0,))


def vector_tile(width):
    return pl.BlockSpec((width,), lambda j, *at: (j,))


def row(ref):
    return ref[...].reshape(1, -1)


def column_tile(rows, width):
    return pl.BlockSpec((rows, width), lambda j, *at: (0, j))


def row_tile(height, width):
    return pl.BlockSpec((height, width), lambda j, *at: (j, 0))


def run(body, grid, operands, in_specs, outs, out_specs, flops, scratch=(), scalars=(), after=(), aliases=None):
    shapes = [jax.ShapeDtypeStruct(shape, dtype) for shape, dtype in outs]
    sizes = [x.size * x.dtype.itemsize for x in list(operands) + shapes]
    used = len(scalars) + len(operands)

    def wrapped(*refs):
        body(*refs[:used], *refs[used + len(after) :])

    return pl.pallas_call(
        wrapped,
        grid_spec=pltpu.PrefetchScalarGridSpec(
            num_scalar_prefetch=len(scalars),
            grid=grid,
            in_specs=in_specs + [pl.BlockSpec(memory_space=pl.ANY)] * len(after),
            out_specs=out_specs,
            scratch_shapes=scratch,
        ),
        out_shape=shapes,
        input_output_aliases=aliases or {},
        compiler_params=pltpu.CompilerParams(vmem_limit_bytes=(63 << 20) + (960 << 10)),
        cost_estimate=pl.CostEstimate(flops=int(flops), bytes_accessed=sum(sizes), transcendentals=0),
    )(*scalars, *operands, *after)


def nothing(*refs):
    pass


def tie(values, after):
    anywhere = pl.BlockSpec(memory_space=pl.ANY)
    return pl.pallas_call(
        nothing,
        in_specs=[anywhere] * (len(values) + len(after)),
        out_specs=[anywhere] * len(values),
        out_shape=[jax.ShapeDtypeStruct(value.shape, value.dtype) for value in values],
        input_output_aliases={k: k for k in range(len(values))},
        compiler_params=pltpu.CompilerParams(vmem_limit_bytes=(63 << 20) + (960 << 10)),
    )(*values, *after)


def normalized(values):
    center = values - jnp.mean(values, axis=-1, keepdims=True)
    spread = jnp.mean(center * center, axis=-1, keepdims=True)
    inverse = lax.rsqrt(spread + norm_epsilon)
    return center * inverse, inverse


def norm_backward(upstream, normed, inverse):
    first_mean = jnp.mean(upstream, axis=-1, keepdims=True)
    second_mean = jnp.mean(upstream * normed, axis=-1, keepdims=True)
    return inverse * (upstream - first_mean - normed * second_mean)


def row_sum(values):
    return jnp.sum(values, axis=0, keepdims=True)


def prepare_body(bits, stamps, src_len, seq_len, flags, inner, inner_bias, outer, outer_bias, cotangent, *outs):
    features, inner_sum, middle, stamp, allowed, valid, masked, cot_other = outs
    cot_other[...] = cotangent[0]
    y = bits[2]
    lane = lax.broadcasted_iota(jnp.int32, (1, TDIM), 1)
    half = TDIM // 2
    frequency = jnp.exp(-math.log(10000.0) * lax.rem(lane, half).astype(f32) / half)
    angles = jnp.broadcast_to(stamps[y].astype(f32), (1, TDIM)) * frequency
    waves = jnp.where(lane < half, jnp.cos(angles), jnp.sin(angles))
    features[...] = waves
    total = jnp.dot(waves, inner[...].astype(f32), precision=highest) + row(inner_bias)
    inner_sum[...] = total
    gated = total * (1.0 / (1.0 + jnp.exp(-total)))
    middle[...] = gated
    stamp[...] = jnp.dot(gated, outer[...].astype(f32), precision=highest) + row(outer_bias)
    source, target = src_len[y], seq_len[y] - src_len[y]
    slots = lax.broadcasted_iota(jnp.int32, (CAP, 1), 0)
    lengths = jnp.where(y == 0, source, target), jnp.where(y == 0, target, source)
    for at, (length, stream) in enumerate(zip(lengths, (y, 1 - y))):
        inside = jnp.where(slots < length, 1.0, 0.0)
        kept = jnp.where(flags[y, pl.ds(stream, 1)] == 1, 1.0, 0.0)
        kept = jnp.broadcast_to(kept, (8, CAP)).T[:, :1]
        here = slice(at * CAP, (at + 1) * CAP)
        valid[here] = inside
        allowed[here] = inside * kept
        masked[here] = (1.0 - inside * kept) * masked_score


def prepare(bits, stamps, src_len, seq_len, flags, inner, inner_bias, outer, outer_bias, cotangent):
    return run(
        prepare_body,
        (1,),
        (flags, inner, inner_bias, outer, outer_bias, cotangent),
        [whole(2, 2, CAP), whole(TDIM, TFF), vector(TFF), whole(TFF, D), vector(D)]
        + [pl.BlockSpec((1, CAP, D), lambda j, bits, *at: (1 - bits[2], 0, 0))],
        [((1, size), f32) for size in (TDIM, TFF, TFF, D)] + [((ROWS, 1), f32)] * 3 + [((CAP, D), bf16)],
        [whole(1, size) for size in (TDIM, TFF, TFF, D)] + [whole(ROWS, 1)] * 3 + [whole(CAP, D)],
        0,
        scalars=(bits, stamps, src_len, seq_len),
    )


def project_body(rows, stamp, keep, qw, qb, kw, vw, vb, q, k, v, low_out):
    low = (rows[...].astype(f32) + stamp[...]).astype(bf16)
    low_out[...] = low
    q[...] = ((nn(low, qw[...]) + row(qb)).astype(bf16).astype(f32) * 0.125).astype(bf16)
    k[...] = (nn(low, kw[...]) * keep[...]).astype(bf16)
    v[...] = (nn(low, vw[...]) + row(vb)).astype(bf16)


def project(rows, half, stamp, keep, qw, qb, kw, vw, vb):
    tile = 256
    return run(
        project_body,
        (D // tile,),
        (rows, stamp, keep, qw, qb, kw, vw, vb),
        [whole(CAP, D), whole(1, D), pl.BlockSpec((CAP, 1), lambda *at: (half, 0))]
        + [column_tile(D, tile), vector_tile(tile), column_tile(D, tile), column_tile(D, tile), vector_tile(tile)],
        [((CAP, D), bf16)] * 4,
        [column_tile(CAP, tile)] * 3 + [whole(CAP, D)],
        6 * CAP * D * D,
    )


def lanes_of(shape):
    return lax.broadcasted_iota(jnp.int32, shape, 1)


def both(own, far):
    return jnp.concatenate([own[...], far[...]], axis=0)


def attend_body(qo, qf, ko, kf, vo, vf, lo, lf, masked, attended, for_core, probs):
    q, k, v = both(qo, qf), both(ko, kf), both(vo, vf)
    lane = lanes_of(q.shape)
    flag = jnp.broadcast_to(masked[...], q.shape).astype(bf16)
    v_turned = v.T
    pieces = []
    for head in range(2):
        mine = (lane // HEAD_DIM) == head
        spare = lane == (1 - head) * HEAD_DIM
        k_head = jnp.where(mine, k, jnp.where(spare, flag, 0))
        q_head = jnp.where(mine, q, jnp.where(spare, 1, 0).astype(bf16))
        scores = nt(k_head, q_head)
        top = jnp.max(scores, axis=0, keepdims=True)
        exponent = jnp.exp(scores - top)
        inverse = 1.0 / jnp.sum(exponent, axis=0, keepdims=True)
        low = (exponent * inverse).astype(bf16)
        probs[head] = low
        pieces.append(nn(v_turned[head * HEAD_DIM : (head + 1) * HEAD_DIM], low))
    low = jnp.concatenate(pieces, axis=0).T.astype(bf16)
    attended[...] = low
    for_core[0], for_core[1] = both(lo, lf), low


def attend(q, k, v, low, masked):
    pair = 2 * HEAD_DIM
    return run(
        attend_body,
        (D // pair,),
        (*q, *k, *v, *low, masked),
        [column_tile(CAP, pair)] * 8 + [whole(ROWS, 1)],
        [((ROWS, D), bf16), ((2, ROWS, D), bf16), ((HEADS, ROWS, ROWS), bf16)],
        [column_tile(ROWS, pair), pl.BlockSpec((2, ROWS, pair), lambda j: (0, 0, j))]
        + [pl.BlockSpec((2, ROWS, ROWS), lambda j: (j, 0, 0))],
        4 * HEADS * ROWS * ROWS * 256,
    )


SHARE = 96
COLOUR = 48


half_tile = pl.BlockSpec((ROWS, D // 2), lambda j, *at: (0, j))


FOR_CORE = (ROWS, FF + 2 * D)


def by_core(values):
    return [
        jnp.concatenate([values[:, at : at + SHARE] for at in range(start, D, 2 * SHARE)], axis=1) for start in (0, SHARE)
    ]


SUB = 256


def feed_forward_body(
    bits, attended, own, far, stamp, ow, ob, gain, shift, ew, eb, rw, rb, gain2, shift2, valid, cot_own, cot_far,
    output, far_output, for_core, activated_own, expanded_own, mixed_low, d_reduced, bias_grad, d_first, d_branch, sums,
    total, normed, inverse, slope, columns,
):
    step = pl.program_id(0)
    tiles = FF // D

    def store(own_out, offset):
        zero, one = by_core(columns[...])
        here = pl.ds(pl.multiple_of(offset, D // 2), D // 2)

        @pl.when(bits[0] == 0)
        def _():
            own_out[...], for_core[:, here] = zero, one

        @pl.when(bits[0] == 1)
        def _():
            own_out[...], for_core[:, here] = one, zero

    @pl.when(step == 0)
    def _():
        hidden = both(own, far).astype(f32) + stamp[...]
        n1, inv = normalized(hidden + nn(attended[...], ow[...]) + row(ob))
        value = n1 * row(gain) + row(shift)
        normed[...] = n1
        inverse[...] = inv
        mixed_low[...] = value.astype(bf16)
        total[...] = value + row(rb)

    @pl.when(step < tiles)
    def _():
        added_up = None
        bias = eb[pl.ds(pl.multiple_of(step * D, D), D)].reshape(1, -1)
        for part in range(D // SUB):
            cut = slice(part * SUB, (part + 1) * SUB)
            expanded = nn(mixed_low[...], ew[:, cut]) + bias[:, cut]
            chance = 0.5 * (1.0 + lax.erf(expanded * root_half))
            slope[step, :, cut] = chance + expanded * jnp.exp(-0.5 * expanded * expanded) * density_scale
            low = (expanded * chance).astype(bf16)
            columns[:, cut] = low
            product = nn(low, rw[cut, :])
            added_up = product if added_up is None else added_up + product
        total[...] += added_up
        store(activated_own, step % 2 * (D // 2))

    @pl.when(step == tiles - 1)
    def _():
        n2, inv = normalized(total[...])
        weight = valid[...]
        rows = ((n2 * row(gain2) + row(shift2)) * weight).astype(bf16)
        output[...], far_output[...] = rows[:CAP], rows[CAP:]
        d_out = jnp.concatenate([cot_own[0], cot_far[...]], axis=0).astype(f32) * weight
        back = norm_backward(d_out * row(gain2), n2, inv)
        low = back.astype(bf16)
        total[...] = back
        d_reduced[...] = low
        sums[...] = jnp.concatenate(
            [jnp.zeros((5, D), f32), row_sum(low.astype(f32)), row_sum(d_out * n2), row_sum(d_out)], axis=0
        )

    @pl.when(step >= tiles)
    def _():
        d_expanded = (nt(d_reduced[...], rw[...]) * slope[step - tiles]).astype(bf16)
        columns[...] = d_expanded
        bias_grad[0] = row_sum(d_expanded.astype(f32))
        total[...] += nt(d_expanded, ew[...])
        store(expanded_own, 0)
        for at in range(tiles):

            @pl.when(step == tiles + at)
            def _():
                source = d_reduced if at < 2 else mixed_low
                for_core[:, D // 2 :] = source[:, at % 2 * (D // 2) : (at % 2 + 1) * (D // 2)]

    @pl.when(step == 2 * tiles - 1)
    def _():
        d_mixed = total[...]
        n1 = normed[...]
        back = norm_backward(d_mixed * row(gain), n1, inverse[...])
        low = back.astype(bf16)
        d_first[...] = back
        d_branch[...] = low
        sums[2:5] = jnp.concatenate([row_sum(low.astype(f32)), row_sum(d_mixed * n1), row_sum(d_mixed)], axis=0)


def feed_forward(
    bits, attended, own, far, stamp, ow, ob, gain, shift, ew, eb, rw, rb, gain2, shift2, valid, cot_own, cot_far
):
    tiles = FF // D
    line, square, half = vector(D), whole(ROWS, D), whole(CAP, D)
    forward = pl.BlockSpec((ROWS, D // 2), lambda j, *at: (0, jnp.minimum(j, tiles - 1)))
    backward = pl.BlockSpec((ROWS, D // 2), lambda j, *at: (0, jnp.maximum(j - tiles, 0)))
    return run(
        feed_forward_body,
        (2 * tiles,),
        (attended, own, far, stamp, ow, ob, gain, shift, ew, eb, rw, rb, gain2, shift2, valid, cot_own, cot_far),
        [square, half, half, whole(1, D), whole(D, D), line, line, line]
        + [pl.BlockSpec((D, D), lambda j, *at: (0, j % tiles)), vector(FF), pl.BlockSpec((D, D), lambda j, *at: (j % tiles, 0))]
        + [line, line, line, whole(ROWS, 1), pl.BlockSpec((1, CAP, D), lambda j, bits: (bits[2], 0, 0)), half],
        [((CAP, D), bf16)] * 2
        + [(FOR_CORE, bf16), ((ROWS, FF // 2), bf16), ((ROWS, FF // 2), bf16), ((ROWS, D), bf16)]
        + [((ROWS, D), bf16), ((tiles, 1, D), f32), ((ROWS, D), f32), ((ROWS, D), bf16), ((8, D), f32)],
        [half, half, pl.BlockSpec((ROWS, D), lambda j, *at: (0, jnp.where(j < tiles, j // 2, j - tiles // 2)))]
        + [forward, backward, square, square]
        + [pl.BlockSpec((1, 1, D), lambda j, *at: (jnp.maximum(j - tiles, 0), 0, 0)), square, square, whole(8, D)],
        2 * ROWS * D * (D + 4 * FF),
        scratch=[pltpu.VMEM((ROWS, D), f32)] * 2
        + [pltpu.VMEM((ROWS, 1), f32), pltpu.VMEM((tiles, ROWS, D), f32), pltpu.VMEM((ROWS, D), bf16)],
        scalars=(bits,),
    )


def hidden_grad_body(bits, activated, d_reduced, d_expanded, mixed, activated_got, *refs):
    halves, (kept, sent) = refs[:6], refs[6:]
    reduced_got, mixed_got, expanded_got = [lambda at=at: jnp.concatenate([halves[at][...], halves[at + 1][...]], axis=1) for at in (0, 2, 4)]
    step = pl.program_id(0)
    tile = step % 2

    def store(kind, grad):
        low = grad.astype(bf16)
        for at in range(8):
            x, z = at % 2, at // 2
            here = jnp.where(bits[0] == 0, tile * 4 + (z % 2 * 2 + z // 2), x * 4 + z)
            block = low[at * SHARE : (at + 1) * SHARE]
            mine = jnp.where(bits[0] == 0, x, tile) == bits[5]

            @pl.when(mine)
            def _():
                kept[here, kind] = block

            @pl.when(jnp.logical_not(mine))
            def _():
                sent[here, kind] = block

    @pl.when(step < 2)
    def _():
        store(0, tn(activated[...], d_reduced[...]) + tn(activated_got[...], reduced_got()))

    @pl.when(step >= 2)
    def _():
        store(1, tn(d_expanded[...], mixed[...]) + tn(expanded_got(), mixed_got()))


def hidden_grad(bits, activated, d_reduced, d_expanded, mixed, got, after):
    first = lambda start: pl.BlockSpec((ROWS, D), lambda j, bits: (0, start + jnp.minimum(j, 1)))
    second = lambda start: pl.BlockSpec((ROWS, D), lambda j, bits: (0, start + jnp.maximum(j - 2, 0)))
    square = lambda at: pl.BlockSpec((ROWS, D), lambda j, bits: (0, at))
    unit = lambda at: pl.BlockSpec((ROWS, D // 2), lambda j, bits: (0, at))
    turn = lambda start: pl.BlockSpec((ROWS, D // 2), lambda j, bits: (0, start + 4 * jnp.maximum(j - 2, 0)))
    return run(
        hidden_grad_body,
        (4,),
        (activated, d_reduced, d_expanded, mixed) + (got,) * 7,
        [first(0), square(0), second(0), square(0), first(0)] + [unit(at) for at in (5, 7, 9, 11)] + [turn(4), turn(6)],
        [((8, 2, SHARE, D), bf16)] * 2,
        [whole(8, 2, SHARE, D)] * 2,
        4 * ROWS * D * FF,
        scalars=(bits,),
        after=after,
    )


def attend_back_body(bits, d_branch, branch, ow, probs, qo, qf, ko, kf, vo, vf, keep, grads, kept, sent, sums):
    q, k, v = both(qo, qf), both(ko, kf), both(vo, vf)
    lane = lanes_of(q.shape)
    low_half = lane < HEAD_DIM
    upstream = nt(d_branch[...], ow[...]).astype(bf16)
    k_turned = k.T
    d_q, d_k, d_v = [], [], []
    for head in range(2):
        rows = slice(head * HEAD_DIM, (head + 1) * HEAD_DIM)
        mine = low_half if head == 0 else jnp.logical_not(low_half)
        low = probs[head]
        wide = low.astype(f32)
        weighted = wide * nt(jnp.where(mine, v, 0), upstream)
        d_scores = (weighted - wide * row_sum(weighted)).astype(bf16)
        d_v.append(nn(low, upstream))
        d_k.append(nn(d_scores, q))
        d_q.append(nn(k_turned[rows], d_scores))
    q_low = (jnp.concatenate(d_q, axis=0).T * 0.125).astype(bf16)
    v_low = jnp.where(low_half, d_v[0], d_v[1]).astype(bf16)
    k_low = (jnp.where(low_half, d_k[0], d_k[1]) * keep[...]).astype(bf16)
    grads[0], grads[1], grads[2] = q_low, k_low, v_low

    def share(first, second):
        first[0], first[1] = q_low, k_low
        second[0], second[1] = v_low, branch[...]

    @pl.when(bits[0] == 0)
    def _():
        share(kept, sent)

    @pl.when(bits[0] == 1)
    def _():
        share(sent, kept)

    sums[...] = jnp.concatenate(
        [row_sum(q_low.astype(f32)), row_sum(v_low.astype(f32)), jnp.zeros((6, q.shape[1]), f32)], axis=0
    )


def attend_back(bits, d_branch, ow, probs, q, k, v, keep, after):
    pair = 2 * HEAD_DIM
    return run(
        attend_back_body,
        (D // pair,),
        (d_branch, d_branch, ow, probs, *q, *k, *v, keep),
        [whole(ROWS, D), column_tile(ROWS, pair), row_tile(pair, D), pl.BlockSpec((2, ROWS, ROWS), lambda j, *at: (j, 0, 0))]
        + [column_tile(CAP, pair)] * 6
        + [whole(ROWS, 1)],
        [((count, ROWS, D), bf16) for count in (3, 2, 2)] + [((8, D), f32)],
        [pl.BlockSpec((count, ROWS, pair), lambda j, *at: (0, 0, j)) for count in (3, 2, 2)] + [column_tile(8, pair)],
        10 * HEADS * ROWS * ROWS * 256,
        scalars=(bits,),
        after=after,
    )


def pair_grad_body(bits, left, right, left_got, right_got, kept, sent):
    low = (tn(left[0], right[0]) + tn(left_got[0], right_got[0])).astype(bf16)
    zero, one = [low[at * D // 2 : (at + 1) * D // 2].reshape(8, COLOUR, D) for at in range(2)]
    kept[:, 0] = jnp.where(bits[5] == 0, zero, one)
    sent[:, 0] = jnp.where(bits[5] == 0, one, zero)


def pair_grad(bits, left, right, left_got, right_got, after):
    lefts = pl.BlockSpec((1, ROWS, D), lambda j, bits: (j * bits[0], 0, 0))
    rights = pl.BlockSpec((1, ROWS, D), lambda j, bits: (j, 0, 0))
    return run(
        pair_grad_body,
        (2,),
        (left, right, left_got, right_got),
        [lefts, rights] * 2,
        [((8, 2, COLOUR, D), bf16)] * 2,
        [pl.BlockSpec((8, 1, COLOUR, D), lambda j, *at: (0, j, 0, 0))] * 2,
        8 * ROWS * D * D,
        scalars=(bits,),
        after=after,
    )


def input_grad_body(grads, qw, kw, vw, d_first, own_rows, far_rows, d_time):
    total = d_first[...] + nt(grads[0], qw[...]) + nt(grads[1], kw[...]) + nt(grads[2], vw[...])
    low = total.astype(bf16)
    own_rows[...], far_rows[...] = low[:CAP], low[CAP:]
    d_time[...] = row_sum(total)


def input_grad(grads, qw, kw, vw, d_first, after):
    tile = 256
    return run(
        input_grad_body,
        (D // tile,),
        (grads, qw, kw, vw, d_first),
        [whole(3, ROWS, D)] + [row_tile(tile, D)] * 3 + [column_tile(ROWS, tile)],
        [((CAP, D), bf16)] * 2 + [((1, D), f32)],
        [column_tile(CAP, tile)] * 2 + [column_tile(1, tile)],
        6 * ROWS * D * D,
        after=after,
    )


everywhere = ("y", "z", "x", "c")


def crossed(value, first):
    sizes = [lax.axis_size(axis) for axis in everywhere]
    pairs = []
    for at in range(math.prod(sizes)):
        c, x = at % 2, at // 2 % 2
        along_x = (c == 0) == first
        step = 2 * (1 - 2 * x) if along_x else (math.prod(sizes) // 2) * (1 - 2 * (at // (math.prod(sizes) // 2)))
        pairs.append((at, at + step))
    return lax.ppermute(value, everywhere, pairs)


def lined(value, first):
    sizes = [lax.axis_size(axis) for axis in everywhere]
    turn = lambda c: 1 if (c == 0) == first else 2
    pairs = [(at, at ^ (turn(at % 2) * 4)) for at in range(math.prod(sizes))]
    return lax.ppermute(value, everywhere, pairs)


def plus(left, right):
    return (left.astype(f32) + right.astype(f32)).astype(bf16)


def halved(own, got, bit):
    own, got = [value.reshape((2, -1) + value.shape[1:]) for value in (own, got)]
    at = lambda place: [lax.dynamic_index_in_dim(value, place, 0, keepdims=False) for value in (own, got)]
    return plus(*at(bit)), plus(*at(1 - bit))


BLOCK = 32


def block_body(bits, first, second, bias, d_time, inner_sum, middle, features, outer, out):
    riders = first[...] + second[...]
    total = inner_sum[...]
    gate = 1.0 / (1.0 + jnp.exp(-total))
    d_middle = lax.dot_general(
        d_time[...], outer[...].astype(f32), (((1,), (1,)), ((), ())), precision=highest, preferred_element_type=f32
    )
    d_inner = d_middle * (gate * (1.0 + total * (1.0 - gate)))
    wide = D - TFF
    rows = [jnp.concatenate([d_time[:, at * wide : (at + 1) * wide], middle[...]], axis=1) for at in range(3)]
    rows.append(jnp.concatenate([d_inner, features[...], jnp.zeros((1, wide - TDIM), f32)], axis=1))
    index = lax.broadcasted_iota(jnp.int32, (16, D), 0)
    factors = jnp.zeros((16, D), f32)
    for at, values in enumerate(rows):
        factors = jnp.where(index == 4 * (bits[3] + 2 * bits[4]) + at, values, factors)
    biases = jnp.zeros((8, D), f32)
    index = lax.broadcasted_iota(jnp.int32, (8, D), 0)
    for at in range(4):
        biases = jnp.where(index == at, bias[at], biases)
    out[...] = jnp.concatenate([riders, biases, factors], axis=0).astype(bf16)


def block_rows(bits, *operands):
    return run(
        block_body,
        (1,),
        operands,
        [whole(*operand.shape) for operand in operands],
        [((BLOCK, D), bf16)],
        [whole(BLOCK, D)],
        0,
        scalars=(bits,),
    )[0]


def sum_rows(own, got):
    return lax.reduce_precision(own.astype(f32) + got.astype(f32), 8, 7).astype(bf16)


def longer(data, block, send):
    got = send(jnp.concatenate([data, block]))
    size = data.shape[0]
    return jnp.concatenate([data, got[:size]]), sum_rows(block, got[size:])


def unpack_body(bits, pieces, outs):
    for turn in range(2):

        @pl.when(pl.program_id(0) == turn)
        def _():
            own, got = pieces[turn], pieces[2 + turn]
            for at in range(4):
                here, there = (bits[6] % 4) ^ at, (bits[7] % 4) ^ at
                for matrix in range(2):
                    rows = slice(at * SHARE + matrix * COLOUR, at * SHARE + (matrix + 1) * COLOUR)
                    mine, other = own[rows].astype(f32), got[rows].astype(f32)
                    outs[matrix][here] = jnp.where(bits[0] == 0, mine, other)
                    outs[2 + matrix][there] = jnp.where(bits[0] == 0, other, mine)


def unpack_specs(turn):
    part = whole(4 * SHARE, D)
    spots = [
        pl.BlockSpec((4, COLOUR, D), lambda j, bits, at=at: ((bits[at] // 4) ^ (2 * turn + j), 0, 0)) for at in (6, 6, 7, 7)
    ]
    return part, spots


matrix_shapes = [((16, COLOUR, D), f32)] * 4


def first_unpack(bits, pieces):
    part, spots = unpack_specs(0)
    body = lambda bits, *refs: unpack_body(bits, refs[:4], refs[4:])
    return run(body, (2,), pieces, [part] * 4, matrix_shapes, spots, 0, scalars=(bits,))


def finish_body(bits, *refs):
    unpack_body(bits, refs[:4], refs[16:20])

    @pl.when(pl.program_id(0) == 1)
    def _():
        vectors_body(refs[4:12], *refs[20:])


def vectors_body(refs, *outs):
    blocks = [ref[...].astype(f32) for ref in refs]
    riders = [block[:16] for block in blocks]
    pairs = [riders[at] + riders[at + 1] for at in range(0, 8, 2)]
    sums = (pairs[0] + pairs[1]) + (pairs[2] + pairs[3])
    for at in range(8):
        outs[at][...] = sums[at]
    for at in range(4):
        outs[8][at] = sums[8 + at : 9 + at]
    factors = jnp.concatenate([block[16:] for block in blocks], axis=0)
    index = lax.broadcasted_iota(jnp.int32, factors.shape, 0) % 4
    wide = D - TFF
    inner, inner_bias, outer, outer_bias = outs[9:]
    for at in range(3):
        rows = jnp.where(index == at, factors, 0.0)
        d_time = rows[:, :wide]
        here = slice(at * wide, (at + 1) * wide)
        outer[:, here] = tn(rows[:, wide:].astype(bf16), d_time.astype(bf16))
        outer_bias[here] = jnp.sum(d_time, axis=0)
    rows = jnp.where(index == 3, factors, 0.0)
    d_inner = rows[:, :TFF]
    inner[...] = tn(rows[:, TFF : TFF + TDIM].astype(bf16), d_inner.astype(bf16))
    inner_bias[...] = jnp.sum(d_inner, axis=0)


def finish(bits, turned, turned_far, pieces, pieces_far, outs):
    part, spots = unpack_specs(1)
    last = pl.BlockSpec((BLOCK, D), lambda j, *at: (4 * SHARE // BLOCK, 0))
    shapes = [(D,)] * 8 + [(4, 1, D), (TDIM, TFF), (TFF,), (TFF, D), (D,)]
    return run(
        finish_body,
        (2,),
        (*turned, *turned_far, *pieces, *turned, *pieces_far, *turned_far, *outs),
        [part] * 4 + [last] * 8 + [pl.BlockSpec(memory_space=pl.ANY)] * 4,
        matrix_shapes + [(shape, f32) for shape in shapes],
        spots + [whole(*shape) for shape in shapes],
        0,
        scalars=(bits,),
        aliases={13 + k: k for k in range(4)},
    )


def plain_rows(first_class, second_class):
    zero = jnp.concatenate(first_class).reshape(2, 2, 2, 2, SHARE, D)
    one = jnp.concatenate(second_class).reshape(2, 2, 2, 2, SHARE, D)
    classes = jnp.stack([jnp.transpose(zero, (1, 3, 2, 0, 4, 5)), jnp.transpose(one, (0, 2, 3, 1, 4, 5))], axis=4)
    return classes.reshape(FF, D)


def everyones(sums, bias, d_time, inner_sum, middle, features, outer):
    gate = jax.nn.sigmoid(inner_sum)
    d_inner = jnp.dot(d_time, outer.astype(f32).T, precision=highest) * (gate * (1.0 + inner_sum * (1.0 - gate)))
    riders = jnp.concatenate([sums, bias.reshape(4, D), jnp.zeros((4, D), f32)])
    factors = jnp.concatenate([d_time, d_inner, middle, features], axis=1)
    for stage in stage_lists()[0]:
        riders = riders + swapped(riders, stage)
        factors = jnp.concatenate([factors, swapped(factors, stage)])
    cuts = (0, D, D + TFF, D + 2 * TFF, D + 2 * TFF + TDIM)
    d_time, d_inner, middle, features = [factors[:, a:b] for a, b in zip(cuts, cuts[1:])]
    inner, outer = matmul(features.T, d_inner), matmul(middle.T, d_time)
    return list(riders[:8]), riders[8:12], inner, column_sum(d_inner), outer, column_sum(d_time)


def on_device(
    layer_input,
    cotangent,
    timesteps,
    src_len,
    seq_len,
    key_keep,
    query_weight,
    query_bias,
    key_weight,
    value_weight,
    value_bias,
    output_weight,
    output_bias,
    first_gain,
    first_shift,
    expand_weight,
    expand_bias,
    reduce_weight,
    reduce_bias,
    second_gain,
    second_shift,
    time_inner,
    time_inner_bias,
    time_outer,
    time_outer_bias,
):
    stream = lax.axis_index("y")
    sizes = [lax.axis_size(axis) for axis in ("y", "z", "x", "c")]
    devices = math.prod(sizes)
    tuned = sizes == [2, 4, 2, 2]
    c, x, z = lax.axis_index("c") if tuned else 0, lax.axis_index("x"), lax.axis_index("z")
    first, second = jnp.where(c == 0, x, stream), jnp.where(c == 0, stream, x)
    wanted = first if tuned else 0
    near_z, across_z = z & 1, z >> 1
    third, fourth = jnp.where(c == 0, near_z, across_z), jnp.where(c == 0, across_z, near_z)
    places = [x * 8 + stream * 4 + near_z * 2 + across_z, stream * 8 + x * 4 + across_z * 2 + near_z]
    bits = jnp.stack([c, x, stream, z & 1, z >> 1, wanted, *places]).astype(jnp.int32)

    def whole_sequence(rows):
        own = lax.dynamic_index_in_dim(rows[:, 0], stream, axis=0, keepdims=False)
        other = lax.dynamic_index_in_dim(rows[:, 0], 1 - stream, axis=0, keepdims=False)
        return own, other

    def both_sequences(rows, far):
        own = rows
        return jnp.where(stream == 0, jnp.stack([own, far]), jnp.stack([far, own]))[:, None]

    own, other = whole_sequence(layer_input)
    far = swapped(other, side)
    cotangent = cotangent[:, 0]
    features, inner_sum, middle, stamp, allowed, valid, masked, cot_other = prepare(
        bits, timesteps, src_len, seq_len, key_keep, time_inner, time_inner_bias, time_outer, time_outer_bias, cotangent
    )
    weights = (query_weight, query_bias, key_weight, value_weight, value_bias)
    *first_rows, own_low = project(own, 0, stamp, allowed, *weights)
    (far,) = tie([far], first_rows[:1])
    cot_other, far = lax.optimization_barrier((cot_other, far))
    cot_far = swapped(cot_other, side)
    *other_rows, far_low = project(far, 1, stamp, allowed, *weights)
    q, k, v = zip(first_rows, other_rows)
    low = (own_low, far_low)
    attended, lefts, probs = attend(q, k, v, low, masked)
    (lefts,) = tie([lefts], [cot_far])
    output, far_output, for_core, activated, d_expanded, mixed_low, d_reduced, *others = feed_forward(
        bits,
        attended,
        own,
        far,
        stamp,
        output_weight,
        output_bias,
        first_gain,
        first_shift,
        expand_weight,
        expand_bias,
        reduce_weight,
        reduce_bias,
        second_gain,
        second_shift,
        valid,
        cotangent,
        cot_far,
    )
    expand_bias_grad, d_first, d_branch, layer_sums = others
    lefts_got = swapped(lefts, core)
    (far_output,) = tie([far_output], [lefts_got])
    output_got = swapped(far_output, side)
    grads, kept, sent, attend_sums = attend_back(bits, d_branch, output_weight, probs, q, k, v, allowed, [far_output])
    block_parts = (inner_sum, middle, features, time_outer)
    if tuned:
        (sent,) = tie([sent], [output_got])
        sent_got = swapped(sent, core)
        (for_core,) = tie([for_core], [sent_got])
        hidden_got = swapped(for_core, core)
        small, small_sent = pair_grad(bits, lefts, kept, lefts_got, sent_got, [for_core])
        (small_sent,) = tie([small_sent], [hidden_got])
        small_got = crossed(small_sent, True)
        hidden, hidden_sent = hidden_grad(bits, activated, d_reduced, d_expanded, mixed_low, hidden_got, [small_sent])
        (small_got,) = tie([small_got], [hidden])
        hidden_got = crossed(hidden_sent, True)
        small_sent = halved(small, small_got, second)[1]
        (small_got,) = tie([small_got], [small_sent])
        small = halved(small, small_got, second)[0]
        small_got = crossed(small_sent, False)
        d_rows, far_grad, d_time = input_grad(grads, query_weight, key_weight, value_weight, d_first, [small_sent])
        block = block_rows(bits, attend_sums, layer_sums, expand_bias_grad, d_time, *block_parts)
        (small_got,) = tie([small_got], [block])
        small, small_sent = halved(small, small_got, third)
        small_got = lined(small_sent, True)
        (far_grad,) = tie([far_grad], [small_sent])
        input_got = swapped(far_grad, side)
        small, small_sent = halved(small, small_got, fourth)
        small_got = lined(small_sent, False)
        hidden_got, input_got = tie([hidden_got, input_got], [small_sent])
        hidden, hidden_sent = halved(hidden, hidden_got, second)
        hidden_got = crossed(hidden_sent, False)
        (small_got,) = tie([small_got], [hidden_sent])
        share = plus(small, small_got).reshape(SHARE, D)
        data, block = longer(share, block, lambda value: lined(value, False))
        (hidden_got,) = tie([hidden_got], [data])
        hidden, hidden_sent = halved(hidden, hidden_got, third)
        hidden_got = lined(hidden_sent, True)
        data, block = longer(data, block, lambda value: lined(value, True))
        piece = jnp.concatenate([data, block])
        cross_got = crossed(piece, False)
        turned = crossed(piece, True)
        hidden, hidden_sent = halved(hidden, hidden_got, fourth)
        hidden_got = lined(hidden_sent, False)
        (cross_got,) = tie([cross_got], [hidden_sent, turned])
        pieces, turned = (piece, cross_got), (turned, crossed(cross_got, True))
        pieces_far = [swapped(value, core) for value in pieces]
        output, output_got, d_rows, input_got = tie([output, output_got, d_rows, input_got], [cross_got])
        outs = first_unpack(bits, (*pieces, *pieces_far))
        output, input_grad_rows = both_sequences(output, output_got), both_sequences(d_rows, input_got)
        turned = tie(turned, [outs[0], output, input_grad_rows])
        turned_far = [swapped(value, core) for value in turned]
        (hidden_got,) = tie([hidden_got], turned)
        shares = (hidden.astype(f32) + hidden_got.astype(f32))[0]
        reduce_share, expand_share = shares[0], shares[1]
        *matrices, expand_bias_grad, inner, inner_bias, outer, outer_bias = finish(
            bits, turned, turned_far, pieces, pieces_far, outs
        )
        grad_query, grad_key, grad_value, grad_output = [out.reshape(D, D) for out in matrices[:4]]
        vectors = matrices[4:]
    else:
        d_rows, far_grad, d_time = input_grad(grads, query_weight, key_weight, value_weight, d_first, ())
        reduce_parts, expand_parts, pairs = [], [], []
        nothing_got = jnp.zeros_like(for_core)
        expanded_other = jnp.concatenate([for_core[:, at * D // 2 : (at + 1) * D // 2] for at in (4, 6, 8, 10)], axis=1)
        for core_bit, pair, left, right in (
            (0, kept, activated, d_expanded),
            (1, sent, for_core[:, : 2 * D], expanded_other),
        ):
            as_core = bits.at[0].set(core_bit)
            hidden = hidden_grad(as_core, left, d_reduced, right, mixed_low, nothing_got, ())
            reduce_parts.append([part[:, 0] for part in hidden])
            expand_parts.append([part[:, 1] for part in hidden])
            grad = pair_grad(as_core, lefts, pair, lefts, jnp.zeros_like(pair), ())
            pairs.append(jnp.moveaxis(jnp.concatenate(grad), 1, 0).reshape(2, D, D))
        per = FF // devices
        reduce_share, _ = scattered_sum(plain_rows(*reduce_parts).reshape(devices, per, D))
        expand_share, _ = scattered_sum(plain_rows(*expand_parts).reshape(devices, per, D))
        small_share, _ = scattered_sum(jnp.concatenate(pairs).reshape(devices, per, D))
        me = ((stream * sizes[1] + z) * 2 + x) * 2 + lax.axis_index("c")
        small = gathered(small_share)[jnp.arange(devices) ^ me].astype(f32).reshape(4, D, D)
        grad_query, grad_key, grad_value, grad_output = [small[at] for at in range(4)]
        vectors, expand_bias_grad, inner, inner_bias, outer, outer_bias = everyones(
            attend_sums + layer_sums, expand_bias_grad, d_time, *block_parts
        )
        input_grad_rows = both_sequences(d_rows, swapped(far_grad, side))
        output = both_sequences(output, output_got)
    return (
        output,
        input_grad_rows,
        grad_query,
        vectors[0],
        grad_key,
        grad_value,
        vectors[1],
        grad_output,
        vectors[2],
        vectors[3],
        vectors[4],
        expand_share.astype(f32).T,
        expand_bias_grad.reshape(FF),
        reduce_share.astype(f32),
        vectors[5],
        vectors[6],
        vectors[7],
        inner,
        inner_bias,
        outer,
        outer_bias,
    )


def solution(mesh):
    seq, batch = mesh.devices.shape
    mesh = jax.sharding.Mesh(mesh.devices.reshape(seq, batch // 4, 2, 2), ("y", "z", "x", "c"))
    sequences, everyone = ("z", "x", "c"), ("y", "z", "x", "c")
    rows = P(sequences, "y", None, None)
    in_specs = (rows, rows) + (P(sequences),) * 3 + (P(sequences, None, None),) + (P(),) * 19
    out_specs = (rows, rows) + (P(),) * 9 + (P(None, everyone), P(), P(everyone, None)) + (P(),) * 7
    return jax.shard_map(on_device, mesh=mesh, in_specs=in_specs, out_specs=out_specs, check_vma=False)
```
